32 devices in a mesh: groups: 2 (over y), tm: 4 (over x, core), space: 4 (over z).
Axes of the slice: x: 2, y: 2, z: 4, core: 2. Of those that a mesh axis runs over, the one named last changes fastest.
Arguments:
- forcing: float32 [32, 4, 64, 1024], P('groups', 'tm', None, 'space'), parts along dimension 0, may hold values from -6 to 6
- iterate: float32 [32, 4, 64, 1024], P('groups', 'tm', None, 'space'), parts along dimension 0, may hold values from -6 to 6
- kappa_mean: float32 [1024], P('space'), may hold values from 0.2 to 2
- kappa_modes: float32 [16, 1024], P(None, 'space'), may hold values from -0.1125 to 0.1125
- grad_mats: float32 [3, 64, 64], replicated, may hold values from -0.4375 to 0.4375
- face_mats: float32 [3, 64, 64], replicated, may hold values from -0.1875 to 0.1875
- lattice_shift: float32 [32], P('groups'), parts along dimension 0, may hold values from 0 to 1
- gen_vector: int32 [16], replicated, may hold values from 1 to 15, as said below
- sweep_counts: int32 [4], replicated, may hold values from 1 to 3, as said below
- face_nbr: int32 [6, 1024], P(None, 'space'), may hold values from -1 to 383, as said below
- halo_send: int32 [2, 256], P(None, 'space'), may hold values from 0 to 255, as said below
Outputs:
- correction: float32 [32, 4, 64, 1024], P('groups', 'tm', None, 'space'), parts along dimension 0
The draws below stay inside these ranges and needn't reach their ends.
There are 2 independent parts, one for each index of `groups`. The reference program is written for one: setup_inputs(seed, part) draws one part's arguments, and reference() takes and returns one part's arrays. A program takes and returns all parts, laid end to end along the dimension named above; an argument that names none is the same for every part. Nothing has to cross between parts.
Inputs may be any that keep to these rules, and one draw needn't show every extreme that they name: `gen_vector`: odd numbers below 16; the first entry is 1 and the second 16 - 1. `sweep_counts`: frequencies k and 4 - k take equal counts; some frequency takes 3 and some 1. `face_nbr`: faces 0 to 5 are -x, +x, -y, +y, -z, +z; an entry below 256 is an element of the same slab in its local numbering, 256 + i the i-th entry of row 1 of the slab below, 320 + i the i-th entry of row 0 of the slab above, -1 the domain's boundary; across face f of e lies an element whose face f xor 1 leads back to e. `halo_send`: each slab's 64 entries in each row are distinct local numbers below 256, listing every element that faces the slab below (row 0) or above (row 1); local number 0 faces the slab below and 255 the slab above.
All inputs are finite; a program needn't handle non-finite values.
Results may differ from the reference program's by a relative error of at most 0.0003.
Values sent between devices are 32-bit elements; how exact they have to be, the bound alone decides.
No kernel may reach another device: no remote copies, remote signals or barrier semaphores. Data moves between devices by JAX's collectives and lax.ppermute only.
A program may use at most 128 MiB of HBM per device.

```python
import math
import jax
import jax.numpy as jnp
from jax import lax

SAMPLES = 16
NDOF = 64
NMODES = 16
SIDE = 8
LAYERS = 4
MAXS = 3
STEPS = 4
E_DEV = 256
HALO = 64
ELEMS = 1024


def mesh_tables(key):
    base_key = jax.random.fold_in(key, 17)
    slabs = ELEMS // E_DEV
    slab_ids = jnp.arange(slabs, dtype=jnp.int32)

    def orders(slab):
        slab_key = jax.random.fold_in(base_key, slab)
        middle = (1 + jax.random.permutation(jax.random.fold_in(slab_key, 1), E_DEV - 2)).astype(jnp.int32)
        numbering = jnp.concatenate([jnp.zeros((1,), jnp.int32), middle, jnp.full((1,), E_DEV - 1, jnp.int32)]).astype(jnp.int32)
        downward = jax.random.permutation(jax.random.fold_in(slab_key, 2), HALO).astype(jnp.int32)
        upward = jax.random.permutation(jax.random.fold_in(slab_key, 3), HALO).astype(jnp.int32)
        return (numbering, downward, upward)
    numbering, downward, upward = jax.vmap(orders)(slab_ids)
    down_slot = jnp.argsort(downward, axis=1).astype(jnp.int32)
    up_slot = jnp.argsort(upward, axis=1).astype(jnp.int32)
    position = jnp.arange(E_DEV, dtype=jnp.int32)
    column_x = position % SIDE
    column_y = position // SIDE % SIDE
    layer = position // HALO
    plane = position % HALO
    slab_col = slab_ids[:, None]

    def beside(offset):
        return numbering[:, jnp.clip(position + offset, 0, E_DEV - 1)]
    face_x_lo = jnp.where(column_x > 0, beside(-1), -1)
    face_x_hi = jnp.where(column_x < SIDE - 1, beside(1), -1)
    face_y_lo = jnp.where(column_y > 0, beside(-SIDE), -1)
    face_y_hi = jnp.where(column_y < SIDE - 1, beside(SIDE), -1)
    below_slot = up_slot[jnp.clip(slab_ids - 1, 0, slabs - 1)][:, plane]
    above_slot = down_slot[jnp.clip(slab_ids + 1, 0, slabs - 1)][:, plane]
    face_z_lo = jnp.where(layer > 0, beside(-HALO), jnp.where(slab_col > 0, E_DEV + below_slot, -1))
    face_z_hi = jnp.where(layer < LAYERS - 1, beside(HALO), jnp.where(slab_col < slabs - 1, E_DEV + HALO + above_slot, -1))
    by_position = jnp.stack([face_x_lo, face_x_hi, face_y_lo, face_y_hi, face_z_lo, face_z_hi]).astype(jnp.int32)
    position_of = jnp.argsort(numbering, axis=1).astype(jnp.int32)
    table = jnp.take_along_axis(by_position, jnp.broadcast_to(position_of[None], by_position.shape), axis=2)
    face_table = table.reshape(6, ELEMS).astype(jnp.int32)
    send_down = jnp.take_along_axis(numbering, downward, axis=1)
    send_up = jnp.take_along_axis(numbering, (LAYERS - 1) * HALO + upward, axis=1)
    halo_table = jnp.stack([send_down.reshape(-1), send_up.reshape(-1)]).astype(jnp.int32)
    return (face_table, halo_table)


def draw_face_nbr(key, part):
    return mesh_tables(key)[0]


def draw_halo_send(key, part):
    return mesh_tables(key)[1]


def draw_sweep_counts(key, part):
    spots = STEPS // 2 + 1
    frequency = jnp.arange(STEPS, dtype=jnp.int32)
    distance = jnp.minimum(frequency, STEPS - frequency)
    per_spot = jax.random.randint(jax.random.fold_in(key, 1), (spots,), 1, MAXS + 1, dtype=jnp.int32)
    order = jax.random.permutation(jax.random.fold_in(key, 2), spots).astype(jnp.int32)
    spot_ids = jnp.arange(spots, dtype=jnp.int32)
    per_spot = jnp.where(spot_ids == order[0], MAXS, per_spot)
    per_spot = jnp.where(spot_ids == order[1], 1, per_spot)
    return per_spot[distance].astype(jnp.int32)


def draw_gen_vector(key, part):
    drawn = (2 * jax.random.randint(key, (NMODES,), 0, SAMPLES // 2, dtype=jnp.int32) + 1).astype(jnp.int32)
    slots = jnp.arange(NMODES, dtype=jnp.int32)
    drawn = jnp.where(slots == 0, 1, drawn)
    drawn = jnp.where(slots == 1, SAMPLES - 1, drawn)
    return drawn.astype(jnp.int32)


def shard_levels(own_key, shape, split, low, high):
    loudness = 1.0
    for axis_at, blocks in split:
        draws = jax.random.uniform(jax.random.fold_in(jax.random.fold_in(own_key, 6), axis_at), (blocks,), jnp.float32, low / len(split), high / len(split))
        loudness = loudness * jnp.repeat(jnp.exp(draws), shape[axis_at] // blocks).reshape((-1,) + (1,) * (len(shape) - 1 - axis_at))
    return loudness


def centred(rng, shape, width, reach, split=(), kind=jnp.bfloat16):
    loudness = shard_levels(rng, shape, split, -0.22, 0.18) if split else 1.0
    values = jax.random.normal(rng, shape, jnp.float32) * width * loudness
    return jnp.minimum(jnp.maximum(values, -reach), reach).astype(kind)


def setup_inputs(seed: int = 0, part: int = 0) -> dict:
    streams_of = jax.random.split(jax.random.key(seed), 12)
    part_splits = jax.random.split(jax.random.fold_in(streams_of[11], part), 12)
    return {
        "forcing": centred(part_splits[0], (SAMPLES, STEPS, NDOF, ELEMS), 1.0, 6.0, ((1, 4), (3, 4)), jnp.float32),
        "iterate": centred(part_splits[1], (SAMPLES, STEPS, NDOF, ELEMS), 1.0, 6.0, ((1, 4), (3, 4)), jnp.float32),
        "kappa_mean": jnp.clip(jnp.exp(math.log(2.0) - 2.3025851 * jax.random.uniform(streams_of[2], (ELEMS,), jnp.float32) ** shard_levels(streams_of[2], (ELEMS,), ((0, 4),), -0.2, 0.2)), 0.2, 2.0),
        "kappa_modes": jnp.clip(jax.random.uniform(streams_of[3], (NMODES, ELEMS), jnp.float32, -0.1125, 0.1125) * shard_levels(streams_of[3], (NMODES, ELEMS), ((1, 4),), -0.4, 0.0), -0.1125, 0.1125),
        "grad_mats": centred(streams_of[4], (3, NDOF, NDOF), (3 * NDOF) ** -0.5, 0.4375, (), jnp.float32),
        "face_mats": centred(streams_of[5], (3, NDOF, NDOF), (16 * NDOF) ** -0.5, 0.1875, (), jnp.float32),
        "lattice_shift": jnp.clip(jax.random.uniform(part_splits[6], (NMODES,), jnp.float32, 0.0, 1.0), 0.0, 1.0),
        "gen_vector": draw_gen_vector(jax.random.fold_in(streams_of[11], 71), part),
        "sweep_counts": draw_sweep_counts(jax.random.fold_in(streams_of[11], 71), part),
        "face_nbr": draw_face_nbr(jax.random.fold_in(streams_of[11], 71), part),
        "halo_send": draw_halo_send(jax.random.fold_in(streams_of[11], 71), part),
    }


alpha_circ = 0.05
time_step = 0.1
relax_rho = 2.3
highest = lax.Precision.HIGHEST


def lattice_points(gen_vector, lattice_shift, number, modulus):
    position = jnp.arange(number, dtype=jnp.int32)
    residue = (position[:, None] * gen_vector[None, :]) % modulus
    shifted = residue.astype(lattice_shift.dtype) / modulus + lattice_shift[None, :]
    fraction = shifted - jnp.floor(shifted)
    return 0.5 - jnp.abs(2.0 * fraction - 1.0)


def conductivity(points, kappa_mean, kappa_modes):
    return kappa_mean[None, :] * (1.0 + jnp.dot(points, kappa_modes, precision=highest))


def volume_block(grad_mats):
    return jnp.eye(grad_mats.shape[1], dtype=grad_mats.dtype) + jnp.einsum('dca,dcb->ab', grad_mats, grad_mats, precision=highest)


def face_blocks(face_mats):
    return [face_mats[0].T, face_mats[0], face_mats[1].T, face_mats[1], face_mats[2].T, face_mats[2]]


def face_coefs(conduct, conduct_nbr, inside):
    coupling = jnp.where(inside[None], 0.5 * (conduct[:, None, :] + conduct_nbr), 0.0)
    diag_coef = conduct + jnp.sum(jnp.where(inside[None], coupling, conduct[:, None, :]), axis=1)
    return coupling, diag_coef


def stiffness(source, extended, nbr_safe, coupling, diag_coef, volume, blocks):
    summed = diag_coef[None, :, None, None, :] * jnp.einsum('ab,csgbe->csgae', volume, source, precision=highest)
    for which_face in range(6):
        across = jnp.take(extended, nbr_safe[which_face], axis=4)
        term = jnp.einsum('ab,csgbe->csgae', blocks[which_face], across, precision=highest)
        summed = summed + coupling[None, :, which_face, None, None, :] * term
    return summed


def shifted_terms(frequency, total_steps, diag_coef):
    magnitude = alpha_circ ** (1.0 / total_steps)
    phase_angle = frequency.astype(diag_coef.dtype) * (2.0 * math.pi / total_steps)
    shift_real = 1.0 - magnitude * jnp.cos(phase_angle)
    shift_imag = magnitude * jnp.sin(phase_angle)
    denom_real = shift_real[None, :, None] + (time_step * relax_rho) * diag_coef[:, None, :]
    denom_imag = jnp.broadcast_to(shift_imag[None, :, None], denom_real.shape)
    modulus = denom_real * denom_real + denom_imag * denom_imag
    return shift_real, shift_imag, denom_real / modulus, -denom_imag / modulus


def times_theta(theta_real, theta_imag, source):
    rate_real = theta_real[:, :, None, :]
    rate_imag = theta_imag[:, :, None, :]
    return jnp.stack([rate_real * source[0] - rate_imag * source[1], rate_real * source[1] + rate_imag * source[0]])


def operator_image(current, applied, shift_real, shift_imag):
    scale_real = shift_real[None, :, None, None]
    scale_imag = shift_imag[None, :, None, None]
    return jnp.stack([scale_real * current[0] - scale_imag * current[1], scale_real * current[1] + scale_imag * current[0]]) + time_step * applied


def dft_tables(length, dtype):
    position = jnp.arange(length, dtype=jnp.int32)
    phase_angle = ((position[:, None] * position[None, :]) % length).astype(dtype) * (2.0 * math.pi / length)
    return jnp.cos(phase_angle), jnp.sin(phase_angle)


def global_neighbors(face_nbr, halo_send):
    element = jnp.arange(face_nbr.shape[1], dtype=jnp.int32)
    slab = (element // E_DEV)[None, :]
    local_ids = face_nbr
    last_entry = halo_send.shape[1] - 1
    own_ids = slab * E_DEV + local_ids
    lower_pos = jnp.clip((slab - 1) * HALO + local_ids - E_DEV, 0, last_entry).astype(jnp.int32)
    lower_ids = (slab - 1) * E_DEV + halo_send[1][lower_pos]
    upper_pos = jnp.clip((slab + 1) * HALO + local_ids - E_DEV - HALO, 0, last_entry).astype(jnp.int32)
    upper_ids = (slab + 1) * E_DEV + halo_send[0][upper_pos]
    result = jnp.where(local_ids < E_DEV, own_ids, jnp.where(local_ids < E_DEV + HALO, lower_ids, upper_ids))
    return jnp.where(local_ids < 0, -1, result).astype(jnp.int32)


def reference(forcing, iterate, kappa_mean, kappa_modes, grad_mats, face_mats, lattice_shift, gen_vector, sweep_counts, face_nbr, halo_send):
    points = lattice_points(gen_vector, lattice_shift, SAMPLES, SAMPLES)
    conduct = conductivity(points, kappa_mean, kappa_modes)
    neighbors = global_neighbors(face_nbr, halo_send)
    inside = neighbors >= 0
    nbr_safe = jnp.maximum(neighbors, 0).astype(jnp.int32)
    coupling, diag_coef = face_coefs(conduct, jnp.take(conduct, nbr_safe, axis=1), inside)
    volume = volume_block(grad_mats)
    blocks = face_blocks(face_mats)
    applied = stiffness(iterate[None], iterate[None], nbr_safe, coupling, diag_coef, volume, blocks)[0]
    earlier = jnp.concatenate([jnp.zeros_like(iterate[:, :1]), iterate[:, :-1]], axis=1)
    residual = forcing - iterate - time_step * applied + earlier
    global_steps = jnp.arange(STEPS, dtype=jnp.int32).astype(forcing.dtype)
    weight = jnp.exp((math.log(alpha_circ) / STEPS) * global_steps)
    scaled = residual * weight[None, :, None, None]
    cosine, sine_table = dft_tables(STEPS, forcing.dtype)
    spectrum_real = jnp.einsum('kn,snde->ksde', cosine, scaled, precision=highest)
    spectrum_imag = -jnp.einsum('kn,snde->ksde', sine_table, scaled, precision=highest)

    def solve(entry):
        source_real, source_imag, frequency = entry
        right_side = jnp.stack([source_real, source_imag])[:, :, None]
        shift_real, shift_imag, theta_real, theta_imag = shifted_terms(frequency[None], STEPS, diag_coef)

        def sweep(sweep_turn, current):
            applied_now = stiffness(current, current, nbr_safe, coupling, diag_coef, volume, blocks)
            image = operator_image(current, applied_now, shift_real, shift_imag)
            return current + times_theta(theta_real, theta_imag, right_side - image)

        result = lax.fori_loop(0, sweep_counts[frequency] - 1, sweep, times_theta(theta_real, theta_imag, right_side))
        return result[:, :, 0]

    solved = lax.map(solve, (spectrum_real, spectrum_imag, jnp.arange(STEPS, dtype=jnp.int32)))
    series = (jnp.einsum('kn,ksde->snde', cosine, solved[:, 0], precision=highest) - jnp.einsum('kn,ksde->snde', sine_table, solved[:, 1], precision=highest)) / STEPS
    unweight = jnp.exp((-math.log(alpha_circ) / STEPS) * global_steps)
    return series * unweight[None, :, None, None]
```

```python
import functools
import math

import jax
import jax.numpy as jnp
from jax import lax
from jax.experimental import pallas as pl
from jax.experimental.pallas import tpu as pltpu
from jax.sharding import PartitionSpec as P

MAXS = 3
alpha_circ = 0.05
time_step = 0.1
relax_rho = 2.3
highest = lax.Precision.HIGHEST
f32, bf16, i32 = jnp.float32, jnp.bfloat16, jnp.int32
FACES = 6


def dot(a, b):
    return jnp.dot(a, b, preferred_element_type=f32)


def split(x):
    hi = x.astype(bf16)
    return hi, (x - hi.astype(f32)).astype(bf16)


def exact_select(x, onehot):
    a, b = split(x)
    c = (x - a.astype(f32) - b.astype(f32)).astype(bf16)
    return dot(a, onehot) + (dot(b, onehot) + dot(c, onehot))


def times_block(stacked, x):
    rows = stacked.shape[0] // 2
    hi, lo = split(x)
    both = dot(stacked, hi)
    return both[:rows] + (both[rows:] + dot(stacked[:rows], lo))


def rows_iota(shape):
    return lax.broadcasted_iota(i32, shape, 0)


def halo_onehot(nbr_row, base, halo):
    elems = nbr_row.shape[1]
    entry = nbr_row - base
    here = (entry >= 0) & (entry < halo)
    entry = jnp.where(here, entry, -2 * halo)
    row = rows_iota((2 * halo, elems))
    left = (row == entry).astype(f32).astype(bf16)
    right = (row == entry + halo).astype(f32).astype(bf16)
    return jnp.concatenate([left, right], axis=1)


def space_even():
    return lax.rem(lax.axis_index("space"), 2) == 0


def sides(even, elems, halo):
    below, above = elems, elems + halo
    return (
        (jnp.where(even, 5, 4), jnp.where(even, above, below)),
        (jnp.where(even, 4, 5), jnp.where(even, below, above)),
    )


def pack_fields(ref, send, outs):
    half = ref.shape[0] // 2
    dofs, elems = ref.shape[1], ref.shape[2]
    group = 4
    width = send.shape[1] // 2
    for j in range(0, half, group):
        left = ref[j : j + group].reshape(group * dofs, elems)
        right = ref[half + j : half + j + group].reshape(group * dofs, elems)
        hi, lo = split(jnp.concatenate([left, right], axis=1))
        got = dot(hi, send) + dot(lo, send)
        for which, out in enumerate(outs):
            out[j * dofs : (j + group) * dofs, :] = got[:, which * width : (which + 1) * width]


def prepare_kernel(
    iterate, halo_send, shift, gen, mean, modes, pack0, pack1, send_out, conduct_out
):
    samples, dofs, elems = iterate.shape
    halo = halo_send.shape[1]
    even = space_even()
    down = jnp.concatenate([halo_send[0:1, :]] * 2, axis=1)
    up = jnp.concatenate([halo_send[1:2, :]] * 2, axis=1)
    lane = lax.broadcasted_iota(i32, (1, 2 * halo), 1)
    row = rows_iota((2 * elems, 2 * halo))
    for which in range(2):
        ids = jnp.where(even == (which == 0), up, down)
        ids = jnp.where(lane < halo, ids, ids + elems)
        send_out[:, which * 2 * halo : (which + 1) * 2 * halo] = (
            (row == ids).astype(f32).astype(bf16)
        )
    position = rows_iota((samples, gen.shape[1]))
    residue = lax.rem(position * gen[...], samples)
    shifted = residue.astype(f32) / samples + shift[...]
    fraction = shifted - jnp.floor(shifted)
    points = 0.5 - jnp.abs(2.0 * fraction - 1.0)
    conduct = mean[...] * (
        1.0 + jnp.dot(points, modes[...], precision=highest, preferred_element_type=f32)
    )
    conduct_out[...] = conduct
    send = send_out[...]
    pack_fields(iterate, send, (pack0, pack1))
    half = samples // 2
    got = exact_select(jnp.concatenate([conduct[:half], conduct[half:]], axis=1), send)
    pack0[half * dofs :, :] = got[:, : 2 * halo]
    pack1[half * dofs :, :] = got[:, 2 * halo :]


def local_part(fields, coef_row, picks, blocks, out, high, low, group):
    dofs, elems = fields.shape[1], fields.shape[2]
    for first in range(0, fields.shape[0], group):
        slots = range(group)
        value = fields[first : first + group]
        hi, lo = split(value.reshape(group * dofs, elems))
        for j in slots:
            a, b = split(value[j] * coef_row(FACES, first + j))
            high[first + j, 0:dofs, :] = a
            low[first + j, 0:dofs, :] = b
        for f in range(FACES):
            pick = picks[:, f * elems : (f + 1) * elems]
            got = (dot(hi, pick) + dot(lo, pick)).reshape(group, dofs, elems)
            at = (f + 1) * dofs
            for j in slots:
                a, b = split(got[j] * coef_row(f, first + j))
                high[first + j, at : at + dofs, :] = a
                low[first + j, at : at + dofs, :] = b
        stacked = blocks[...]
        for j in slots:
            both = dot(stacked, high[first + j])
            out[first + j] = both[:dofs] + (
                both[dofs:] + dot(stacked[:dofs], low[first + j])
            )


def first_local_kernel(
    iterate,
    conduct_ref,
    face_nbr,
    grads,
    face_mats,
    out,
    coefs,
    picks,
    blocks,
    face_blocks,
    halo_picks,
    general,
    high,
    low,
    wide,
):
    samples, dofs, elems = iterate.shape
    halo = halo_picks.shape[1] // 2
    even = space_even()
    row = rows_iota((elems, elems))
    for f in range(FACES):
        picks[:, f * elems : (f + 1) * elems] = (
            (row == face_nbr[f : f + 1, :]).astype(f32).astype(bf16)
        )
    conduct = conduct_ref[...]
    diag = conduct
    for f in range(FACES):
        nbr = face_nbr[f : f + 1, :]
        across = exact_select(conduct, picks[:, f * elems : (f + 1) * elems])
        inside = (nbr >= 0) & (nbr < elems)
        coupling = jnp.where(inside, 0.5 * (conduct + across), 0.0)
        coefs[f] = coupling
        diag = diag + jnp.where(nbr < 0, conduct, coupling)
    coefs[FACES] = diag
    coefs[FACES + 1] = conduct
    volume = (rows_iota((dofs, dofs)) == lax.broadcasted_iota(i32, (dofs, dofs), 1)).astype(f32)
    for d in range(grads.shape[0]):
        volume = volume + lax.dot_general(
            grads[d], grads[d], (((0,), (0,)), ((), ())), precision=highest,
            preferred_element_type=f32,
        )
    wide[...] = jnp.zeros(wide.shape, f32)
    wide[0:dofs, 0:dofs] = volume
    for f in range(FACES):
        block = face_mats[f // 2]
        at = (f + 1) * dofs
        wide[at : at + dofs, 0:dofs] = block if f % 2 == 0 else block.T
    turned = wide[...].T[:dofs, :]
    hi, lo = split(turned)
    blocks[0:dofs, :] = hi
    blocks[dofs:, :] = lo
    for f in range(FACES):
        block = face_mats[f // 2]
        hi, lo = split(block.T if f % 2 == 0 else block)
        face_blocks[f, 0:dofs, :] = hi
        face_blocks[f, dofs:, :] = lo
    for which, (face, base) in enumerate(sides(even, elems, halo)):
        nbr = jnp.where(face == 4, face_nbr[4:5, :], face_nbr[5:6, :])
        halo_picks[which] = halo_onehot(nbr, base, halo)
    crossing = jnp.max(jnp.where(face_nbr[0:4, :] >= elems, 1, 0))
    crossing = crossing + jnp.max(jnp.where(face_nbr[4:5, :] >= elems + halo, 1, 0))
    fifth = face_nbr[5:6, :]
    crossing = crossing + jnp.max(
        jnp.where((fifth >= elems) & (fifth < elems + halo), 1, 0)
    )
    general[0] = crossing
    local_part(
        iterate, lambda f, j: coefs[f, j : j + 1, :], picks, blocks, out, high, low, 4
    )


def halo_blocks(arrived, block, pick, turned):
    dofs = block.shape[1]
    pairs = turned.shape[0] // dofs
    width = turned.shape[1]
    for j in range(0, pairs, 2):
        both = jnp.concatenate(
            [
                arrived[j * dofs : (j + 1) * dofs, :],
                arrived[(j + 1) * dofs : (j + 2) * dofs, :],
            ],
            axis=1,
        )
        got = times_block(block, both)
        turned[j * dofs : (j + 1) * dofs, :] = got[:, :width]
        turned[(j + 1) * dofs : (j + 2) * dofs, :] = got[:, width:]
    hi, lo = split(turned[...])
    return dot(hi, pick) + dot(lo, pick)


def other_sides(general, even, face_nbr, halo, body):
    elems = face_nbr.shape[1]

    @pl.when(general[0] > 0)
    def _():
        for which, (usual, base) in enumerate(sides(even, elems, halo)):

            def step(face, carry, which=which, usual=usual, base=base):
                @pl.when(face != usual)
                def _():
                    body(which, face, halo_onehot(face_nbr[pl.ds(face, 1), :], base, halo))

                return carry

            lax.fori_loop(0, FACES, step, 0)


def add_halo(arrived, even, general, face_nbr, face_blocks, halo_picks, coef_row, total, turned):
    elems = face_nbr.shape[1]
    halo = halo_picks.shape[1] // 2
    half = total.shape[0] // 2
    dofs = total.shape[1]
    usual = sides(even, elems, halo)
    picked = [
        halo_blocks(arrived[w], face_blocks[usual[w][0]], halo_picks[w], turned)
        for w in range(2)
    ]
    for j in range(2 * half):
        rows = slice((j % half) * dofs, (j % half + 1) * dofs)
        cols = slice((j // half) * elems, (j // half + 1) * elems)
        value = total[j]
        for w in range(2):
            value = value + coef_row(usual[w][0], j) * picked[w][rows, cols]
        total[j] = value

    def body(which, face, pick):
        got = halo_blocks(arrived[which], face_blocks[face], pick, turned)
        for j in range(2 * half):
            rows = slice((j % half) * dofs, (j % half + 1) * dofs)
            cols = slice((j // half) * elems, (j // half + 1) * elems)
            total[j] = total[j] + coef_row(face, j) * got[rows, cols]

    other_sides(general, even, face_nbr, halo, body)


def residual_kernel(
    forcing,
    iterate,
    earlier,
    local,
    arrived0,
    arrived1,
    coefs_in,
    face_nbr,
    blocks,
    face_blocks,
    halo_picks,
    general,
    out,
    coefs,
    total,
    turned,
    extra,
    *,
    total_steps,
):
    samples, dofs, elems = forcing.shape
    halo = halo_picks.shape[1] // 2
    half = samples // 2
    even = space_even()
    arrived = (arrived0, arrived1)
    coefs[...] = coefs_in[...]
    conduct = coefs_in[FACES + 1]
    extra[...] = jnp.zeros(extra.shape, f32)

    def add_coupling(which, face, pick):
        got = exact_select(arrived[which][half * dofs :, :], pick)
        nbr = face_nbr[pl.ds(face, 1), :]
        base = sides(even, elems, halo)[which][1]
        here = (nbr >= base) & (nbr < base + halo)
        across = jnp.concatenate([got[:, :elems], got[:, elems:]], axis=0)
        coupling = jnp.where(here, 0.5 * (conduct + across), 0.0)
        coefs[face] = coefs[face] + coupling
        extra[...] = extra[...] + coupling

    for which, (face, _) in enumerate(sides(even, elems, halo)):
        add_coupling(which, face, halo_picks[which])
    other_sides(general, even, face_nbr, halo, add_coupling)
    coefs[FACES] = coefs[FACES] + extra[...]
    volume = blocks[:, 0 : 2 * dofs][:, :dofs]
    for j in range(samples):
        total[j] = local[j] + times_block(volume, iterate[j] * extra[j : j + 1, :])
    add_halo(
        arrived,
        even,
        general,
        face_nbr,
        face_blocks,
        halo_picks,
        lambda f, j: coefs[f, j : j + 1, :],
        total,
        turned,
    )
    step = lax.axis_index("tm")
    weight = jnp.float32(0.0)
    for n in range(total_steps):
        weight = jnp.where(step == n, jnp.float32(alpha_circ ** (n / total_steps)), weight)
    for j in range(samples):
        out[j] = weight * (
            (forcing[j] - iterate[j]) - time_step * total[j] + earlier[j]
        )


def real_fields(total_steps):
    order = [(0, False)]
    if total_steps % 2 == 0:
        order.append((total_steps // 2, False))
    for k in range(1, (total_steps + 1) // 2):
        order += [(k, False), (k, True)]
    return order


def cos_sin(k, n, total_steps):
    turn = 2.0 * math.pi * ((k * n) % total_steps) / total_steps
    c, s = math.cos(turn), math.sin(turn)
    snap = lambda v: float(round(v)) if abs(v - round(v)) < 1e-12 else v
    return snap(c), snap(s)


def weighted(terms):
    total = None
    for constant, value in terms:
        if constant == 0.0:
            continue
        if total is None:
            total = value if constant == 1.0 else constant * value
        elif constant == 1.0:
            total = total + value
        elif constant == -1.0:
            total = total - value
        else:
            total = total + constant * value
    return total


def shift_of(k, total_steps):
    magnitude = alpha_circ ** (1.0 / total_steps)
    c, s = cos_sin(k, 1, total_steps)
    return 1.0 - magnitude * c, magnitude * s


def theta_rows(k, total_steps, diag):
    shift_real, shift_imag = shift_of(k, total_steps)
    denom = shift_real + (time_step * relax_rho) * diag
    if shift_imag == 0.0:
        return 1.0 / denom, None
    modulus = denom * denom + shift_imag * shift_imag
    return denom / modulus, -shift_imag / modulus


def frequencies(total_steps):
    order = real_fields(total_steps)
    return [
        (k, at, order.index((k, True)) if (k, True) in order else None)
        for at, (k, imag) in enumerate(order)
        if not imag
    ]


def my_first(samples):
    return lax.axis_index("tm") * samples


def spectrum_kernel(pieces, coefs, send_ref, spectrum, first_w, pack0, pack1):
    total_steps, samples, dofs, elems = pieces.shape
    first = my_first(samples)
    for s in range(samples):
        diag = coefs[FACES, pl.ds(first + s, 1), :]
        base = s * total_steps
        for k, re, im in frequencies(total_steps):
            tables = [cos_sin(k, n, total_steps) for n in range(total_steps)]
            real = weighted([(tables[n][0], pieces[n, s]) for n in range(total_steps)])
            rate_real, rate_imag = theta_rows(k, total_steps, diag)
            spectrum[base + re] = real
            if im is None:
                first_w[base + re] = rate_real * real
            else:
                imag = weighted([(-tables[n][1], pieces[n, s]) for n in range(total_steps)])
                spectrum[base + im] = imag
                first_w[base + re] = rate_real * real - rate_imag * imag
                first_w[base + im] = rate_real * imag + rate_imag * real
    pack_fields(first_w, send_ref[...], (pack0, pack1))


def sweep_local_kernel(fields, coefs, picks, blocks, out, high, low, *, total_steps):
    first = my_first(fields.shape[0] // total_steps)
    local_part(
        fields,
        lambda f, j: coefs[f, pl.ds(first + j // total_steps, 1), :],
        picks,
        blocks,
        out,
        high,
        low,
        4,
    )


def updated_fields(current, spectrum, total, coefs, counts, turn, total_steps, store):
    samples = current.shape[0] // total_steps
    first = my_first(samples)
    for s in range(samples):
        diag = coefs[FACES, pl.ds(first + s, 1), :]
        base = s * total_steps
        for k, re, im in frequencies(total_steps):
            active = counts[k] > turn + 1
            shift_real, shift_imag = shift_of(k, total_steps)
            rate_real, rate_imag = theta_rows(k, total_steps, diag)
            value = current[base + re]
            rest = spectrum[base + re] - (shift_real * value + time_step * total[base + re])
            if im is None:
                store(base + re, jnp.where(active, value + rate_real * rest, value))
            else:
                other = current[base + im]
                rest = rest + shift_imag * other
                rest_imag = spectrum[base + im] - (
                    shift_real * other + shift_imag * value + time_step * total[base + im]
                )
                store(
                    base + re,
                    jnp.where(active, value + (rate_real * rest - rate_imag * rest_imag), value),
                )
                store(
                    base + im,
                    jnp.where(active, other + (rate_real * rest_imag + rate_imag * rest), other),
                )


def sweep_update_kernel(
    counts,
    general,
    current,
    spectrum,
    local,
    arrived0,
    arrived1,
    coefs,
    face_nbr,
    face_blocks,
    halo_picks,
    *rest,
    turn,
    total_steps,
    last,
):
    even = space_even()
    if last:
        series, total, turned, solved = rest
    else:
        send_ref, solved, pack0, pack1, total, turned = rest
    fields, dofs, elems = current.shape
    samples = fields // total_steps
    first = my_first(samples)
    total[...] = local[...]
    add_halo(
        (arrived0, arrived1),
        even,
        general,
        face_nbr,
        face_blocks,
        halo_picks,
        lambda f, j: coefs[f, pl.ds(first + j // total_steps, 1), :],
        total,
        turned,
    )

    def store(at, value):
        solved[at] = value

    updated_fields(current, spectrum, total, coefs, counts, turn, total_steps, store)
    if not last:
        pack_fields(solved, send_ref[...], (pack0, pack1))
        return
    for s in range(samples):
        base = s * total_steps
        for n in range(total_steps):
            scale = alpha_circ ** (-n / total_steps) / total_steps
            terms = []
            for k, re, im in frequencies(total_steps):
                c, sn = cos_sin(k, n, total_steps)
                if im is None:
                    terms.append((c, solved[base + re]))
                else:
                    terms += [(2.0 * c, solved[base + re]), (-2.0 * sn, solved[base + im])]
            series[n, s] = scale * weighted(terms)


vmem = pl.BlockSpec(memory_space=pltpu.VMEM)
smem = pl.BlockSpec(memory_space=pltpu.SMEM)


def run(kernel, inputs, outs, scratch=(), in_smem=(), out_smem=(), flops=10**9):
    spec = lambda i, small: smem if i in small else vmem
    return pl.pallas_call(
        kernel,
        out_shape=[jax.ShapeDtypeStruct(*o) for o in outs],
        in_specs=[spec(i, in_smem) for i in range(len(inputs))],
        out_specs=[spec(i, out_smem) for i in range(len(outs))],
        scratch_shapes=[pltpu.VMEM(*s) for s in scratch],
        compiler_params=pltpu.CompilerParams(vmem_limit_bytes=40 << 20),
        cost_estimate=pl.CostEstimate(flops=flops, bytes_accessed=1 << 22, transcendentals=0),
    )(*inputs)


def neighbour_swap(value, start):
    count = lax.axis_size("space")
    pairs = []
    for low in range(start, count - 1, 2):
        pairs += [(low, low + 1), (low + 1, low)]
    return lax.ppermute(value, "space", pairs)


def per_device(
    forcing,
    iterate,
    kappa_mean,
    kappa_modes,
    grad_mats,
    face_mats,
    lattice_shift,
    gen_vector,
    sweep_counts,
    face_nbr,
    halo_send,
):
    samples, steps_dev, dofs, elems = forcing.shape
    halo = halo_send.shape[1]
    devs = lax.axis_size("tm")
    total_steps = steps_dev * devs
    part = samples // devs
    half = samples // 2
    cube = (samples, dofs, elems)
    forcing = forcing.reshape(cube)
    iterate = iterate.reshape(cube)
    earlier = lax.ppermute(iterate, "tm", [(i, i + 1) for i in range(devs - 1)])

    rows = half * dofs
    pack0, pack1, send, conduct = run(
        prepare_kernel,
        (
            iterate,
            halo_send,
            lattice_shift.reshape(1, -1),
            gen_vector.reshape(1, -1),
            kappa_mean.reshape(1, -1),
            kappa_modes,
        ),
        [
            ((rows + half, 2 * halo), f32),
            ((rows + half, 2 * halo), f32),
            ((2 * elems, 4 * halo), bf16),
            ((samples, elems), f32),
        ],
    )
    arrived0 = neighbour_swap(pack0, 0)
    arrived1 = neighbour_swap(pack1, 1)
    blocks_wide = (FACES + 1) * dofs
    splits = [((samples, blocks_wide, elems), bf16)] * 2
    local, coefs, picks, blocks, face_blocks, halo_picks, general = run(
        first_local_kernel,
        (iterate, conduct, face_nbr, grad_mats, face_mats),
        [
            (cube, f32),
            ((FACES + 2, samples, elems), f32),
            ((elems, FACES * elems), bf16),
            ((2 * dofs, blocks_wide), bf16),
            ((FACES, 2 * dofs, dofs), bf16),
            ((2, 2 * halo, 2 * elems), bf16),
            ((1,), i32),
        ],
        splits + [((blocks_wide, 2 * dofs), f32)],
        out_smem=(6,),
    )
    turned = ((rows, 2 * halo), f32)
    scaled, coefs = run(
        functools.partial(residual_kernel, total_steps=total_steps),
        (
            forcing,
            iterate,
            earlier,
            local,
            arrived0,
            arrived1,
            coefs,
            face_nbr,
            blocks,
            face_blocks,
            halo_picks,
            general,
        ),
        [(cube, f32), ((FACES + 2, samples, elems), f32)],
        [(cube, f32), turned, ((samples, elems), f32)],
        in_smem=(11,),
    )
    pieces = lax.all_to_all(scaled, "tm", split_axis=0, concat_axis=0, tiled=True)
    pieces = pieces.reshape(total_steps, part, dofs, elems)
    packs = [((rows, 2 * halo), f32)] * 2
    spectrum, current, pack0, pack1 = run(
        spectrum_kernel,
        (pieces, coefs, send),
        [(cube, f32), (cube, f32)] + packs,
    )
    for turn in range(MAXS - 1):
        arrived0 = neighbour_swap(pack0, 0)
        arrived1 = neighbour_swap(pack1, 1)
        (local,) = run(
            functools.partial(sweep_local_kernel, total_steps=total_steps),
            (current, coefs, picks, blocks),
            [(cube, f32)],
            splits,
        )
        last = turn == MAXS - 2
        inputs = (
            sweep_counts,
            general,
            current,
            spectrum,
            local,
            arrived0,
            arrived1,
            coefs,
            face_nbr,
            face_blocks,
            halo_picks,
        )
        kernel = functools.partial(
            sweep_update_kernel, turn=turn, total_steps=total_steps, last=last
        )
        if last:
            (series,) = run(
                kernel,
                inputs,
                [((total_steps, part, dofs, elems), f32)],
                [(cube, f32), turned, (cube, f32)],
                in_smem=(0, 1),
            )
        else:
            current, pack0, pack1 = run(
                kernel,
                inputs + (send,),
                [(cube, f32)] + packs,
                [(cube, f32), turned],
                in_smem=(0, 1),
            )
    series = series.reshape(cube)
    restored = lax.all_to_all(series, "tm", split_axis=0, concat_axis=0, tiled=True)
    return restored.reshape(samples, steps_dev, dofs, elems)


def solution(mesh):
    placed = (
        P("groups", "tm", None, "space"),
        P("groups", "tm", None, "space"),
        P("space"),
        P(None, "space"),
        P(),
        P(),
        P("groups"),
        P(),
        P(),
        P(None, "space"),
        P(None, "space"),
    )
    return jax.shard_map(
        per_device,
        mesh=mesh,
        in_specs=placed,
        out_specs=P("groups", "tm", None, "space"),
        check_vma=False,
    )
```

```python
import functools
import math

import jax
import jax.numpy as jnp
from jax import lax
from jax.experimental import pallas as pl
from jax.experimental.pallas import tpu as pltpu
from jax.sharding import PartitionSpec as P

MAXS = 3
alpha_circ = 0.05
time_step = 0.1
relax_rho = 2.3
highest = lax.Precision.HIGHEST
f32, bf16, i32 = jnp.float32, jnp.bfloat16, jnp.int32
FACES = 6
GROUPS = 1


def dot(a, b):
    return jnp.dot(a, b, preferred_element_type=f32)


def split(x):
    hi = x.astype(bf16)
    return hi, (x - hi.astype(f32)).astype(bf16)


def exact_select(x, onehot):
    a, b = split(x)
    c = (x - a.astype(f32) - b.astype(f32)).astype(bf16)
    return dot(a, onehot) + (dot(b, onehot) + dot(c, onehot))


def times_block(stacked, x):
    rows = stacked.shape[0] // 2
    hi, lo = split(x)
    both = dot(stacked, hi)
    return both[:rows] + (both[rows:] + dot(stacked[:rows], lo))


def rows_iota(shape):
    return lax.broadcasted_iota(i32, shape, 0)


def halo_onehot(nbr_row, base, halo):
    elems = nbr_row.shape[1]
    entry = nbr_row - base
    here = (entry >= 0) & (entry < halo)
    entry = jnp.where(here, entry, -2 * halo)
    row = rows_iota((2 * halo, elems))
    left = (row == entry).astype(f32).astype(bf16)
    right = (row == entry + halo).astype(f32).astype(bf16)
    return jnp.concatenate([left, right], axis=1)


def space_even():
    return lax.rem(lax.axis_index("space") + lax.axis_index("tm"), 2) == 0


def sides(even, elems, halo):
    below, above = elems, elems + halo
    return (
        (jnp.where(even, 5, 4), jnp.where(even, above, below)),
        (jnp.where(even, 4, 5), jnp.where(even, below, above)),
    )


def group_size(count):
    return next(size for size in (4, 3, 2, 1) if count % size == 0)


def pack_group(ref, left, right, send, first, outs):
    dofs = ref.shape[1]
    width = send.shape[1] // 2
    sides_by_side = [jnp.concatenate([ref[i] for i in side], axis=0) for side in (left, right)]
    hi, lo = split(jnp.concatenate(sides_by_side, axis=1))
    got = dot(hi, send) + dot(lo, send)
    rows = slice(first * dofs, (first + len(left)) * dofs)
    for which, out in enumerate(outs):
        out[rows, :] = got[:, which * width : (which + 1) * width]


def pack_fields(ref, fields, send, outs):
    half = len(fields) // 2
    size = group_size(half)
    for j in range(0, half, size):
        pack_group(
            ref, fields[j : j + size], fields[half + j : half + j + size], send, j, outs
        )


def prepare_kernel(
    iterate_in,
    halo_send_in,
    shift_in,
    gen_in,
    mean_in,
    modes_in,
    pack0,
    pack1,
    send_out,
    conduct_out,
    iterate,
    halo_send,
    shift,
    gen,
    mean,
    modes,
    small_done,
    field_done,
):
    samples, dofs, elems = iterate.shape
    halo = halo_send.shape[1]
    half = samples // 2
    size = group_size(half)
    small = [
        pltpu.make_async_copy(source, target, small_done.at[i])
        for i, (source, target) in enumerate(
            (
                (halo_send_in, halo_send),
                (shift_in, shift),
                (gen_in, gen),
                (mean_in, mean),
                (modes_in, modes),
            )
        )
    ]
    large = []
    for j in range(0, half, size):
        for at in (j, half + j):
            part = pl.ds(at, size)
            large.append(
                pltpu.make_async_copy(
                    iterate_in.at[part], iterate.at[part], field_done.at[len(large)]
                )
            )
    for copy in small + large:
        copy.start()
    for copy in small:
        copy.wait()
    even = space_even()
    down = jnp.concatenate([halo_send[0:1, :]] * 2, axis=1)
    up = jnp.concatenate([halo_send[1:2, :]] * 2, axis=1)
    lane = lax.broadcasted_iota(i32, (1, 2 * halo), 1)
    row = rows_iota((2 * elems, 2 * halo))
    for which in range(2):
        ids = jnp.where(even == (which == 0), up, down)
        ids = jnp.where(lane < halo, ids, ids + elems)
        send_out[:, which * 2 * halo : (which + 1) * 2 * halo] = (
            (row == ids).astype(f32).astype(bf16)
        )
    position = rows_iota((samples, gen.shape[1]))
    residue = lax.rem(position * gen[...], samples)
    shifted = residue.astype(f32) / samples + shift[...]
    fraction = shifted - jnp.floor(shifted)
    points = 0.5 - jnp.abs(2.0 * fraction - 1.0)
    conduct = mean[...] * (
        1.0 + jnp.dot(points, modes[...], precision=highest, preferred_element_type=f32)
    )
    conduct_out[...] = conduct
    send = send_out[...]
    got = exact_select(jnp.concatenate([conduct[:half], conduct[half:]], axis=1), send)
    pack0[half * dofs :, :] = got[:, : 2 * halo]
    pack1[half * dofs :, :] = got[:, 2 * halo :]
    for at, j in enumerate(range(0, half, size)):
        large[2 * at].wait()
        large[2 * at + 1].wait()
        left = list(range(j, j + size))
        pack_group(iterate, left, [half + i for i in left], send, j, (pack0, pack1))


def local_part(fields, slots, coef_row, picks, blocks, out, high, low):
    dofs, elems = fields.shape[1], fields.shape[2]
    size = group_size(len(slots))
    for first in range(0, len(slots), size):
        group = range(first, first + size)
        values = [fields[slots[t]] for t in group]
        hi, lo = split(jnp.concatenate(values, axis=0))
        for t, value in zip(group, values):
            a, b = split(value * coef_row(FACES, t))
            high[t, 0:dofs, :] = a
            low[t, 0:dofs, :] = b
        for f in range(FACES):
            pick = picks[:, f * elems : (f + 1) * elems]
            got = dot(hi, pick) + dot(lo, pick)
            at = (f + 1) * dofs
            for i, t in enumerate(group):
                a, b = split(got[i * dofs : (i + 1) * dofs] * coef_row(f, t))
                high[t, at : at + dofs, :] = a
                low[t, at : at + dofs, :] = b
        stacked = blocks[...]
        for t in group:
            both = dot(stacked, high[t])
            out[slots[t]] = both[:dofs] + (both[dofs:] + dot(stacked[:dofs], low[t]))


def first_local_kernel(
    iterate,
    conduct_ref,
    face_nbr,
    grads,
    face_mats,
    counts_in,
    out,
    coefs,
    picks,
    blocks,
    face_blocks,
    halo_picks,
    general,
    counts,
    high,
    low,
    wide,
):
    for k in range(counts.shape[0]):
        counts[k] = counts_in[0, k]
    samples, dofs, elems = iterate.shape
    halo = halo_picks.shape[1] // 2
    even = space_even()
    row = rows_iota((elems, elems))
    for f in range(FACES):
        picks[:, f * elems : (f + 1) * elems] = (
            (row == face_nbr[f : f + 1, :]).astype(f32).astype(bf16)
        )
    conduct = conduct_ref[...]
    diag = conduct
    for f in range(FACES):
        nbr = face_nbr[f : f + 1, :]
        across = exact_select(conduct, picks[:, f * elems : (f + 1) * elems])
        inside = (nbr >= 0) & (nbr < elems)
        coupling = jnp.where(inside, 0.5 * (conduct + across), 0.0)
        coefs[f] = coupling
        diag = diag + jnp.where(nbr < 0, conduct, coupling)
    coefs[FACES] = diag
    coefs[FACES + 1] = conduct
    volume = (rows_iota((dofs, dofs)) == lax.broadcasted_iota(i32, (dofs, dofs), 1)).astype(f32)
    for d in range(grads.shape[0]):
        volume = volume + lax.dot_general(
            grads[d], grads[d], (((0,), (0,)), ((), ())), precision=highest,
            preferred_element_type=f32,
        )
    wide[...] = jnp.zeros(wide.shape, f32)
    wide[0:dofs, 0:dofs] = volume
    for f in range(FACES):
        block = face_mats[f // 2]
        at = (f + 1) * dofs
        wide[at : at + dofs, 0:dofs] = block if f % 2 == 0 else block.T
    turned = wide[...].T[:dofs, :]
    hi, lo = split(turned)
    blocks[0:dofs, :] = hi
    blocks[dofs:, :] = lo
    for f in range(FACES):
        block = face_mats[f // 2]
        hi, lo = split(block.T if f % 2 == 0 else block)
        face_blocks[f, 0:dofs, :] = hi
        face_blocks[f, dofs:, :] = lo
    for which, (face, base) in enumerate(sides(even, elems, halo)):
        nbr = jnp.where(face == 4, face_nbr[4:5, :], face_nbr[5:6, :])
        halo_picks[which] = halo_onehot(nbr, base, halo)
    crossing = jnp.max(jnp.where(face_nbr[0:4, :] >= elems, 1, 0))
    crossing = crossing + jnp.max(jnp.where(face_nbr[4:5, :] >= elems + halo, 1, 0))
    fifth = face_nbr[5:6, :]
    crossing = crossing + jnp.max(
        jnp.where((fifth >= elems) & (fifth < elems + halo), 1, 0)
    )
    general[0] = crossing
    local_part(
        iterate,
        list(range(samples)),
        lambda f, t: coefs[f, t : t + 1, :],
        picks,
        blocks,
        out,
        high,
        low,
    )


def halo_blocks(arrived, block, pick, turned):
    dofs = block.shape[1]
    pairs = turned.shape[0] // dofs
    width = turned.shape[1]
    size = 2 if pairs % 2 == 0 else 1
    for j in range(0, pairs, size):
        rows = [slice((j + i) * dofs, (j + i + 1) * dofs) for i in range(size)]
        got = times_block(block, jnp.concatenate([arrived[r, :] for r in rows], axis=1))
        for i, r in enumerate(rows):
            turned[r, :] = got[:, i * width : (i + 1) * width]
    hi, lo = split(turned[...])
    return dot(hi, pick) + dot(lo, pick)


def other_sides(general, even, face_nbr, halo, body):
    elems = face_nbr.shape[1]

    @pl.when(general[0] > 0)
    def _():
        for which, (usual, base) in enumerate(sides(even, elems, halo)):

            def step(face, carry, which=which, usual=usual, base=base):
                @pl.when(face != usual)
                def _():
                    body(which, face, halo_onehot(face_nbr[pl.ds(face, 1), :], base, halo))

                return carry

            lax.fori_loop(0, FACES, step, 0)


def add_halo(
    arrived, even, general, face_nbr, face_blocks, halo_picks, slots, coef_row, total, turned
):
    elems = face_nbr.shape[1]
    halo = halo_picks.shape[1] // 2
    dofs = total.shape[1]
    half = turned.shape[0] // dofs
    usual = sides(even, elems, halo)
    picked = [
        halo_blocks(arrived[w], face_blocks[usual[w][0]], halo_picks[w], turned)
        for w in range(2)
    ]

    def place(t):
        row, col = t % half * dofs, t // half * elems
        return slice(row, row + dofs), slice(col, col + elems)

    for t, field in enumerate(slots):
        value = total[field]
        for w in range(2):
            value = value + coef_row(usual[w][0], t) * picked[w][place(t)]
        total[field] = value

    def body(which, face, pick):
        got = halo_blocks(arrived[which], face_blocks[face], pick, turned)
        for t, field in enumerate(slots):
            total[field] = total[field] + coef_row(face, t) * got[place(t)]

    other_sides(general, even, face_nbr, halo, body)


def residual_kernel(
    forcing,
    iterate,
    earlier,
    local,
    arrived0,
    arrived1,
    coefs_in,
    face_nbr,
    blocks,
    face_blocks,
    halo_picks,
    general,
    *rest,
    total_steps,
    groups,
):
    outs = rest[: groups * total_steps]
    coefs, total, turned, extra = rest[groups * total_steps :]
    samples, dofs, elems = forcing.shape
    halo = halo_picks.shape[1] // 2
    half = samples // 2
    even = space_even()
    arrived = (arrived0, arrived1)
    coefs[...] = coefs_in[...]
    conduct = coefs_in[FACES + 1]
    extra[...] = jnp.zeros(extra.shape, f32)

    def add_coupling(which, face, pick):
        got = exact_select(arrived[which][half * dofs :, :], pick)
        nbr = face_nbr[pl.ds(face, 1), :]
        base = sides(even, elems, halo)[which][1]
        here = (nbr >= base) & (nbr < base + halo)
        across = jnp.concatenate([got[:, :elems], got[:, elems:]], axis=0)
        coupling = jnp.where(here, 0.5 * (conduct + across), 0.0)
        coefs[face] = coefs[face] + coupling
        extra[...] = extra[...] + coupling

    for which, (face, _) in enumerate(sides(even, elems, halo)):
        add_coupling(which, face, halo_picks[which])
    other_sides(general, even, face_nbr, halo, add_coupling)
    coefs[FACES] = coefs[FACES] + extra[...]
    volume = blocks[:, 0 : 2 * dofs][:, :dofs]
    for j in range(samples):
        total[j] = local[j] + times_block(volume, iterate[j] * extra[j : j + 1, :])
    add_halo(
        arrived,
        even,
        general,
        face_nbr,
        face_blocks,
        halo_picks,
        list(range(samples)),
        lambda f, t: coefs[f, t : t + 1, :],
        total,
        turned,
    )
    step = lax.axis_index("tm")
    weight = jnp.float32(0.0)
    for n in range(total_steps):
        weight = jnp.where(step == n, jnp.float32(alpha_circ ** (n / total_steps)), weight)
    gate = jnp.where(step > 0, weight, 0.0)
    size = samples // (groups * total_steps)
    for which, out in enumerate(outs):
        at, turn = divmod(which, total_steps)
        for i in range(size):
            j = (partner(step, turn, total_steps) * groups + at) * size + i
            out[i] = weight * (
                (forcing[j] - iterate[j]) - time_step * total[j]
            ) + gate * earlier[j]


def partner(rank, turn, count):
    if count & (count - 1) == 0:
        return rank ^ turn
    return lax.rem(turn + count - rank, count)


def real_fields(total_steps):
    order = [(0, False)]
    if total_steps % 2 == 0:
        order.append((total_steps // 2, False))
    for k in range(1, (total_steps + 1) // 2):
        order += [(k, False), (k, True)]
    return order


def cos_sin(k, n, total_steps):
    turn = 2.0 * math.pi * ((k * n) % total_steps) / total_steps
    c, s = math.cos(turn), math.sin(turn)
    snap = lambda v: float(round(v)) if abs(v - round(v)) < 1e-12 else v
    return snap(c), snap(s)


def weighted(terms):
    total = None
    for constant, value in terms:
        if constant == 0.0:
            continue
        if total is None:
            total = value if constant == 1.0 else constant * value
        elif constant == 1.0:
            total = total + value
        elif constant == -1.0:
            total = total - value
        else:
            total = total + constant * value
    return total


def shift_of(k, total_steps):
    magnitude = alpha_circ ** (1.0 / total_steps)
    c, s = cos_sin(k, 1, total_steps)
    return 1.0 - magnitude * c, magnitude * s


def theta_rows(k, total_steps, diag):
    shift_real, shift_imag = shift_of(k, total_steps)
    denom = shift_real + (time_step * relax_rho) * diag
    if shift_imag == 0.0:
        return 1.0 / denom, None
    modulus = denom * denom + shift_imag * shift_imag
    return denom / modulus, -shift_imag / modulus


def frequencies(total_steps):
    order = real_fields(total_steps)
    return [
        (k, at, order.index((k, True)) if (k, True) in order else None)
        for at, (k, imag) in enumerate(order)
        if not imag
    ]


def kept_slots(counts, samples, total_steps):
    skip = jnp.int32(0)
    for k, re, _ in frequencies(total_steps):
        skip = jnp.where(counts[k] == 1, re, skip)
    kept = total_steps - 1
    slots = []
    for t in range(samples * kept):
        s, i = divmod(t, kept)
        slots.append(s * total_steps + jnp.where(skip <= i, i + 1, i))
    return slots


def even_slots(slots):
    return slots + slots[: len(slots) % 2]


def my_first(samples, at, groups):
    return (lax.axis_index("tm") * groups + at) * samples


def sample_row(coefs, total_steps, first):
    kept = total_steps - 1
    return lambda f, t: coefs[f, pl.ds(first + t // kept, 1), :]


def spectrum_kernel(counts, coefs, send_ref, *rest, total_steps, at, groups):
    arrived, (spectrum, first_w, pack0, pack1, pieces) = (
        rest[:total_steps],
        rest[total_steps:],
    )
    samples = arrived[0].shape[0]
    first = my_first(samples, at, groups)
    rank = lax.axis_index("tm")
    for turn, piece in enumerate(arrived):
        pieces[partner(rank, turn, total_steps)] = piece[...]
    for s in range(samples):
        diag = coefs[FACES, pl.ds(first + s, 1), :]
        base = s * total_steps
        for k, re, im in frequencies(total_steps):
            tables = [cos_sin(k, n, total_steps) for n in range(total_steps)]
            real = weighted([(tables[n][0], pieces[n, s]) for n in range(total_steps)])
            rate_real, rate_imag = theta_rows(k, total_steps, diag)
            spectrum[base + re] = real
            if im is None:
                first_w[base + re] = rate_real * real
            else:
                imag = weighted([(-tables[n][1], pieces[n, s]) for n in range(total_steps)])
                spectrum[base + im] = imag
                first_w[base + re] = rate_real * real - rate_imag * imag
                first_w[base + im] = rate_real * imag + rate_imag * real
    slots = kept_slots(counts, samples, total_steps)
    pack_fields(first_w, even_slots(slots), send_ref[...], (pack0, pack1))


def sweep_local_kernel(
    counts, fields, coefs, picks, blocks, out, high, low, *, total_steps, at, groups
):
    samples = fields.shape[0] // total_steps
    local_part(
        fields,
        kept_slots(counts, samples, total_steps),
        sample_row(coefs, total_steps, my_first(samples, at, groups)),
        picks,
        blocks,
        out,
        high,
        low,
    )


def updated_fields(current, spectrum, total, coefs, counts, turn, total_steps, first, store):
    samples = current.shape[0] // total_steps
    for s in range(samples):
        diag = coefs[FACES, pl.ds(first + s, 1), :]
        base = s * total_steps
        for k, re, im in frequencies(total_steps):
            active = counts[k] > turn + 1
            shift_real, shift_imag = shift_of(k, total_steps)
            rate_real, rate_imag = theta_rows(k, total_steps, diag)
            value = current[base + re]
            rest = spectrum[base + re] - (shift_real * value + time_step * total[base + re])
            if im is None:
                store(base + re, jnp.where(active, value + rate_real * rest, value))
            else:
                other = current[base + im]
                rest = rest + shift_imag * other
                rest_imag = spectrum[base + im] - (
                    shift_real * other + shift_imag * value + time_step * total[base + im]
                )
                store(
                    base + re,
                    jnp.where(active, value + (rate_real * rest - rate_imag * rest_imag), value),
                )
                store(
                    base + im,
                    jnp.where(active, other + (rate_real * rest_imag + rate_imag * rest), other),
                )


def sweep_update_kernel(
    counts,
    general,
    current,
    spectrum,
    local,
    arrived0,
    arrived1,
    coefs,
    face_nbr,
    face_blocks,
    halo_picks,
    *rest,
    turn,
    total_steps,
    last,
    at,
    groups,
):
    even = space_even()
    if last:
        outs, (total, turned, solved) = rest[:total_steps], rest[total_steps:]
    else:
        send_ref, solved, pack0, pack1, total, turned = rest
    fields = current.shape[0]
    samples = fields // total_steps
    first = my_first(samples, at, groups)
    slots = kept_slots(counts, samples, total_steps)
    total[...] = local[...]
    add_halo(
        (arrived0, arrived1),
        even,
        general,
        face_nbr,
        face_blocks,
        halo_picks,
        slots,
        sample_row(coefs, total_steps, first),
        total,
        turned,
    )

    def store(field, value):
        solved[field] = value

    updated_fields(current, spectrum, total, coefs, counts, turn, total_steps, first, store)
    if not last:
        pack_fields(solved, even_slots(slots), send_ref[...], (pack0, pack1))
        return
    rank = lax.axis_index("tm")
    for s in range(samples):
        base = s * total_steps
        for n in range(total_steps):
            scale = alpha_circ ** (-n / total_steps) / total_steps
            terms = []
            for k, re, im in frequencies(total_steps):
                c, sn = cos_sin(k, n, total_steps)
                if im is None:
                    terms.append((c, solved[base + re]))
                else:
                    terms += [(2.0 * c, solved[base + re]), (-2.0 * sn, solved[base + im])]
            total[n * samples + s] = scale * weighted(terms)
    for turn_to, out in enumerate(outs):
        step = partner(rank, turn_to, total_steps)
        for s in range(samples):
            out[s] = total[step * samples + s]


def assemble_kernel(*rest, total_steps, groups):
    pieces, (out, done) = rest[:-2], rest[-2:]
    size = pieces[0].shape[0]
    rank = lax.axis_index("tm")
    copies = []
    for which, piece in enumerate(pieces):
        at, turn = divmod(which, total_steps)
        first = (partner(rank, turn, total_steps) * groups + at) * size
        copies.append(
            pltpu.make_async_copy(piece, out.at[pl.ds(first, size)], done.at[which])
        )
    for copy in copies:
        copy.start()
    for copy in copies:
        copy.wait()


vmem = pl.BlockSpec(memory_space=pltpu.VMEM)
smem = pl.BlockSpec(memory_space=pltpu.SMEM)


def run(
    kernel, inputs, outs, scratch=(), in_smem=(), out_smem=(), in_hbm=(), out_hbm=(), flops=10**9
):
    def spec(i, small, outside=()):
        if i in outside:
            return pl.BlockSpec(memory_space=pltpu.HBM)
        return smem if i in small else vmem

    inputs = [
        pltpu.with_memory_space_constraint(value, pltpu.HBM) if i in in_hbm else value
        for i, value in enumerate(inputs)
    ]
    return pl.pallas_call(
        kernel,
        out_shape=[jax.ShapeDtypeStruct(*o) for o in outs],
        in_specs=[spec(i, in_smem, in_hbm) for i in range(len(inputs))],
        out_specs=[spec(i, out_smem, out_hbm) for i in range(len(outs))],
        scratch_shapes=[pltpu.VMEM(*s) if isinstance(s, tuple) else s for s in scratch],
        compiler_params=pltpu.CompilerParams(vmem_limit_bytes=40 << 20),
        cost_estimate=pl.CostEstimate(flops=flops, bytes_accessed=1 << 22, transcendentals=0),
    )(*inputs)


def neighbour_swap(value, start):
    axes = ("groups", "tm", "space")
    parts, devs, count = (lax.axis_size(axis) for axis in axes)
    pairs = []
    for part in range(parts):
        for tm in range(devs):
            for space in range(count):
                step = 1 if (space + tm + start) % 2 == 0 else -1
                to_part, to_space = part, space + step
                if not 0 <= to_space < count:
                    to_part, to_space = part ^ 1, space
                if to_part < parts:
                    pairs.append(
                        ((part * devs + tm) * count + space, (to_part * devs + tm) * count + to_space)
                    )
    return lax.ppermute(value, axes, pairs)


def time_swap(value, turn):
    count = lax.axis_size("tm")
    pairs = [(i, int(partner(i, turn, count))) for i in range(count)]
    return value if turn == 0 else lax.ppermute(value, "tm", pairs)


def per_device(
    forcing,
    iterate,
    kappa_mean,
    kappa_modes,
    grad_mats,
    face_mats,
    lattice_shift,
    gen_vector,
    sweep_counts,
    face_nbr,
    halo_send,
):
    samples, steps_dev, dofs, elems = forcing.shape
    halo = halo_send.shape[1]
    devs = lax.axis_size("tm")
    total_steps = steps_dev * devs
    part = samples // devs
    half = samples // 2
    cube = (samples, dofs, elems)
    forcing = forcing.reshape(cube)
    iterate = iterate.reshape(cube)
    earlier = lax.ppermute(iterate, "tm", [(i, (i + 1) % devs) for i in range(devs)])
    rows = half * dofs
    copies = 2 * (half // group_size(half))
    pack0, pack1, send, conduct, iterate = run(
        prepare_kernel,
        (
            iterate,
            halo_send,
            lattice_shift.reshape(1, -1),
            gen_vector.reshape(1, -1),
            kappa_mean.reshape(1, -1),
            kappa_modes,
        ),
        [
            ((rows + half, 2 * halo), f32),
            ((rows + half, 2 * halo), f32),
            ((2 * elems, 4 * halo), bf16),
            ((samples, elems), f32),
            (cube, f32),
        ],
        [
            (halo_send.shape, i32),
            ((1, lattice_shift.shape[0]), f32),
            ((1, gen_vector.shape[0]), i32),
            ((1, elems), f32),
            (kappa_modes.shape, f32),
            pltpu.SemaphoreType.DMA((5,)),
            pltpu.SemaphoreType.DMA((copies,)),
        ],
        in_hbm=range(6),
    )
    arrived0 = neighbour_swap(pack0, 0)
    arrived1 = neighbour_swap(pack1, 1)
    blocks_wide = (FACES + 1) * dofs
    splits = lambda count: [((count, blocks_wide, elems), bf16)] * 2
    local, coefs, picks, blocks, face_blocks, halo_picks, general, counts = run(
        first_local_kernel,
        (iterate, conduct, face_nbr, grad_mats, face_mats, sweep_counts.reshape(1, -1)),
        [
            (cube, f32),
            ((FACES + 2, samples, elems), f32),
            ((elems, FACES * elems), bf16),
            ((2 * dofs, blocks_wide), bf16),
            ((FACES, 2 * dofs, dofs), bf16),
            ((2, 2 * halo, 2 * elems), bf16),
            ((1,), i32),
            (sweep_counts.shape, i32),
        ],
        splits(samples) + [((blocks_wide, 2 * dofs), f32)],
        out_smem=(6, 7),
        flops=4 * 10**9,
    )
    groups = GROUPS if part % GROUPS == 0 else 1
    share = part // groups
    piece = ((share, dofs, elems), f32)
    *scaled, coefs = run(
        functools.partial(residual_kernel, total_steps=total_steps, groups=groups),
        (
            forcing,
            iterate,
            earlier,
            local,
            arrived0,
            arrived1,
            coefs,
            face_nbr,
            blocks,
            face_blocks,
            halo_picks,
            general,
        ),
        [piece] * (groups * devs) + [((FACES + 2, samples, elems), f32)],
        [(cube, f32), ((rows, 2 * halo), f32), ((samples, elems), f32)],
        in_smem=(11,),
    )
    fields = share * total_steps
    swept = share * (total_steps - 1)
    some = (fields, dofs, elems)
    turned = ((((swept + 1) // 2) * dofs, 2 * halo), f32)
    restored = []
    for at in range(groups):
        mine = dict(total_steps=total_steps, at=at, groups=groups)
        pieces = [time_swap(scaled[at * devs + turn], turn) for turn in range(devs)]
        spectrum, current, pack0, pack1 = run(
            functools.partial(spectrum_kernel, **mine),
            (counts, coefs, send, *pieces),
            [(some, f32), (some, f32), turned, turned],
            [((total_steps, share, dofs, elems), f32)],
            in_smem=(0,),
        )
        for turn in range(MAXS - 1):
            arrived0 = neighbour_swap(pack0, 0)
            arrived1 = neighbour_swap(pack1, 1)
            (local,) = run(
                functools.partial(sweep_local_kernel, **mine),
                (counts, current, coefs, picks, blocks),
                [(some, f32)],
                splits(swept),
                in_smem=(0,),
                flops=3 * 10**9 // groups,
            )
            last = turn == MAXS - 2
            inputs = (
                counts,
                general,
                current,
                spectrum,
                local,
                arrived0,
                arrived1,
                coefs,
                face_nbr,
                face_blocks,
                halo_picks,
            )
            kernel = functools.partial(sweep_update_kernel, turn=turn, last=last, **mine)
            if last:
                series = run(
                    kernel,
                    inputs,
                    [piece] * devs,
                    [(some, f32), turned, (some, f32)],
                    in_smem=(0, 1),
                )
            else:
                current, pack0, pack1 = run(
                    kernel,
                    inputs + (send,),
                    [(some, f32), turned, turned],
                    [(some, f32), turned],
                    in_smem=(0, 1),
                )
        restored += [time_swap(series[turn], turn) for turn in range(devs)]
    (out,) = run(
        functools.partial(assemble_kernel, total_steps=total_steps, groups=groups),
        tuple(restored),
        [(cube, f32)],
        [pltpu.SemaphoreType.DMA((len(restored),))],
        out_hbm=(0,),
    )
    return out.reshape(samples, steps_dev, dofs, elems)


def solution(mesh):
    placed = (
        P("groups", "tm", None, "space"),
        P("groups", "tm", None, "space"),
        P("space"),
        P(None, "space"),
        P(),
        P(),
        P("groups"),
        P(),
        P(),
        P(None, "space"),
        P(None, "space"),
    )
    return jax.shard_map(
        per_device,
        mesh=mesh,
        in_specs=placed,
        out_specs=P("groups", "tm", None, "space"),
        check_vma=False,
    )
```

```python
import functools
import math

import jax
import jax.numpy as jnp
from jax import lax
from jax.experimental import pallas as pl
from jax.experimental.pallas import tpu as pltpu
from jax.sharding import PartitionSpec as P

MAXS = 3
alpha_circ = 0.05
time_step = 0.1
relax_rho = 2.3
highest = lax.Precision.HIGHEST
f32, bf16, i32 = jnp.float32, jnp.bfloat16, jnp.int32
FACES = 6
GROUPS = 1


def dot(a, b):
    return jnp.dot(a, b, preferred_element_type=f32)


def split(x):
    hi = x.astype(bf16)
    return hi, (x - hi.astype(f32)).astype(bf16)


def exact_select(x, onehot, across=0):
    a, b = split(x)
    c = (x - a.astype(f32) - b.astype(f32)).astype(bf16)
    times = lambda v: lax.dot_general(
        v, onehot, (((1,), (across,)), ((), ())), preferred_element_type=f32
    )
    return times(a) + (times(b) + times(c))


def times_block(stacked, x):
    rows = stacked.shape[0] // 2
    hi, lo = split(x)
    both = dot(stacked, hi)
    return both[:rows] + (both[rows:] + dot(stacked[:rows], lo))


def rows_iota(shape):
    return lax.broadcasted_iota(i32, shape, 0)


def halo_onehot(nbr_row, base, halo):
    elems = nbr_row.shape[1]
    entry = nbr_row - base
    here = (entry >= 0) & (entry < halo)
    entry = jnp.where(here, entry, -2 * halo)
    row = rows_iota((2 * halo, elems))
    left = (row == entry).astype(f32).astype(bf16)
    right = (row == entry + halo).astype(f32).astype(bf16)
    return jnp.concatenate([left, right], axis=1)


def space_even():
    return lax.rem(lax.axis_index("space") + lax.axis_index("tm"), 2) == 0


def sides(even, elems, halo):
    below, above = elems, elems + halo
    return (
        (jnp.where(even, 5, 4), jnp.where(even, above, below)),
        (jnp.where(even, 4, 5), jnp.where(even, below, above)),
    )


def group_size(count):
    return next(size for size in (4, 3, 2, 1) if count % size == 0)


def pack_group(ref, left, right, send, first, outs):
    dofs = ref.shape[1]
    width = send.shape[1] // 2
    sides_by_side = [jnp.concatenate([ref[i] for i in side], axis=0) for side in (left, right)]
    hi, lo = split(jnp.concatenate(sides_by_side, axis=1))
    got = dot(hi, send) + dot(lo, send)
    rows = slice(first * dofs, (first + len(left)) * dofs)
    for which, out in enumerate(outs):
        out[rows, :] = got[:, which * width : (which + 1) * width]


def pack_fields(ref, fields, send, outs):
    half = len(fields) // 2
    size = group_size(half)
    for j in range(0, half, size):
        pack_group(
            ref, fields[j : j + size], fields[half + j : half + j + size], send, j, outs
        )


def prepare_kernel(
    iterate_in,
    halo_send_in,
    shift_in,
    gen_in,
    mean_in,
    modes_in,
    nbr_in,
    grads_in,
    face_mats_in,
    counts_in,
    pack0,
    pack1,
    send_out,
    conduct_out,
    low,
    high,
    nbr,
    grads,
    face_mats,
    counts,
    halo_send,
    shift,
    gen,
    mean,
    modes,
    small_done,
    field_done,
    later_done,
):
    iterate = Halves(low, high)
    samples, dofs, elems = iterate.shape
    halo = halo_send.shape[1]
    half = samples // 2
    size = group_size(half)
    small = [
        pltpu.make_async_copy(source, target, small_done.at[i])
        for i, (source, target) in enumerate(
            (
                (halo_send_in, halo_send),
                (shift_in, shift),
                (gen_in, gen),
                (mean_in, mean),
                (modes_in, modes),
            )
        )
    ]
    large = []
    for j in range(0, half, size):
        for at, side in ((j, low), (half + j, high)):
            large.append(
                pltpu.make_async_copy(
                    iterate_in.at[pl.ds(at, size)],
                    side.at[pl.ds(j, size)],
                    field_done.at[len(large)],
                )
            )
    later = [
        pltpu.make_async_copy(source, target, later_done.at[i])
        for i, (source, target) in enumerate(
            ((nbr_in, nbr), (grads_in, grads), (face_mats_in, face_mats), (counts_in, counts))
        )
    ]
    for copy in small + large + later:
        copy.start()
    for copy in small:
        copy.wait()
    even = space_even()
    down = jnp.concatenate([halo_send[0:1, :]] * 2, axis=1)
    up = jnp.concatenate([halo_send[1:2, :]] * 2, axis=1)
    lane = lax.broadcasted_iota(i32, (1, 2 * halo), 1)
    row = rows_iota((2 * elems, 2 * halo))
    for which in range(2):
        ids = jnp.where(even == (which == 0), up, down)
        ids = jnp.where(lane < halo, ids, ids + elems)
        send_out[:, which * 2 * halo : (which + 1) * 2 * halo] = (
            (row == ids).astype(f32).astype(bf16)
        )
    position = rows_iota((samples, gen.shape[1]))
    residue = lax.rem(position * gen[...], samples)
    shifted = residue.astype(f32) / samples + shift[...]
    fraction = shifted - jnp.floor(shifted)
    points = 0.5 - jnp.abs(2.0 * fraction - 1.0)
    conduct = mean[...] * (
        1.0 + jnp.dot(points, modes[...], precision=highest, preferred_element_type=f32)
    )
    conduct_out[...] = conduct
    send = send_out[...]
    got = exact_select(jnp.concatenate([conduct[:half], conduct[half:]], axis=1), send)
    pack0[half * dofs :, :] = got[:, : 2 * halo]
    pack1[half * dofs :, :] = got[:, 2 * halo :]
    for at, j in enumerate(range(0, half, size)):
        large[2 * at].wait()
        large[2 * at + 1].wait()
        left = list(range(j, j + size))
        pack_group(iterate, left, [half + i for i in left], send, j, (pack0, pack1))
    for copy in later:
        copy.wait()


def local_part(fields, slots, coef_row, picks, blocks, out, high, low):
    dofs, elems = fields.shape[1], fields.shape[2]
    size = group_size(len(slots))
    for first in range(0, len(slots), size):
        group = range(first, first + size)
        values = [fields[slots[t]] for t in group]
        hi, lo = split(jnp.concatenate(values, axis=0))
        for t, value in zip(group, values):
            a, b = split(value * coef_row(FACES, t))
            high[t, 0:dofs, :] = a
            low[t, 0:dofs, :] = b
        for f in range(FACES):
            pick = picks[:, f * elems : (f + 1) * elems]
            got = dot(hi, pick) + dot(lo, pick)
            at = (f + 1) * dofs
            for i, t in enumerate(group):
                a, b = split(got[i * dofs : (i + 1) * dofs] * coef_row(f, t))
                high[t, at : at + dofs, :] = a
                low[t, at : at + dofs, :] = b
        stacked = blocks[...]
        for t in group:
            both = dot(stacked, high[t])
            out[slots[t]] = both[:dofs] + (both[dofs:] + dot(stacked[:dofs], low[t]))


def first_local_kernel(
    low_fields,
    high_fields,
    conduct_ref,
    face_nbr,
    grads,
    face_mats,
    counts_in,
    out,
    coefs,
    picks,
    blocks,
    face_blocks,
    halo_picks,
    general,
    counts,
    facing,
    high,
    low,
    wide,
):
    for k in range(counts.shape[0]):
        counts[k] = counts_in[0, k]
    iterate = Halves(low_fields, high_fields)
    samples, dofs, elems = iterate.shape
    halo = halo_picks.shape[0] // 4
    even = space_even()
    row = rows_iota((elems, elems))
    for f in range(FACES):
        picks[:, f * elems : (f + 1) * elems] = (
            (row == face_nbr[f : f + 1, :]).astype(f32).astype(bf16)
        )
    conduct = conduct_ref[...]
    diag = conduct
    for f in range(FACES):
        nbr = face_nbr[f : f + 1, :]
        across = exact_select(conduct, picks[:, f * elems : (f + 1) * elems])
        inside = (nbr >= 0) & (nbr < elems)
        coupling = jnp.where(inside, 0.5 * (conduct + across), 0.0)
        coefs[f] = coupling
        diag = diag + jnp.where(nbr < 0, conduct, coupling)
    coefs[FACES] = diag
    coefs[FACES + 1] = conduct
    volume = (rows_iota((dofs, dofs)) == lax.broadcasted_iota(i32, (dofs, dofs), 1)).astype(f32)
    for d in range(grads.shape[0]):
        volume = volume + lax.dot_general(
            grads[d], grads[d], (((0,), (0,)), ((), ())), precision=highest,
            preferred_element_type=f32,
        )
    wide[...] = jnp.zeros(wide.shape, f32)
    wide[0:dofs, 0:dofs] = volume
    for f in range(FACES):
        block = face_mats[f // 2]
        at = (f + 1) * dofs
        wide[at : at + dofs, 0:dofs] = block if f % 2 == 0 else block.T
    turned = wide[...].T[:dofs, :]
    hi, lo = split(turned)
    blocks[0:dofs, :] = hi
    blocks[dofs:, :] = lo
    for f in range(FACES):
        block = face_mats[f // 2]
        hi, lo = split(block.T if f % 2 == 0 else block)
        face_blocks[f, 0:dofs, :] = hi
        face_blocks[f, dofs:, :] = lo
    for which, (face, base) in enumerate(sides(even, elems, halo)):
        nbr = jnp.where(face == 4, face_nbr[4:5, :], face_nbr[5:6, :])
        pick = halo_onehot(nbr, base, halo)
        halo_picks[which * 2 * halo : (which + 1) * 2 * halo, :] = pick
        facing[which] = exact_select(side_by_side(conduct), pick, 1)
    crossing = jnp.max(jnp.where(face_nbr[0:4, :] >= elems, 1, 0))
    crossing = crossing + jnp.max(jnp.where(face_nbr[4:5, :] >= elems + halo, 1, 0))
    fifth = face_nbr[5:6, :]
    crossing = crossing + jnp.max(
        jnp.where((fifth >= elems) & (fifth < elems + halo), 1, 0)
    )
    general[0] = crossing
    local_part(
        iterate,
        list(range(samples)),
        lambda f, t: coefs[f, t : t + 1, :],
        picks,
        blocks,
        out,
        high,
        low,
    )


def side_by_side(x):
    half = x.shape[0] // 2
    return jnp.concatenate([x[:half], x[half:]], axis=1)


def stacked_halves(x):
    width = x.shape[1] // 2
    return jnp.concatenate([x[:, :width], x[:, width:]], axis=0)


def usual_halo(arrived, scales, blocks, picks):
    dofs = blocks[0].shape[1]
    columns = []
    for which in range(2):
        value = arrived[which]
        width = value.shape[1]
        pairs = scales[which].shape[0]
        scaled = [
            value[j * dofs : (j + 1) * dofs, :] * scales[which][j : j + 1, :]
            for j in range(pairs)
        ]
        got = times_block(blocks[which], jnp.concatenate(scaled, axis=1))
        columns.append(
            jnp.concatenate([got[:, j * width : (j + 1) * width] for j in range(pairs)], axis=0)
        )
    hi, lo = split(jnp.concatenate(columns, axis=1))
    return dot(hi, picks) + dot(lo, picks)


class Halves:
    def __init__(self, low, high):
        self.low, self.high = low, high
        self.shape = (2 * low.shape[0],) + tuple(low.shape[1:])

    def __getitem__(self, at):
        half = self.low.shape[0]
        return self.low[at] if at < half else self.high[at - half]


def other_halo(arrived, block, pick):
    dofs = block.shape[1]
    hi, lo = split(times_block(block, arrived))
    got = dot(hi, pick) + dot(lo, pick)
    return got


def other_sides(general, even, face_nbr, halo, body):
    elems = face_nbr.shape[1]

    @pl.when(general[0] > 0)
    def _():
        for which, (usual, base) in enumerate(sides(even, elems, halo)):

            def step(face, carry, which=which, usual=usual, base=base):
                @pl.when(face != usual)
                def _():
                    body(which, face, halo_onehot(face_nbr[pl.ds(face, 1), :], base, halo))

                return carry

            lax.fori_loop(0, FACES, step, 0)


def pair_place(t, half, dofs, elems):
    row, col = t % half * dofs, t // half * elems
    return slice(row, row + dofs), slice(col, col + elems)


def add_others(arrived, even, general, face_nbr, face_blocks, halo, half, slots, coef_row, factor, total):
    elems = face_nbr.shape[1]
    dofs = total.shape[1]

    def body(which, face, pick):
        block = face_blocks[face]
        for j in range(half):
            got = other_halo(arrived[which][j * dofs : (j + 1) * dofs, :], block, pick)
            for t in (j, half + j):
                if t < len(slots):
                    cols = slice(t // half * elems, (t // half + 1) * elems)
                    field = slots[t]
                    total[field] = total[field] + factor * coef_row(face, t) * got[:, cols]

    other_sides(general, even, face_nbr, halo, body)


def residual_kernel(
    forcing,
    low_fields,
    high_fields,
    earlier_low,
    earlier_high,
    local,
    arrived0,
    arrived1,
    coefs_in,
    face_nbr,
    blocks,
    face_blocks,
    halo_picks,
    facing,
    general,
    *rest,
    total_steps,
    groups,
):
    outs = rest[: groups * total_steps]
    coefs, total, extra = rest[groups * total_steps :]
    iterate = Halves(low_fields, high_fields)
    samples, dofs, elems = forcing.shape
    halo = halo_picks.shape[0] // 4
    half = samples // 2
    even = space_even()
    usual = sides(even, elems, halo)
    arrived = (arrived0, arrived1)
    coefs[...] = coefs_in[...]
    conduct = coefs_in[FACES + 1]
    scales = [0.5 * (facing[w] + arrived[w][half * dofs :, :]) for w in range(2)]
    couplings = [
        stacked_halves(
            exact_select(scales[w], halo_picks[w * 2 * halo : (w + 1) * 2 * halo, :])
        )
        for w in range(2)
    ]
    extra[...] = couplings[0] + couplings[1]
    for w in range(2):
        coefs[usual[w][0]] = coefs[usual[w][0]] + couplings[w]

    def add_coupling(which, face, pick):
        got = exact_select(arrived[which][half * dofs :, :], pick)
        nbr = face_nbr[pl.ds(face, 1), :]
        base = usual[which][1]
        here = (nbr >= base) & (nbr < base + halo)
        coupling = jnp.where(here, 0.5 * (conduct + stacked_halves(got)), 0.0)
        coefs[face] = coefs[face] + coupling
        extra[...] = extra[...] + coupling

    other_sides(general, even, face_nbr, halo, add_coupling)
    coefs[FACES] = coefs[FACES] + extra[...]
    volume = blocks[:, 0 : 2 * dofs][:, :dofs]
    brought = usual_halo(
        arrived, scales, [face_blocks[usual[w][0]] for w in range(2)], halo_picks[...]
    )
    for j in range(samples):
        value = iterate[j]
        total[j] = value + time_step * (
            local[j]
            + brought[pair_place(j, half, dofs, elems)]
            + times_block(volume, value * extra[j : j + 1, :])
        )
    add_others(
        arrived,
        even,
        general,
        face_nbr,
        face_blocks,
        halo,
        half,
        list(range(samples)),
        lambda f, t: coefs[f, t : t + 1, :],
        time_step,
        total,
    )
    step = lax.axis_index("tm")
    weight = jnp.float32(0.0)
    for n in range(total_steps):
        weight = jnp.where(step == n, jnp.float32(alpha_circ ** (n / total_steps)), weight)
    gate_high = jnp.where(step > 0, weight, 0.0)
    gate_low = jnp.where(step % 2 == 1, weight, 0.0) if two_chips(total_steps) else gate_high
    size = samples // (groups * total_steps)
    for which, out in enumerate(outs):
        at, turn = divmod(which, total_steps)
        first = (partner(step, turn, total_steps) * groups + at) * size
        for i in range(size):
            j = first + i
            inner = forcing[j] - total[j]
            before = lax.rem(j, half)
            late = j >= half
            earlier = jnp.where(late, earlier_high[before], earlier_low[before])
            out[i] = weight * inner + jnp.where(late, gate_high, gate_low) * earlier


def two_chips(devs):
    return devs == 4


def partner(rank, turn, count):
    if count & (count - 1) == 0:
        return rank ^ turn
    return lax.rem(turn + count - rank, count)


def real_fields(total_steps):
    order = [(0, False)]
    if total_steps % 2 == 0:
        order.append((total_steps // 2, False))
    for k in range(1, (total_steps + 1) // 2):
        order += [(k, False), (k, True)]
    return order


def cos_sin(k, n, total_steps):
    turn = 2.0 * math.pi * ((k * n) % total_steps) / total_steps
    c, s = math.cos(turn), math.sin(turn)
    snap = lambda v: float(round(v)) if abs(v - round(v)) < 1e-12 else v
    return snap(c), snap(s)


def weighted(terms):
    total = None
    for constant, value in terms:
        if constant == 0.0:
            continue
        if total is None:
            total = value if constant == 1.0 else constant * value
        elif constant == 1.0:
            total = total + value
        elif constant == -1.0:
            total = total - value
        else:
            total = total + constant * value
    return total


def shift_of(k, total_steps):
    magnitude = alpha_circ ** (1.0 / total_steps)
    c, s = cos_sin(k, 1, total_steps)
    return 1.0 - magnitude * c, magnitude * s


def theta_rows(k, total_steps, diag):
    shift_real, shift_imag = shift_of(k, total_steps)
    denom = shift_real + (time_step * relax_rho) * diag
    if shift_imag == 0.0:
        return 1.0 / denom, None
    modulus = denom * denom + shift_imag * shift_imag
    return denom / modulus, -shift_imag / modulus


def frequencies(total_steps):
    order = real_fields(total_steps)
    return [
        (k, at, order.index((k, True)) if (k, True) in order else None)
        for at, (k, imag) in enumerate(order)
        if not imag
    ]


def kept_slots(counts, samples, total_steps):
    skip = jnp.int32(0)
    for k, re, _ in frequencies(total_steps):
        skip = jnp.where(counts[k] == 1, re, skip)
    kept = total_steps - 1
    slots = []
    for t in range(samples * kept):
        s, i = divmod(t, kept)
        slots.append(s * total_steps + jnp.where(skip <= i, i + 1, i))
    return slots


def even_slots(slots):
    return slots + slots[: len(slots) % 2]


def my_first(samples, at, groups):
    return (lax.axis_index("tm") * groups + at) * samples


def sample_row(coefs, total_steps, first):
    kept = total_steps - 1
    return lambda f, t: coefs[f, pl.ds(first + t // kept, 1), :]


def spectrum_kernel(
    counts, coefs, send_ref, own, near, *rest, total_steps, at, groups
):
    arrived, (spectrum, first_w, pack0, pack1, pieces) = (
        rest[:total_steps],
        rest[total_steps:],
    )
    samples = arrived[0].shape[0]
    first = my_first(samples, at, groups)
    rank = lax.axis_index("tm")
    for turn, piece in enumerate(arrived):
        pieces[partner(rank, turn, total_steps)] = piece[...]
    if two_chips(total_steps):
        here = at * samples
        there = groups * samples + here
        gate = jnp.where(rank < 2, jnp.float32(alpha_circ ** (2 / total_steps)), 0.0)
        for s in range(samples):
            before = jnp.where(rank == 0, near[here + s], own[there + s])
            pieces[2, s] = pieces[2, s] + gate * before
    for s in range(samples):
        diag = coefs[FACES, pl.ds(first + s, 1), :]
        base = s * total_steps
        for k, re, im in frequencies(total_steps):
            tables = [cos_sin(k, n, total_steps) for n in range(total_steps)]
            real = weighted([(tables[n][0], pieces[n, s]) for n in range(total_steps)])
            rate_real, rate_imag = theta_rows(k, total_steps, diag)
            spectrum[base + re] = real
            if im is None:
                first_w[base + re] = rate_real * real
            else:
                imag = weighted([(-tables[n][1], pieces[n, s]) for n in range(total_steps)])
                spectrum[base + im] = imag
                first_w[base + re] = rate_real * real - rate_imag * imag
                first_w[base + im] = rate_real * imag + rate_imag * real
    slots = kept_slots(counts, samples, total_steps)
    pack_fields(first_w, even_slots(slots), send_ref[...], (pack0, pack1))


def sweep_local_kernel(
    counts,
    fields,
    spectrum,
    coefs,
    picks,
    blocks,
    halo_picks,
    *rest,
    total_steps,
    at,
    groups,
    first_turn,
):
    if first_turn:
        out, thetas, scales, total, high, low = rest
    else:
        out, total, high, low = rest
    elems = fields.shape[2]
    samples = fields.shape[0] // total_steps
    first = my_first(samples, at, groups)
    slots = kept_slots(counts, samples, total_steps)
    row = sample_row(coefs, total_steps, first)
    if first_turn:
        halo = halo_picks.shape[0] // 4
        half = scales.shape[1]
        usual = sides(space_even(), elems, halo)
        count = len(slots)
        for w in range(2):
            lines = [
                row(usual[w][0], t if t < count else 0) for t in range(2 * half)
            ]
            sides_of = [jnp.concatenate(lines[:half], 0), jnp.concatenate(lines[half:], 0)]
            scales[w] = time_step * exact_select(
                jnp.concatenate(sides_of, axis=1),
                halo_picks[w * 2 * halo : (w + 1) * 2 * halo, :],
                1,
            )
        diag = jnp.concatenate(
            [coefs[FACES, pl.ds(first + s, 1), :] for s in range(samples)], axis=0
        )
        for i, (k, _, im) in enumerate(frequencies(total_steps)):
            rate_real, rate_imag = theta_rows(k, total_steps, diag)
            thetas[2 * i] = rate_real
            if im is not None:
                thetas[2 * i + 1] = rate_imag
    local_part(fields, slots, row, picks, blocks, total, high, low)
    for s in range(samples):
        base = s * total_steps
        for k, re, im in frequencies(total_steps):
            shift_real, shift_imag = shift_of(k, total_steps)
            value = fields[base + re]
            kept = spectrum[base + re] - (shift_real * value + time_step * total[base + re])
            if im is not None:
                other = fields[base + im]
                kept = kept + shift_imag * other
                out[base + im] = spectrum[base + im] - (
                    shift_real * other + shift_imag * value + time_step * total[base + im]
                )
            out[base + re] = kept


def sweep_update_kernel(
    counts,
    general,
    current,
    inner,
    arrived0,
    arrived1,
    coefs,
    face_nbr,
    face_blocks,
    halo_picks,
    thetas,
    scales,
    *rest,
    turn,
    total_steps,
    last,
    at,
    groups,
):
    even = space_even()
    if last:
        outs, (total, solved) = rest[:total_steps], rest[total_steps:]
    else:
        send_ref, solved, pack0, pack1, total = rest
    fields, dofs, elems = current.shape
    samples = fields // total_steps
    first = my_first(samples, at, groups)
    slots = kept_slots(counts, samples, total_steps)
    arrived = (arrived0, arrived1)
    halo = halo_picks.shape[0] // 4
    half = scales.shape[1]
    usual = sides(even, elems, halo)
    brought = usual_halo(
        arrived,
        [scales[w] for w in range(2)],
        [face_blocks[usual[w][0]] for w in range(2)],
        halo_picks[...],
    )
    for t, field in enumerate(slots):
        total[field] = inner[field] - brought[pair_place(t, half, dofs, elems)]
    add_others(
        arrived,
        even,
        general,
        face_nbr,
        face_blocks,
        halo,
        half,
        slots,
        sample_row(coefs, total_steps, first),
        -time_step,
        total,
    )
    for s in range(samples):
        base = s * total_steps
        for i, (k, re, im) in enumerate(frequencies(total_steps)):
            active = counts[k] > turn + 1
            rate_real = thetas[2 * i, s : s + 1, :]
            value, rest_real = current[base + re], total[base + re]
            change = rate_real * rest_real
            if im is not None:
                rate_imag = thetas[2 * i + 1, s : s + 1, :]
                other, rest_imag = current[base + im], total[base + im]
                change = change - rate_imag * rest_imag
                solved[base + im] = jnp.where(
                    active, other + (rate_real * rest_imag + rate_imag * rest_real), other
                )
            solved[base + re] = jnp.where(active, value + change, value)
    if not last:
        pack_fields(solved, even_slots(slots), send_ref[...], (pack0, pack1))
        return
    rank = lax.axis_index("tm")
    for s in range(samples):
        base = s * total_steps
        for n in range(total_steps):
            scale = alpha_circ ** (-n / total_steps) / total_steps
            terms = []
            for k, re, im in frequencies(total_steps):
                c, sn = cos_sin(k, n, total_steps)
                if im is None:
                    terms.append((c, solved[base + re]))
                else:
                    terms += [(2.0 * c, solved[base + re]), (-2.0 * sn, solved[base + im])]
            total[n * samples + s] = scale * weighted(terms)
    for turn_to, out in enumerate(outs):
        step = partner(rank, turn_to, total_steps)
        for s in range(samples):
            out[s] = total[step * samples + s]


def assemble_kernel(*rest, total_steps, groups):
    pieces, (out, done) = rest[:-2], rest[-2:]
    size = pieces[0].shape[0]
    rank = lax.axis_index("tm")
    copies = []
    for which, piece in enumerate(pieces):
        at, turn = divmod(which, total_steps)
        first = (partner(rank, turn, total_steps) * groups + at) * size
        copies.append(
            pltpu.make_async_copy(piece, out.at[pl.ds(first, size)], done.at[which])
        )
    for copy in copies:
        copy.start()
    for copy in copies:
        copy.wait()


vmem = pl.BlockSpec(memory_space=pltpu.VMEM)
smem = pl.BlockSpec(memory_space=pltpu.SMEM)


def run(
    kernel, inputs, outs, scratch=(), in_smem=(), out_smem=(), in_hbm=(), out_hbm=(), flops=10**9
):
    def spec(i, small, outside=()):
        if i in outside:
            return pl.BlockSpec(memory_space=pltpu.HBM)
        return smem if i in small else vmem

    inputs = [
        pltpu.with_memory_space_constraint(value, pltpu.HBM) if i in in_hbm else value
        for i, value in enumerate(inputs)
    ]
    return pl.pallas_call(
        kernel,
        out_shape=[jax.ShapeDtypeStruct(*o) for o in outs],
        in_specs=[spec(i, in_smem, in_hbm) for i in range(len(inputs))],
        out_specs=[spec(i, out_smem, out_hbm) for i in range(len(outs))],
        scratch_shapes=[pltpu.VMEM(*s) if isinstance(s, tuple) else s for s in scratch],
        compiler_params=pltpu.CompilerParams(vmem_limit_bytes=40 << 20),
        cost_estimate=pl.CostEstimate(flops=flops, bytes_accessed=1 << 22, transcendentals=0),
    )(*inputs)


def neighbour_swap(value, start):
    axes = ("groups", "tm", "space")
    parts, devs, count = (lax.axis_size(axis) for axis in axes)
    pairs = []
    for part in range(parts):
        for tm in range(devs):
            for space in range(count):
                step = 1 if (space + tm + start) % 2 == 0 else -1
                to_part, to_space = part, space + step
                if not 0 <= to_space < count:
                    to_part, to_space = part ^ 1, space
                if to_part < parts:
                    pairs.append(
                        ((part * devs + tm) * count + space, (to_part * devs + tm) * count + to_space)
                    )
    return lax.ppermute(value, axes, pairs)


def time_swap(value, turn):
    count = lax.axis_size("tm")
    pairs = [(i, int(partner(i, turn, count))) for i in range(count)]
    return value if turn == 0 else lax.ppermute(value, "tm", pairs)


def per_device(
    forcing,
    iterate,
    kappa_mean,
    kappa_modes,
    grad_mats,
    face_mats,
    lattice_shift,
    gen_vector,
    sweep_counts,
    face_nbr,
    halo_send,
):
    samples, steps_dev, dofs, elems = forcing.shape
    halo = halo_send.shape[1]
    devs = lax.axis_size("tm")
    total_steps = steps_dev * devs
    part = samples // devs
    half = samples // 2
    cube = (samples, dofs, elems)
    forcing = forcing.reshape(cube)
    iterate = iterate.reshape(cube)
    onward = [(i, (i + 1) % devs) for i in range(devs)]
    rows = half * dofs
    copies = 2 * (half // group_size(half))
    (
        pack0, pack1, send, conduct, low, high, face_nbr, grad_mats, face_mats, counts_line
    ) = run(
        prepare_kernel,
        (
            iterate,
            halo_send,
            lattice_shift.reshape(1, -1),
            gen_vector.reshape(1, -1),
            kappa_mean.reshape(1, -1),
            kappa_modes,
            face_nbr,
            grad_mats,
            face_mats,
            sweep_counts.reshape(1, -1),
        ),
        [
            ((rows + half, 2 * halo), f32),
            ((rows + half, 2 * halo), f32),
            ((2 * elems, 4 * halo), bf16),
            ((samples, elems), f32),
            ((half, dofs, elems), f32),
            ((half, dofs, elems), f32),
            (face_nbr.shape, i32),
            (grad_mats.shape, f32),
            (face_mats.shape, f32),
            ((1, sweep_counts.shape[0]), i32),
        ],
        [
            (halo_send.shape, i32),
            ((1, lattice_shift.shape[0]), f32),
            ((1, gen_vector.shape[0]), i32),
            ((1, elems), f32),
            (kappa_modes.shape, f32),
            pltpu.SemaphoreType.DMA((5,)),
            pltpu.SemaphoreType.DMA((copies,)),
            pltpu.SemaphoreType.DMA((4,)),
        ],
        in_hbm=range(10),
    )
    arrived0 = neighbour_swap(pack0, 0)
    arrived1 = neighbour_swap(pack1, 1)
    earlier_high = lax.ppermute(high, "tm", onward)
    if two_chips(devs):
        earlier_low = time_swap(low, 1)
    else:
        earlier_low = lax.ppermute(low, "tm", onward)
    blocks_wide = (FACES + 1) * dofs
    splits = lambda count: [((count, blocks_wide, elems), bf16)] * 2
    (
        local, coefs, picks, blocks, face_blocks, halo_picks, general, counts, facing
    ) = run(
        first_local_kernel,
        (low, high, conduct, face_nbr, grad_mats, face_mats, counts_line),
        [
            (cube, f32),
            ((FACES + 2, samples, elems), f32),
            ((elems, FACES * elems), bf16),
            ((2 * dofs, blocks_wide), bf16),
            ((FACES, 2 * dofs, dofs), bf16),
            ((4 * halo, 2 * elems), bf16),
            ((1,), i32),
            (sweep_counts.shape, i32),
            ((2, half, 2 * halo), f32),
        ],
        splits(samples) + [((blocks_wide, 2 * dofs), f32)],
        out_smem=(6, 7),
        flops=4 * 10**9,
    )
    groups = GROUPS if part % GROUPS == 0 else 1
    share = part // groups
    piece = ((share, dofs, elems), f32)
    *scaled, coefs = run(
        functools.partial(residual_kernel, total_steps=total_steps, groups=groups),
        (
            forcing,
            low,
            high,
            earlier_low,
            earlier_high,
            local,
            arrived0,
            arrived1,
            coefs,
            face_nbr,
            blocks,
            face_blocks,
            halo_picks,
            facing,
            general,
        ),
        [piece] * (groups * devs) + [((FACES + 2, samples, elems), f32)],
        [(cube, f32), ((samples, elems), f32)],
        in_smem=(14,),
    )
    fields = share * total_steps
    swept = share * (total_steps - 1)
    pairs = (swept + 1) // 2
    some = ((fields, dofs, elems), f32)
    packed = ((pairs * dofs, 2 * halo), f32)
    restored = []
    for at in range(groups):
        mine = dict(total_steps=total_steps, at=at, groups=groups)
        pieces = [time_swap(scaled[at * devs + turn], turn) for turn in range(devs)]
        spectrum, current, pack0, pack1 = run(
            functools.partial(spectrum_kernel, **mine),
            (counts, coefs, send, low, earlier_low, *pieces),
            [some, some, packed, packed],
            [((total_steps, share, dofs, elems), f32)],
            in_smem=(0,),
        )
        for turn in range(MAXS - 1):
            arrived0 = neighbour_swap(pack0, 0)
            arrived1 = neighbour_swap(pack1, 1)
            inner, *tables = run(
                functools.partial(sweep_local_kernel, first_turn=turn == 0, **mine),
                (counts, current, spectrum, coefs, picks, blocks, halo_picks),
                [some]
                + [
                    ((2 * len(frequencies(total_steps)), share, elems), f32),
                    ((2, pairs, 2 * halo), f32),
                ]
                * (turn == 0),
                [some] + splits(swept),
                in_smem=(0,),
                flops=3 * 10**9 // groups,
            )
            if turn == 0:
                thetas, scales = tables
            last = turn == MAXS - 2
            inputs = (
                counts,
                general,
                current,
                inner,
                arrived0,
                arrived1,
                coefs,
                face_nbr,
                face_blocks,
                halo_picks,
                thetas,
                scales,
            )
            kernel = functools.partial(sweep_update_kernel, turn=turn, last=last, **mine)
            if last:
                series = run(
                    kernel, inputs, [piece] * devs, [some, some], in_smem=(0, 1)
                )
            else:
                current, pack0, pack1 = run(
                    kernel,
                    inputs + (send,),
                    [some, packed, packed],
                    [some],
                    in_smem=(0, 1),
                )
        restored += [time_swap(series[turn], turn) for turn in range(devs)]
    (out,) = run(
        functools.partial(assemble_kernel, total_steps=total_steps, groups=groups),
        tuple(restored),
        [(cube, f32)],
        [pltpu.SemaphoreType.DMA((len(restored),))],
        out_hbm=(0,),
    )
    return out.reshape(samples, steps_dev, dofs, elems)


def solution(mesh):
    placed = (
        P("groups", "tm", None, "space"),
        P("groups", "tm", None, "space"),
        P("space"),
        P(None, "space"),
        P(),
        P(),
        P("groups"),
        P(),
        P(),
        P(None, "space"),
        P(None, "space"),
    )
    return jax.shard_map(
        per_device,
        mesh=mesh,
        in_specs=placed,
        out_specs=P("groups", "tm", None, "space"),
        check_vma=False,
    )
```

```python
import functools
import math

import jax
import jax.numpy as jnp
from jax import lax
from jax.experimental import pallas as pl
from jax.experimental.pallas import tpu as pltpu
from jax.sharding import PartitionSpec as P

MAXS = 3
alpha_circ = 0.05
time_step = 0.1
relax_rho = 2.3
highest = lax.Precision.HIGHEST
f32, bf16, i32 = jnp.float32, jnp.bfloat16, jnp.int32
FACES = 6
GROUPS = 1


def dot(a, b):
    return jnp.dot(a, b, preferred_element_type=f32)


def split(x):
    hi = x.astype(bf16)
    return hi, (x - hi.astype(f32)).astype(bf16)


def exact_select(x, onehot, across=0):
    a, b = split(x)
    c = (x - a.astype(f32) - b.astype(f32)).astype(bf16)
    times = lambda v: lax.dot_general(
        v, onehot, (((1,), (across,)), ((), ())), preferred_element_type=f32
    )
    return times(a) + (times(b) + times(c))


def times_block(stacked, x):
    rows = stacked.shape[0] // 2
    hi, lo = split(x)
    both = dot(stacked, hi)
    return both[:rows] + (both[rows:] + dot(stacked[:rows], lo))


def rows_iota(shape):
    return lax.broadcasted_iota(i32, shape, 0)


def halo_onehot(nbr_row, base, halo):
    elems = nbr_row.shape[1]
    entry = nbr_row - base
    here = (entry >= 0) & (entry < halo)
    entry = jnp.where(here, entry, -2 * halo)
    row = rows_iota((2 * halo, elems))
    left = (row == entry).astype(f32).astype(bf16)
    right = (row == entry + halo).astype(f32).astype(bf16)
    return jnp.concatenate([left, right], axis=1)


def space_even():
    return lax.rem(lax.axis_index("space") + lax.axis_index("tm"), 2) == 0


def sides(even, elems, halo):
    below, above = elems, elems + halo
    return (
        (jnp.where(even, 5, 4), jnp.where(even, above, below)),
        (jnp.where(even, 4, 5), jnp.where(even, below, above)),
    )


def group_size(count):
    return next(size for size in (4, 3, 2, 1) if count % size == 0)


def pack_group(ref, left, right, send, first, outs):
    dofs = ref.shape[1]
    width = send.shape[1] // 2
    sides_by_side = [jnp.concatenate([ref[i] for i in side], axis=0) for side in (left, right)]
    hi, lo = split(jnp.concatenate(sides_by_side, axis=1))
    got = dot(hi, send) + dot(lo, send)
    rows = slice(first * dofs, (first + len(left)) * dofs)
    for which, out in enumerate(outs):
        out[rows, :] = got[:, which * width : (which + 1) * width]


def pack_fields(ref, fields, send, outs):
    half = len(fields) // 2
    size = group_size(half)
    for j in range(0, half, size):
        pack_group(
            ref, fields[j : j + size], fields[half + j : half + j + size], send, j, outs
        )


def prepare_kernel(
    iterate_in,
    halo_send_in,
    shift_in,
    gen_in,
    mean_in,
    modes_in,
    nbr_in,
    grads_in,
    face_mats_in,
    counts_in,
    pack0,
    pack1,
    send_out,
    conduct_out,
    low,
    high,
    nbr,
    grads,
    face_mats,
    counts,
    halo_send,
    shift,
    gen,
    mean,
    modes,
    small_done,
    field_done,
    later_done,
):
    iterate = Halves(low, high)
    samples, dofs, elems = iterate.shape
    halo = halo_send.shape[1]
    half = samples // 2
    size = group_size(half)
    small = [
        pltpu.make_async_copy(source, target, small_done.at[i])
        for i, (source, target) in enumerate(
            (
                (halo_send_in, halo_send),
                (shift_in, shift),
                (gen_in, gen),
                (mean_in, mean),
                (modes_in, modes),
            )
        )
    ]
    large = []
    for j in range(0, half, size):
        for at, side in ((j, low), (half + j, high)):
            large.append(
                pltpu.make_async_copy(
                    iterate_in.at[pl.ds(at, size)],
                    side.at[pl.ds(j, size)],
                    field_done.at[len(large)],
                )
            )
    later = [
        pltpu.make_async_copy(source, target, later_done.at[i])
        for i, (source, target) in enumerate(
            ((nbr_in, nbr), (grads_in, grads), (face_mats_in, face_mats), (counts_in, counts))
        )
    ]
    for copy in small + large + later:
        copy.start()
    for copy in small:
        copy.wait()
    even = space_even()
    down = jnp.concatenate([halo_send[0:1, :]] * 2, axis=1)
    up = jnp.concatenate([halo_send[1:2, :]] * 2, axis=1)
    lane = lax.broadcasted_iota(i32, (1, 2 * halo), 1)
    row = rows_iota((2 * elems, 2 * halo))
    for which in range(2):
        ids = jnp.where(even == (which == 0), up, down)
        ids = jnp.where(lane < halo, ids, ids + elems)
        send_out[:, which * 2 * halo : (which + 1) * 2 * halo] = (
            (row == ids).astype(f32).astype(bf16)
        )
    position = rows_iota((samples, gen.shape[1]))
    residue = lax.rem(position * gen[...], samples)
    shifted = residue.astype(f32) / samples + shift[...]
    fraction = shifted - jnp.floor(shifted)
    points = 0.5 - jnp.abs(2.0 * fraction - 1.0)
    conduct = mean[...] * (
        1.0 + jnp.dot(points, modes[...], precision=highest, preferred_element_type=f32)
    )
    conduct_out[...] = conduct
    send = send_out[...]
    got = exact_select(jnp.concatenate([conduct[:half], conduct[half:]], axis=1), send)
    pack0[half * dofs :, :] = got[:, : 2 * halo]
    pack1[half * dofs :, :] = got[:, 2 * halo :]
    for at, j in enumerate(range(0, half, size)):
        large[2 * at].wait()
        large[2 * at + 1].wait()
        left = list(range(j, j + size))
        pack_group(iterate, left, [half + i for i in left], send, j, (pack0, pack1))
    for copy in later:
        copy.wait()


def local_part(fields, slots, coef_row, picks, blocks, out, high, low):
    dofs, elems = fields.shape[1], fields.shape[2]
    size = group_size(len(slots))
    for first in range(0, len(slots), size):
        group = range(first, first + size)
        values = [fields[slots[t]] for t in group]
        hi, lo = split(jnp.concatenate(values, axis=0))
        for t, value in zip(group, values):
            a, b = split(value * coef_row(FACES, t))
            high[t, 0:dofs, :] = a
            low[t, 0:dofs, :] = b
        for f in range(FACES):
            pick = picks[:, f * elems : (f + 1) * elems]
            got = dot(hi, pick) + dot(lo, pick)
            at = (f + 1) * dofs
            for i, t in enumerate(group):
                a, b = split(got[i * dofs : (i + 1) * dofs] * coef_row(f, t))
                high[t, at : at + dofs, :] = a
                low[t, at : at + dofs, :] = b
        stacked = blocks[...]
        for t in group:
            both = dot(stacked, high[t])
            out[slots[t]] = both[:dofs] + (both[dofs:] + dot(stacked[:dofs], low[t]))


def first_local_kernel(
    low_fields,
    high_fields,
    conduct_ref,
    face_nbr,
    grads,
    face_mats,
    counts_in,
    out,
    coefs,
    picks,
    blocks,
    face_blocks,
    halo_picks,
    flags,
    facing,
    high,
    low,
    wide,
):
    iterate = Halves(low_fields, high_fields)
    samples, dofs, elems = iterate.shape
    halo = halo_picks.shape[0] // 4
    even = space_even()
    row = rows_iota((elems, elems))
    for f in range(FACES):
        picks[:, f * elems : (f + 1) * elems] = (
            (row == face_nbr[f : f + 1, :]).astype(f32).astype(bf16)
        )
    conduct = conduct_ref[...]
    diag = conduct
    for f in range(FACES):
        nbr = face_nbr[f : f + 1, :]
        across = exact_select(conduct, picks[:, f * elems : (f + 1) * elems])
        inside = (nbr >= 0) & (nbr < elems)
        coupling = jnp.where(inside, 0.5 * (conduct + across), 0.0)
        coefs[f] = coupling
        diag = diag + jnp.where(nbr < 0, conduct, coupling)
    coefs[FACES] = diag
    coefs[FACES + 1] = conduct
    volume = (rows_iota((dofs, dofs)) == lax.broadcasted_iota(i32, (dofs, dofs), 1)).astype(f32)
    for d in range(grads.shape[0]):
        volume = volume + lax.dot_general(
            grads[d], grads[d], (((0,), (0,)), ((), ())), precision=highest,
            preferred_element_type=f32,
        )
    wide[...] = jnp.zeros(wide.shape, f32)
    wide[0:dofs, 0:dofs] = volume
    for f in range(FACES):
        block = face_mats[f // 2]
        at = (f + 1) * dofs
        wide[at : at + dofs, 0:dofs] = block if f % 2 == 0 else block.T
    turned = wide[...].T[:dofs, :]
    hi, lo = split(turned)
    blocks[0:dofs, :] = hi
    blocks[dofs:, :] = lo
    for f in range(FACES):
        block = face_mats[f // 2]
        hi, lo = split(block.T if f % 2 == 0 else block)
        face_blocks[f, 0:dofs, :] = hi
        face_blocks[f, dofs:, :] = lo
    for which, (face, base) in enumerate(sides(even, elems, halo)):
        nbr = jnp.where(face == 4, face_nbr[4:5, :], face_nbr[5:6, :])
        pick = halo_onehot(nbr, base, halo)
        halo_picks[which * 2 * halo : (which + 1) * 2 * halo, :] = pick
        facing[which] = exact_select(side_by_side(conduct), pick, 1)
    crossing = jnp.max(jnp.where(face_nbr[0:4, :] >= elems, 1, 0))
    crossing = crossing + jnp.max(jnp.where(face_nbr[4:5, :] >= elems + halo, 1, 0))
    fifth = face_nbr[5:6, :]
    crossing = crossing + jnp.max(
        jnp.where((fifth >= elems) & (fifth < elems + halo), 1, 0)
    )
    lane = lax.broadcasted_iota(i32, flags.shape, 1)
    line = jnp.where(lane == 0, crossing, 0)
    skip = jnp.int32(0)
    for k in range(counts_in.shape[1]):
        line = jnp.where(lane == 2 + k, counts_in[0, k], line)
    for k, re, _ in frequencies(counts_in.shape[1]):
        skip = jnp.where(counts_in[0, k] == 1, re, skip)
    flags[...] = jnp.where(lane == 1, skip, line)
    local_part(
        iterate,
        list(range(samples)),
        lambda f, t: coefs[f, t : t + 1, :],
        picks,
        blocks,
        out,
        high,
        low,
    )


def side_by_side(x):
    half = x.shape[0] // 2
    return jnp.concatenate([x[:half], x[half:]], axis=1)


def stacked_halves(x):
    width = x.shape[1] // 2
    return jnp.concatenate([x[:, :width], x[:, width:]], axis=0)


def usual_halo(arrived, scales, blocks, picks):
    dofs = blocks[0].shape[1]
    columns = []
    for which in range(2):
        value = arrived[which]
        width = value.shape[1]
        pairs = scales[which].shape[0]
        scaled = [
            value[j * dofs : (j + 1) * dofs, :] * scales[which][j : j + 1, :]
            for j in range(pairs)
        ]
        got = times_block(blocks[which], jnp.concatenate(scaled, axis=1))
        columns.append(
            jnp.concatenate([got[:, j * width : (j + 1) * width] for j in range(pairs)], axis=0)
        )
    hi, lo = split(jnp.concatenate(columns, axis=1))
    return dot(hi, picks) + dot(lo, picks)


class Halves:
    def __init__(self, low, high):
        self.low, self.high = low, high
        self.shape = (2 * low.shape[0],) + tuple(low.shape[1:])

    def __getitem__(self, at):
        half = self.low.shape[0]
        return self.low[at] if at < half else self.high[at - half]


def other_halo(arrived, block, pick):
    dofs = block.shape[1]
    hi, lo = split(times_block(block, arrived))
    got = dot(hi, pick) + dot(lo, pick)
    return got


def other_sides(flags, even, face_nbr, halo, body):
    elems = face_nbr.shape[1]

    @pl.when(flags[0, 0] > 0)
    def _():
        for which, (usual, base) in enumerate(sides(even, elems, halo)):

            def step(face, carry, which=which, usual=usual, base=base):
                @pl.when(face != usual)
                def _():
                    body(which, face, halo_onehot(face_nbr[pl.ds(face, 1), :], base, halo))

                return carry

            lax.fori_loop(0, FACES, step, 0)


def pair_place(t, half, dofs, elems):
    row, col = t % half * dofs, t // half * elems
    return slice(row, row + dofs), slice(col, col + elems)


def add_others(arrived, even, flags, face_nbr, face_blocks, halo, half, slots, coef_row, factor, total):
    elems = face_nbr.shape[1]
    dofs = total.shape[1]

    def body(which, face, pick):
        block = face_blocks[face]
        for j in range(half):
            got = other_halo(arrived[which][j * dofs : (j + 1) * dofs, :], block, pick)
            for t in (j, half + j):
                if t < len(slots):
                    cols = slice(t // half * elems, (t // half + 1) * elems)
                    field = slots[t]
                    total[field] = total[field] + factor * coef_row(face, t) * got[:, cols]

    other_sides(flags, even, face_nbr, halo, body)


def residual_kernel(
    forcing,
    low_fields,
    high_fields,
    earlier_low,
    earlier_high,
    local,
    arrived0,
    arrived1,
    coefs_in,
    face_nbr,
    blocks,
    face_blocks,
    halo_picks,
    facing,
    flags,
    *rest,
    total_steps,
    groups,
):
    outs = rest[: groups * total_steps]
    coefs, total, extra = rest[groups * total_steps :]
    iterate = Halves(low_fields, high_fields)
    samples, dofs, elems = forcing.shape
    halo = halo_picks.shape[0] // 4
    half = samples // 2
    even = space_even()
    usual = sides(even, elems, halo)
    arrived = (arrived0, arrived1)
    coefs[...] = coefs_in[...]
    conduct = coefs_in[FACES + 1]
    scales = [0.5 * (facing[w] + arrived[w][half * dofs :, :]) for w in range(2)]
    couplings = [
        stacked_halves(
            exact_select(scales[w], halo_picks[w * 2 * halo : (w + 1) * 2 * halo, :])
        )
        for w in range(2)
    ]
    extra[...] = couplings[0] + couplings[1]
    for w in range(2):
        coefs[usual[w][0]] = coefs[usual[w][0]] + couplings[w]

    def add_coupling(which, face, pick):
        got = exact_select(arrived[which][half * dofs :, :], pick)
        nbr = face_nbr[pl.ds(face, 1), :]
        base = usual[which][1]
        here = (nbr >= base) & (nbr < base + halo)
        coupling = jnp.where(here, 0.5 * (conduct + stacked_halves(got)), 0.0)
        coefs[face] = coefs[face] + coupling
        extra[...] = extra[...] + coupling

    other_sides(flags, even, face_nbr, halo, add_coupling)
    coefs[FACES] = coefs[FACES] + extra[...]
    volume = blocks[:, 0 : 2 * dofs][:, :dofs]
    brought = usual_halo(
        arrived, scales, [face_blocks[usual[w][0]] for w in range(2)], halo_picks[...]
    )
    for j in range(samples):
        value = iterate[j]
        total[j] = value + time_step * (
            local[j]
            + brought[pair_place(j, half, dofs, elems)]
            + times_block(volume, value * extra[j : j + 1, :])
        )
    add_others(
        arrived,
        even,
        flags,
        face_nbr,
        face_blocks,
        halo,
        half,
        list(range(samples)),
        lambda f, t: coefs[f, t : t + 1, :],
        time_step,
        total,
    )
    step = lax.axis_index("tm")
    weight = jnp.float32(0.0)
    for n in range(total_steps):
        weight = jnp.where(step == n, jnp.float32(alpha_circ ** (n / total_steps)), weight)
    gate_high = jnp.where(step > 0, weight, 0.0)
    gate_low = jnp.where(step % 2 == 1, weight, 0.0) if two_chips(total_steps) else gate_high
    size = samples // (groups * total_steps)
    for which, out in enumerate(outs):
        at, turn = divmod(which, total_steps)
        first = (partner(step, turn, total_steps) * groups + at) * size
        for i in range(size):
            j = first + i
            inner = forcing[j] - total[j]
            before = lax.rem(j, half)
            late = j >= half
            earlier = jnp.where(late, earlier_high[before], earlier_low[before])
            out[i] = weight * inner + jnp.where(late, gate_high, gate_low) * earlier


def two_chips(devs):
    return devs == 4


def partner(rank, turn, count):
    if count & (count - 1) == 0:
        return rank ^ turn
    return lax.rem(turn + count - rank, count)


def real_fields(total_steps):
    order = [(0, False)]
    if total_steps % 2 == 0:
        order.append((total_steps // 2, False))
    for k in range(1, (total_steps + 1) // 2):
        order += [(k, False), (k, True)]
    return order


def cos_sin(k, n, total_steps):
    turn = 2.0 * math.pi * ((k * n) % total_steps) / total_steps
    c, s = math.cos(turn), math.sin(turn)
    snap = lambda v: float(round(v)) if abs(v - round(v)) < 1e-12 else v
    return snap(c), snap(s)


def weighted(terms):
    total = None
    for constant, value in terms:
        if constant == 0.0:
            continue
        if total is None:
            total = value if constant == 1.0 else constant * value
        elif constant == 1.0:
            total = total + value
        elif constant == -1.0:
            total = total - value
        else:
            total = total + constant * value
    return total


def shift_of(k, total_steps):
    magnitude = alpha_circ ** (1.0 / total_steps)
    c, s = cos_sin(k, 1, total_steps)
    return 1.0 - magnitude * c, magnitude * s


def theta_rows(k, total_steps, diag):
    shift_real, shift_imag = shift_of(k, total_steps)
    denom = shift_real + (time_step * relax_rho) * diag
    if shift_imag == 0.0:
        return 1.0 / denom, None
    modulus = denom * denom + shift_imag * shift_imag
    return denom / modulus, -shift_imag / modulus


def frequencies(total_steps):
    order = real_fields(total_steps)
    return [
        (k, at, order.index((k, True)) if (k, True) in order else None)
        for at, (k, imag) in enumerate(order)
        if not imag
    ]


def kept_slots(flags, samples, total_steps):
    skip = flags[0, 1]
    kept = total_steps - 1
    slots = []
    for t in range(samples * kept):
        s, i = divmod(t, kept)
        slots.append(s * total_steps + jnp.where(skip <= i, i + 1, i))
    return slots


def even_slots(slots):
    return slots + slots[: len(slots) % 2]


def my_first(samples, at, groups):
    return (lax.axis_index("tm") * groups + at) * samples


def sample_row(coefs, total_steps, first):
    kept = total_steps - 1
    return lambda f, t: coefs[f, pl.ds(first + t // kept, 1), :]


def spectrum_kernel(
    flags, coefs, send_ref, own, near, *rest, total_steps, at, groups
):
    arrived, (spectrum, first_w, pack0, pack1, pieces) = (
        rest[:total_steps],
        rest[total_steps:],
    )
    samples = arrived[0].shape[0]
    first = my_first(samples, at, groups)
    rank = lax.axis_index("tm")
    for turn, piece in enumerate(arrived):
        pieces[partner(rank, turn, total_steps)] = piece[...]
    if two_chips(total_steps):
        here = at * samples
        there = groups * samples + here
        gate = jnp.where(rank < 2, jnp.float32(alpha_circ ** (2 / total_steps)), 0.0)
        for s in range(samples):
            before = jnp.where(rank == 0, near[here + s], own[there + s])
            pieces[2, s] = pieces[2, s] + gate * before
    for s in range(samples):
        diag = coefs[FACES, pl.ds(first + s, 1), :]
        base = s * total_steps
        for k, re, im in frequencies(total_steps):
            tables = [cos_sin(k, n, total_steps) for n in range(total_steps)]
            real = weighted([(tables[n][0], pieces[n, s]) for n in range(total_steps)])
            rate_real, rate_imag = theta_rows(k, total_steps, diag)
            spectrum[base + re] = real
            if im is None:
                first_w[base + re] = rate_real * real
            else:
                imag = weighted([(-tables[n][1], pieces[n, s]) for n in range(total_steps)])
                spectrum[base + im] = imag
                first_w[base + re] = rate_real * real - rate_imag * imag
                first_w[base + im] = rate_real * imag + rate_imag * real
    slots = kept_slots(flags, samples, total_steps)
    pack_fields(first_w, even_slots(slots), send_ref[...], (pack0, pack1))


def sweep_local_kernel(
    flags,
    fields,
    spectrum,
    coefs,
    picks,
    blocks,
    halo_picks,
    *rest,
    total_steps,
    at,
    groups,
    first_turn,
):
    if first_turn:
        out, thetas, scales, total, high, low = rest
    else:
        out, total, high, low = rest
    elems = fields.shape[2]
    samples = fields.shape[0] // total_steps
    first = my_first(samples, at, groups)
    slots = kept_slots(flags, samples, total_steps)
    row = sample_row(coefs, total_steps, first)
    if first_turn:
        halo = halo_picks.shape[0] // 4
        half = scales.shape[1]
        usual = sides(space_even(), elems, halo)
        count = len(slots)
        for w in range(2):
            lines = [
                row(usual[w][0], t if t < count else 0) for t in range(2 * half)
            ]
            sides_of = [jnp.concatenate(lines[:half], 0), jnp.concatenate(lines[half:], 0)]
            scales[w] = time_step * exact_select(
                jnp.concatenate(sides_of, axis=1),
                halo_picks[w * 2 * halo : (w + 1) * 2 * halo, :],
                1,
            )
        diag = jnp.concatenate(
            [coefs[FACES, pl.ds(first + s, 1), :] for s in range(samples)], axis=0
        )
        for i, (k, _, im) in enumerate(frequencies(total_steps)):
            rate_real, rate_imag = theta_rows(k, total_steps, diag)
            thetas[2 * i] = rate_real
            if im is not None:
                thetas[2 * i + 1] = rate_imag
    local_part(fields, slots, row, picks, blocks, total, high, low)
    for s in range(samples):
        base = s * total_steps
        for k, re, im in frequencies(total_steps):
            shift_real, shift_imag = shift_of(k, total_steps)
            value = fields[base + re]
            kept = spectrum[base + re] - (shift_real * value + time_step * total[base + re])
            if im is not None:
                other = fields[base + im]
                kept = kept + shift_imag * other
                out[base + im] = spectrum[base + im] - (
                    shift_real * other + shift_imag * value + time_step * total[base + im]
                )
            out[base + re] = kept


def sweep_update_kernel(
    flags,
    current,
    inner,
    arrived0,
    arrived1,
    coefs,
    face_nbr,
    face_blocks,
    halo_picks,
    thetas,
    scales,
    *rest,
    turn,
    total_steps,
    last,
    at,
    groups,
):
    even = space_even()
    if last:
        outs, (total, solved) = rest[:total_steps], rest[total_steps:]
    else:
        send_ref, solved, pack0, pack1, total = rest
    fields, dofs, elems = current.shape
    samples = fields // total_steps
    first = my_first(samples, at, groups)
    slots = kept_slots(flags, samples, total_steps)
    arrived = (arrived0, arrived1)
    halo = halo_picks.shape[0] // 4
    half = scales.shape[1]
    usual = sides(even, elems, halo)
    brought = usual_halo(
        arrived,
        [scales[w] for w in range(2)],
        [face_blocks[usual[w][0]] for w in range(2)],
        halo_picks[...],
    )
    for t, field in enumerate(slots):
        total[field] = inner[field] - brought[pair_place(t, half, dofs, elems)]
    add_others(
        arrived,
        even,
        flags,
        face_nbr,
        face_blocks,
        halo,
        half,
        slots,
        sample_row(coefs, total_steps, first),
        -time_step,
        total,
    )
    for s in range(samples):
        base = s * total_steps
        for i, (k, re, im) in enumerate(frequencies(total_steps)):
            active = flags[0, 2 + k] > turn + 1
            rate_real = thetas[2 * i, s : s + 1, :]
            value, rest_real = current[base + re], total[base + re]
            change = rate_real * rest_real
            if im is not None:
                rate_imag = thetas[2 * i + 1, s : s + 1, :]
                other, rest_imag = current[base + im], total[base + im]
                change = change - rate_imag * rest_imag
                solved[base + im] = jnp.where(
                    active, other + (rate_real * rest_imag + rate_imag * rest_real), other
                )
            solved[base + re] = jnp.where(active, value + change, value)
    if not last:
        pack_fields(solved, even_slots(slots), send_ref[...], (pack0, pack1))
        return
    rank = lax.axis_index("tm")
    for s in range(samples):
        base = s * total_steps
        for n in range(total_steps):
            scale = alpha_circ ** (-n / total_steps) / total_steps
            terms = []
            for k, re, im in frequencies(total_steps):
                c, sn = cos_sin(k, n, total_steps)
                if im is None:
                    terms.append((c, solved[base + re]))
                else:
                    terms += [(2.0 * c, solved[base + re]), (-2.0 * sn, solved[base + im])]
            total[n * samples + s] = scale * weighted(terms)
    for turn_to, out in enumerate(outs):
        step = partner(rank, turn_to, total_steps)
        for s in range(samples):
            out[s] = total[step * samples + s]


def assemble_kernel(*rest, total_steps, groups):
    pieces, (out, done) = rest[:-2], rest[-2:]
    size = pieces[0].shape[0]
    rank = lax.axis_index("tm")
    copies = []
    for which, piece in enumerate(pieces):
        at, turn = divmod(which, total_steps)
        first = (partner(rank, turn, total_steps) * groups + at) * size
        copies.append(
            pltpu.make_async_copy(piece, out.at[pl.ds(first, size)], done.at[which])
        )
    for copy in copies:
        copy.start()
    for copy in copies:
        copy.wait()


vmem = pl.BlockSpec(memory_space=pltpu.VMEM)


def run(
    kernel, inputs, outs, scratch=(), in_hbm=(), out_hbm=(), flops=10**9
):
    def spec(i, outside):
        return pl.BlockSpec(memory_space=pltpu.HBM) if i in outside else vmem

    inputs = [
        pltpu.with_memory_space_constraint(value, pltpu.HBM) if i in in_hbm else value
        for i, value in enumerate(inputs)
    ]
    return pl.pallas_call(
        kernel,
        out_shape=[jax.ShapeDtypeStruct(*o) for o in outs],
        in_specs=[spec(i, in_hbm) for i in range(len(inputs))],
        out_specs=[spec(i, out_hbm) for i in range(len(outs))],
        scratch_shapes=[pltpu.VMEM(*s) if isinstance(s, tuple) else s for s in scratch],
        compiler_params=pltpu.CompilerParams(vmem_limit_bytes=40 << 20),
        cost_estimate=pl.CostEstimate(flops=flops, bytes_accessed=1 << 22, transcendentals=0),
    )(*inputs)


def neighbour_swap(value, start):
    axes = ("groups", "tm", "space")
    parts, devs, count = (lax.axis_size(axis) for axis in axes)
    pairs = []
    for part in range(parts):
        for tm in range(devs):
            for space in range(count):
                step = 1 if (space + tm + start) % 2 == 0 else -1
                to_part, to_space = part, space + step
                if not 0 <= to_space < count:
                    to_part, to_space = part ^ 1, space
                if to_part < parts:
                    pairs.append(
                        ((part * devs + tm) * count + space, (to_part * devs + tm) * count + to_space)
                    )
    return lax.ppermute(value, axes, pairs)


def time_swap(value, turn):
    count = lax.axis_size("tm")
    pairs = [(i, int(partner(i, turn, count))) for i in range(count)]
    return value if turn == 0 else lax.ppermute(value, "tm", pairs)


def per_device(
    forcing,
    iterate,
    kappa_mean,
    kappa_modes,
    grad_mats,
    face_mats,
    lattice_shift,
    gen_vector,
    sweep_counts,
    face_nbr,
    halo_send,
):
    samples, steps_dev, dofs, elems = forcing.shape
    halo = halo_send.shape[1]
    devs = lax.axis_size("tm")
    total_steps = steps_dev * devs
    part = samples // devs
    half = samples // 2
    cube = (samples, dofs, elems)
    forcing = forcing.reshape(cube)
    iterate = iterate.reshape(cube)
    onward = [(i, (i + 1) % devs) for i in range(devs)]
    rows = half * dofs
    copies = 2 * (half // group_size(half))
    (
        pack0, pack1, send, conduct, low, high, face_nbr, grad_mats, face_mats, counts_line
    ) = run(
        prepare_kernel,
        (
            iterate,
            halo_send,
            lattice_shift.reshape(1, -1),
            gen_vector.reshape(1, -1),
            kappa_mean.reshape(1, -1),
            kappa_modes,
            face_nbr,
            grad_mats,
            face_mats,
            sweep_counts.reshape(1, -1),
        ),
        [
            ((rows + half, 2 * halo), f32),
            ((rows + half, 2 * halo), f32),
            ((2 * elems, 4 * halo), bf16),
            ((samples, elems), f32),
            ((half, dofs, elems), f32),
            ((half, dofs, elems), f32),
            (face_nbr.shape, i32),
            (grad_mats.shape, f32),
            (face_mats.shape, f32),
            ((1, sweep_counts.shape[0]), i32),
        ],
        [
            (halo_send.shape, i32),
            ((1, lattice_shift.shape[0]), f32),
            ((1, gen_vector.shape[0]), i32),
            ((1, elems), f32),
            (kappa_modes.shape, f32),
            pltpu.SemaphoreType.DMA((5,)),
            pltpu.SemaphoreType.DMA((copies,)),
            pltpu.SemaphoreType.DMA((4,)),
        ],
        in_hbm=range(10),
    )
    arrived0 = neighbour_swap(pack0, 0)
    arrived1 = neighbour_swap(pack1, 1)
    earlier_high = lax.ppermute(high, "tm", onward)
    if two_chips(devs):
        earlier_low = time_swap(low, 1)
    else:
        earlier_low = lax.ppermute(low, "tm", onward)
    blocks_wide = (FACES + 1) * dofs
    splits = lambda count: [((count, blocks_wide, elems), bf16)] * 2
    (
        local, coefs, picks, blocks, face_blocks, halo_picks, flags, facing
    ) = run(
        first_local_kernel,
        (low, high, conduct, face_nbr, grad_mats, face_mats, counts_line),
        [
            (cube, f32),
            ((FACES + 2, samples, elems), f32),
            ((elems, FACES * elems), bf16),
            ((2 * dofs, blocks_wide), bf16),
            ((FACES, 2 * dofs, dofs), bf16),
            ((4 * halo, 2 * elems), bf16),
            ((1, 2 * halo), i32),
            ((2, half, 2 * halo), f32),
        ],
        splits(samples) + [((blocks_wide, 2 * dofs), f32)],
        flops=4 * 10**9,
    )
    groups = GROUPS if part % GROUPS == 0 else 1
    share = part // groups
    piece = ((share, dofs, elems), f32)
    *scaled, coefs = run(
        functools.partial(residual_kernel, total_steps=total_steps, groups=groups),
        (
            forcing,
            low,
            high,
            earlier_low,
            earlier_high,
            local,
            arrived0,
            arrived1,
            coefs,
            face_nbr,
            blocks,
            face_blocks,
            halo_picks,
            facing,
            flags,
        ),
        [piece] * (groups * devs) + [((FACES + 2, samples, elems), f32)],
        [(cube, f32), ((samples, elems), f32)],
    )
    fields = share * total_steps
    swept = share * (total_steps - 1)
    pairs = (swept + 1) // 2
    some = ((fields, dofs, elems), f32)
    packed = ((pairs * dofs, 2 * halo), f32)
    restored = []
    for at in range(groups):
        mine = dict(total_steps=total_steps, at=at, groups=groups)
        pieces = [time_swap(scaled[at * devs + turn], turn) for turn in range(devs)]
        spectrum, current, pack0, pack1 = run(
            functools.partial(spectrum_kernel, **mine),
            (flags, coefs, send, low, earlier_low, *pieces),
            [some, some, packed, packed],
            [((total_steps, share, dofs, elems), f32)],
        )
        for turn in range(MAXS - 1):
            arrived0 = neighbour_swap(pack0, 0)
            arrived1 = neighbour_swap(pack1, 1)
            inner, *tables = run(
                functools.partial(sweep_local_kernel, first_turn=turn == 0, **mine),
                (flags, current, spectrum, coefs, picks, blocks, halo_picks),
                [some]
                + [
                    ((2 * len(frequencies(total_steps)), share, elems), f32),
                    ((2, pairs, 2 * halo), f32),
                ]
                * (turn == 0),
                [some] + splits(swept),
                    flops=3 * 10**9 // groups,
            )
            if turn == 0:
                thetas, scales = tables
            last = turn == MAXS - 2
            inputs = (
                flags,
                current,
                inner,
                arrived0,
                arrived1,
                coefs,
                face_nbr,
                face_blocks,
                halo_picks,
                thetas,
                scales,
            )
            kernel = functools.partial(sweep_update_kernel, turn=turn, last=last, **mine)
            if last:
                series = run(
                    kernel, inputs, [piece] * devs, [some, some]
                )
            else:
                current, pack0, pack1 = run(
                    kernel,
                    inputs + (send,),
                    [some, packed, packed],
                    [some],
                )
        restored += [time_swap(series[turn], turn) for turn in range(devs)]
    (out,) = run(
        functools.partial(assemble_kernel, total_steps=total_steps, groups=groups),
        tuple(restored),
        [(cube, f32)],
        [pltpu.SemaphoreType.DMA((len(restored),))],
        out_hbm=(0,),
    )
    return out.reshape(samples, steps_dev, dofs, elems)


def solution(mesh):
    placed = (
        P("groups", "tm", None, "space"),
        P("groups", "tm", None, "space"),
        P("space"),
        P(None, "space"),
        P(),
        P(),
        P("groups"),
        P(),
        P(),
        P(None, "space"),
        P(None, "space"),
    )
    return jax.shard_map(
        per_device,
        mesh=mesh,
        in_specs=placed,
        out_specs=P("groups", "tm", None, "space"),
        check_vma=False,
    )
```

```python
import functools
import math

import jax
import jax.numpy as jnp
from jax import lax
from jax.experimental import pallas as pl
from jax.experimental.pallas import tpu as pltpu
from jax.sharding import PartitionSpec as P

MAXS = 3
alpha_circ = 0.05
time_step = 0.1
relax_rho = 2.3
highest = lax.Precision.HIGHEST
f32, bf16, i32 = jnp.float32, jnp.bfloat16, jnp.int32
FACES = 6
GROUPS = 2


def dot(a, b):
    return jnp.dot(a, b, preferred_element_type=f32)


def split(x):
    hi = x.astype(bf16)
    return hi, (x - hi.astype(f32)).astype(bf16)


def exact_select(x, onehot, across=0):
    a, b = split(x)
    c = (x - a.astype(f32) - b.astype(f32)).astype(bf16)
    times = lambda v: lax.dot_general(
        v, onehot, (((1,), (across,)), ((), ())), preferred_element_type=f32
    )
    return times(a) + (times(b) + times(c))


def times_block(stacked, x):
    rows = stacked.shape[0] // 2
    hi, lo = split(x)
    both = dot(stacked, hi)
    return both[:rows] + (both[rows:] + dot(stacked[:rows], lo))


def rows_iota(shape):
    return lax.broadcasted_iota(i32, shape, 0)


def halo_onehot(nbr_row, base, halo):
    elems = nbr_row.shape[1]
    entry = nbr_row - base
    here = (entry >= 0) & (entry < halo)
    entry = jnp.where(here, entry, -2 * halo)
    row = rows_iota((2 * halo, elems))
    left = (row == entry).astype(f32).astype(bf16)
    right = (row == entry + halo).astype(f32).astype(bf16)
    return jnp.concatenate([left, right], axis=1)


def space_even():
    return lax.rem(lax.axis_index("space") + lax.axis_index("tm"), 2) == 0


def sides(even, elems, halo):
    below, above = elems, elems + halo
    return (
        (jnp.where(even, 5, 4), jnp.where(even, above, below)),
        (jnp.where(even, 4, 5), jnp.where(even, below, above)),
    )


def group_size(count):
    return next(size for size in (4, 3, 2, 1) if count % size == 0)


def pack_group(ref, left, right, send, first, outs):
    dofs = ref.shape[1]
    width = send.shape[1] // 2
    sides_by_side = [jnp.concatenate([ref[i] for i in side], axis=0) for side in (left, right)]
    hi, lo = split(jnp.concatenate(sides_by_side, axis=1))
    got = dot(hi, send) + dot(lo, send)
    rows = slice(first * dofs, (first + len(left)) * dofs)
    for which, out in enumerate(outs):
        out[rows, :] = got[:, which * width : (which + 1) * width]


def pack_fields(ref, fields, send, outs):
    half = len(fields) // 2
    size = group_size(half)
    for j in range(0, half, size):
        pack_group(
            ref, fields[j : j + size], fields[half + j : half + j + size], send, j, outs
        )


def prepare_kernel(
    iterate_in,
    halo_send_in,
    shift_in,
    gen_in,
    mean_in,
    modes_in,
    nbr_in,
    grads_in,
    face_mats_in,
    counts_in,
    pack0,
    pack1,
    send_out,
    conduct_out,
    low,
    high,
    nbr,
    grads,
    face_mats,
    counts,
    halo_send,
    shift,
    gen,
    mean,
    modes,
    small_done,
    field_done,
    later_done,
):
    iterate = Halves(low, high)
    samples, dofs, elems = iterate.shape
    halo = halo_send.shape[1]
    half = samples // 2
    size = group_size(half)
    small = [
        pltpu.make_async_copy(source, target, small_done.at[i])
        for i, (source, target) in enumerate(
            (
                (halo_send_in, halo_send),
                (shift_in, shift),
                (gen_in, gen),
                (mean_in, mean),
                (modes_in, modes),
            )
        )
    ]
    large = []
    for j in range(0, half, size):
        for at, side in ((j, low), (half + j, high)):
            large.append(
                pltpu.make_async_copy(
                    iterate_in.at[pl.ds(at, size)],
                    side.at[pl.ds(j, size)],
                    field_done.at[len(large)],
                )
            )
    later = [
        pltpu.make_async_copy(source, target, later_done.at[i])
        for i, (source, target) in enumerate(
            ((nbr_in, nbr), (grads_in, grads), (face_mats_in, face_mats), (counts_in, counts))
        )
    ]
    for copy in small + large + later:
        copy.start()
    for copy in small + large:
        copy.wait()
    even = space_even()
    down = jnp.concatenate([halo_send[0:1, :]] * 2, axis=1)
    up = jnp.concatenate([halo_send[1:2, :]] * 2, axis=1)
    lane = lax.broadcasted_iota(i32, (1, 2 * halo), 1)
    row = rows_iota((2 * elems, 2 * halo))
    for which in range(2):
        ids = jnp.where(even == (which == 0), up, down)
        ids = jnp.where(lane < halo, ids, ids + elems)
        send_out[:, which * 2 * halo : (which + 1) * 2 * halo] = (
            (row == ids).astype(f32).astype(bf16)
        )
    position = rows_iota((samples, gen.shape[1]))
    residue = lax.rem(position * gen[...], samples)
    shifted = residue.astype(f32) / samples + shift[...]
    fraction = shifted - jnp.floor(shifted)
    points = 0.5 - jnp.abs(2.0 * fraction - 1.0)
    conduct = mean[...] * (
        1.0 + jnp.dot(points, modes[...], precision=highest, preferred_element_type=f32)
    )
    conduct_out[...] = conduct
    send = send_out[...]
    got = exact_select(jnp.concatenate([conduct[:half], conduct[half:]], axis=1), send)
    pack0[half * dofs :, :] = got[:, : 2 * halo]
    pack1[half * dofs :, :] = got[:, 2 * halo :]
    for j in range(0, half, size):
        left = list(range(j, j + size))
        pack_group(iterate, left, [half + i for i in left], send, j, (pack0, pack1))
    for copy in later:
        copy.wait()


def local_part(fields, slots, coef_row, picks, blocks, out, high, low):
    dofs, elems = fields.shape[1], fields.shape[2]
    size = group_size(len(slots))
    for first in range(0, len(slots), size):
        group = range(first, first + size)
        values = [fields[slots[t]] for t in group]
        hi, lo = split(jnp.concatenate(values, axis=0))
        for t, value in zip(group, values):
            a, b = split(value * coef_row(FACES, t))
            high[t, 0:dofs, :] = a
            low[t, 0:dofs, :] = b
        for f in range(FACES):
            pick = picks[:, f * elems : (f + 1) * elems]
            got = dot(hi, pick) + dot(lo, pick)
            at = (f + 1) * dofs
            for i, t in enumerate(group):
                a, b = split(got[i * dofs : (i + 1) * dofs] * coef_row(f, t))
                high[t, at : at + dofs, :] = a
                low[t, at : at + dofs, :] = b
        stacked = blocks[...]
        for t in group:
            both = dot(stacked, high[t])
            out[slots[t]] = both[:dofs] + (both[dofs:] + dot(stacked[:dofs], low[t]))


def first_local_kernel(
    low_fields,
    high_fields,
    conduct_ref,
    face_nbr,
    grads,
    face_mats,
    counts_in,
    out,
    coefs,
    picks,
    blocks,
    face_blocks,
    halo_picks,
    flags,
    facing,
    high,
    low,
    wide,
):
    iterate = Halves(low_fields, high_fields)
    samples, dofs, elems = iterate.shape
    halo = halo_picks.shape[0] // 4
    even = space_even()
    row = rows_iota((elems, elems))
    for f in range(FACES):
        picks[:, f * elems : (f + 1) * elems] = (
            (row == face_nbr[f : f + 1, :]).astype(f32).astype(bf16)
        )
    conduct = conduct_ref[...]
    diag = conduct
    for f in range(FACES):
        nbr = face_nbr[f : f + 1, :]
        across = exact_select(conduct, picks[:, f * elems : (f + 1) * elems])
        inside = (nbr >= 0) & (nbr < elems)
        coupling = jnp.where(inside, 0.5 * (conduct + across), 0.0)
        coefs[f] = coupling
        diag = diag + jnp.where(nbr < 0, conduct, coupling)
    coefs[FACES] = diag
    coefs[FACES + 1] = conduct
    volume = (rows_iota((dofs, dofs)) == lax.broadcasted_iota(i32, (dofs, dofs), 1)).astype(f32)
    for d in range(grads.shape[0]):
        volume = volume + lax.dot_general(
            grads[d], grads[d], (((0,), (0,)), ((), ())), precision=highest,
            preferred_element_type=f32,
        )
    wide[...] = jnp.zeros(wide.shape, f32)
    wide[0:dofs, 0:dofs] = volume
    for f in range(FACES):
        block = face_mats[f // 2]
        at = (f + 1) * dofs
        wide[at : at + dofs, 0:dofs] = block if f % 2 == 0 else block.T
    turned = wide[...].T[:dofs, :]
    hi, lo = split(turned)
    blocks[0:dofs, :] = hi
    blocks[dofs:, :] = lo
    for f in range(FACES):
        block = face_mats[f // 2]
        hi, lo = split(block.T if f % 2 == 0 else block)
        face_blocks[f, 0:dofs, :] = hi
        face_blocks[f, dofs:, :] = lo
    for which, (face, base) in enumerate(sides(even, elems, halo)):
        nbr = jnp.where(face == 4, face_nbr[4:5, :], face_nbr[5:6, :])
        pick = halo_onehot(nbr, base, halo)
        halo_picks[which * 2 * halo : (which + 1) * 2 * halo, :] = pick
        facing[which] = exact_select(side_by_side(conduct), pick, 1)
    crossing = jnp.max(jnp.where(face_nbr[0:4, :] >= elems, 1, 0))
    crossing = crossing + jnp.max(jnp.where(face_nbr[4:5, :] >= elems + halo, 1, 0))
    fifth = face_nbr[5:6, :]
    crossing = crossing + jnp.max(
        jnp.where((fifth >= elems) & (fifth < elems + halo), 1, 0)
    )
    lane = lax.broadcasted_iota(i32, flags.shape, 1)
    line = jnp.where(lane == 0, crossing, 0)
    skip = jnp.int32(0)
    for k in range(counts_in.shape[1]):
        line = jnp.where(lane == 2 + k, counts_in[0, k], line)
    for k, re, _ in frequencies(counts_in.shape[1]):
        skip = jnp.where(counts_in[0, k] == 1, re, skip)
    flags[...] = jnp.where(lane == 1, skip, line)
    local_part(
        iterate,
        list(range(samples)),
        lambda f, t: coefs[f, t : t + 1, :],
        picks,
        blocks,
        out,
        high,
        low,
    )


def side_by_side(x):
    half = x.shape[0] // 2
    return jnp.concatenate([x[:half], x[half:]], axis=1)


def stacked_halves(x):
    width = x.shape[1] // 2
    return jnp.concatenate([x[:, :width], x[:, width:]], axis=0)


def usual_halo(arrived, scales, blocks, picks):
    dofs = blocks[0].shape[1]
    columns = []
    for which in range(2):
        value = arrived[which]
        width = value.shape[1]
        pairs = scales[which].shape[0]
        scaled = [
            value[j * dofs : (j + 1) * dofs, :] * scales[which][j : j + 1, :]
            for j in range(pairs)
        ]
        got = times_block(blocks[which], jnp.concatenate(scaled, axis=1))
        columns.append(
            jnp.concatenate([got[:, j * width : (j + 1) * width] for j in range(pairs)], axis=0)
        )
    hi, lo = split(jnp.concatenate(columns, axis=1))
    return dot(hi, picks) + dot(lo, picks)


class Halves:
    def __init__(self, low, high):
        self.low, self.high = low, high
        self.shape = (2 * low.shape[0],) + tuple(low.shape[1:])

    def __getitem__(self, at):
        half = self.low.shape[0]
        return self.low[at] if at < half else self.high[at - half]


def other_halo(arrived, block, pick):
    dofs = block.shape[1]
    hi, lo = split(times_block(block, arrived))
    got = dot(hi, pick) + dot(lo, pick)
    return got


def other_sides(flags, even, face_nbr, halo, body):
    elems = face_nbr.shape[1]

    @pl.when(flags[0, 0] > 0)
    def _():
        for which, (usual, base) in enumerate(sides(even, elems, halo)):

            def step(face, carry, which=which, usual=usual, base=base):
                @pl.when(face != usual)
                def _():
                    body(which, face, halo_onehot(face_nbr[pl.ds(face, 1), :], base, halo))

                return carry

            lax.fori_loop(0, FACES, step, 0)


def pair_place(t, half, dofs, elems):
    row, col = t % half * dofs, t // half * elems
    return slice(row, row + dofs), slice(col, col + elems)


def add_others(arrived, even, flags, face_nbr, face_blocks, halo, half, slots, coef_row, factor, total):
    elems = face_nbr.shape[1]
    dofs = total.shape[1]

    def body(which, face, pick):
        block = face_blocks[face]
        for j in range(half):
            got = other_halo(arrived[which][j * dofs : (j + 1) * dofs, :], block, pick)
            for t in (j, half + j):
                if t < len(slots):
                    cols = slice(t // half * elems, (t // half + 1) * elems)
                    field = slots[t]
                    total[field] = total[field] + factor * coef_row(face, t) * got[:, cols]

    other_sides(flags, even, face_nbr, halo, body)


def residual_kernel(
    forcing,
    low_fields,
    high_fields,
    earlier_low,
    earlier_high,
    local,
    arrived0,
    arrived1,
    coefs_in,
    face_nbr,
    blocks,
    face_blocks,
    halo_picks,
    facing,
    flags,
    *rest,
    total_steps,
    groups,
):
    outs = rest[: groups * total_steps]
    coefs, total, extra = rest[groups * total_steps :]
    iterate = Halves(low_fields, high_fields)
    samples, dofs, elems = forcing.shape
    halo = halo_picks.shape[0] // 4
    half = samples // 2
    even = space_even()
    usual = sides(even, elems, halo)
    arrived = (arrived0, arrived1)
    coefs[...] = coefs_in[...]
    conduct = coefs_in[FACES + 1]
    scales = [0.5 * (facing[w] + arrived[w][half * dofs :, :]) for w in range(2)]
    couplings = [
        stacked_halves(
            exact_select(scales[w], halo_picks[w * 2 * halo : (w + 1) * 2 * halo, :])
        )
        for w in range(2)
    ]
    extra[...] = couplings[0] + couplings[1]
    for w in range(2):
        coefs[usual[w][0]] = coefs[usual[w][0]] + couplings[w]

    def add_coupling(which, face, pick):
        got = exact_select(arrived[which][half * dofs :, :], pick)
        nbr = face_nbr[pl.ds(face, 1), :]
        base = usual[which][1]
        here = (nbr >= base) & (nbr < base + halo)
        coupling = jnp.where(here, 0.5 * (conduct + stacked_halves(got)), 0.0)
        coefs[face] = coefs[face] + coupling
        extra[...] = extra[...] + coupling

    other_sides(flags, even, face_nbr, halo, add_coupling)
    coefs[FACES] = coefs[FACES] + extra[...]
    volume = blocks[:, 0 : 2 * dofs][:, :dofs]
    brought = usual_halo(
        arrived, scales, [face_blocks[usual[w][0]] for w in range(2)], halo_picks[...]
    )
    for j in range(samples):
        value = iterate[j]
        total[j] = value + time_step * (
            local[j]
            + brought[pair_place(j, half, dofs, elems)]
            + times_block(volume, value * extra[j : j + 1, :])
        )
    add_others(
        arrived,
        even,
        flags,
        face_nbr,
        face_blocks,
        halo,
        half,
        list(range(samples)),
        lambda f, t: coefs[f, t : t + 1, :],
        time_step,
        total,
    )
    step = lax.axis_index("tm")
    weight = jnp.float32(0.0)
    for n in range(total_steps):
        weight = jnp.where(step == n, jnp.float32(alpha_circ ** (n / total_steps)), weight)
    gate_high = jnp.where(step > 0, weight, 0.0)
    gate_low = jnp.where(step % 2 == 1, weight, 0.0) if two_chips(total_steps) else gate_high
    size = samples // (groups * total_steps)
    for which, out in enumerate(outs):
        at, turn = divmod(which, total_steps)
        first = (partner(step, turn, total_steps) * groups + at) * size
        for i in range(size):
            j = first + i
            inner = forcing[j] - total[j]
            before = lax.rem(j, half)
            late = j >= half
            earlier = jnp.where(late, earlier_high[before], earlier_low[before])
            out[i] = weight * inner + jnp.where(late, gate_high, gate_low) * earlier


def two_chips(devs):
    return devs == 4


def partner(rank, turn, count):
    if count & (count - 1) == 0:
        return rank ^ turn
    return lax.rem(turn + count - rank, count)


def real_fields(total_steps):
    order = [(0, False)]
    if total_steps % 2 == 0:
        order.append((total_steps // 2, False))
    for k in range(1, (total_steps + 1) // 2):
        order += [(k, False), (k, True)]
    return order


def cos_sin(k, n, total_steps):
    turn = 2.0 * math.pi * ((k * n) % total_steps) / total_steps
    c, s = math.cos(turn), math.sin(turn)
    snap = lambda v: float(round(v)) if abs(v - round(v)) < 1e-12 else v
    return snap(c), snap(s)


def weighted(terms):
    total = None
    for constant, value in terms:
        if constant == 0.0:
            continue
        if total is None:
            total = value if constant == 1.0 else constant * value
        elif constant == 1.0:
            total = total + value
        elif constant == -1.0:
            total = total - value
        else:
            total = total + constant * value
    return total


def shift_of(k, total_steps):
    magnitude = alpha_circ ** (1.0 / total_steps)
    c, s = cos_sin(k, 1, total_steps)
    return 1.0 - magnitude * c, magnitude * s


def theta_rows(k, total_steps, diag):
    shift_real, shift_imag = shift_of(k, total_steps)
    denom = shift_real + (time_step * relax_rho) * diag
    if shift_imag == 0.0:
        return 1.0 / denom, None
    modulus = denom * denom + shift_imag * shift_imag
    return denom / modulus, -shift_imag / modulus


def frequencies(total_steps):
    order = real_fields(total_steps)
    return [
        (k, at, order.index((k, True)) if (k, True) in order else None)
        for at, (k, imag) in enumerate(order)
        if not imag
    ]


def slot_order(samples, total_steps, inner):
    size = samples // inner
    lists = [
        [(g * size + s, i) for s in range(size) for i in range(total_steps - 1)]
        for g in range(inner)
    ]
    if inner == 1:
        return lists[0]
    middle = len(lists[0]) // 2
    return [pair for part in lists for pair in part[:middle]] + [
        pair for part in lists for pair in part[middle:]
    ]


def kept_slots(flags, order, total_steps):
    skip = flags[0, 1]
    return [s * total_steps + jnp.where(skip <= i, i + 1, i) for s, i in order]


def even_slots(slots):
    return slots + slots[: len(slots) % 2]


def my_first(samples, at, groups):
    return (lax.axis_index("tm") * groups + at) * samples


def sample_row(coefs, order, first):
    return lambda f, t: coefs[f, pl.ds(first + order[t][0], 1), :]


def spectrum_kernel(
    flags, coefs, send_ref, own, near, *rest, total_steps, at, groups
):
    arrived, (spectrum, first_w, pack0, pack1, pieces) = rest[:total_steps], rest[-5:]
    samples = arrived[0].shape[0]
    first = my_first(samples, at, groups)
    rank = lax.axis_index("tm")
    for turn, piece in enumerate(arrived):
        pieces[partner(rank, turn, total_steps)] = piece[...]
    if two_chips(total_steps):
        here = at * samples
        there = groups * samples + here
        gate = jnp.where(rank < 2, jnp.float32(alpha_circ ** (2 / total_steps)), 0.0)
        for s in range(samples):
            before = jnp.where(rank == 0, near[here + s], own[there + s])
            pieces[2, s] = pieces[2, s] + gate * before
    for s in range(samples):
        diag = coefs[FACES, pl.ds(first + s, 1), :]
        base = s * total_steps
        for k, re, im in frequencies(total_steps):
            tables = [cos_sin(k, n, total_steps) for n in range(total_steps)]
            real = weighted([(tables[n][0], pieces[n, s]) for n in range(total_steps)])
            rate_real, rate_imag = theta_rows(k, total_steps, diag)
            spectrum[base + re] = real
            if im is None:
                first_w[base + re] = rate_real * real
            else:
                imag = weighted([(-tables[n][1], pieces[n, s]) for n in range(total_steps)])
                spectrum[base + im] = imag
                first_w[base + re] = rate_real * real - rate_imag * imag
                first_w[base + im] = rate_real * imag + rate_imag * real
    slots = kept_slots(flags, slot_order(samples, total_steps, 1), total_steps)
    pack_fields(first_w, even_slots(slots), send_ref[...], (pack0, pack1))


def sweep_local_kernel(
    flags,
    fields,
    coefs,
    picks,
    blocks,
    halo_picks,
    *rest,
    total_steps,
    at,
    groups,
    first_turn,
    inner,
):
    spectra, rest = rest[:inner], rest[inner:]
    if first_turn:
        out, thetas, scales, total, high, low = rest
    else:
        out, total, high, low = rest
    elems = fields.shape[2]
    samples = fields.shape[0] // total_steps
    first = my_first(samples, at, groups)
    order = slot_order(samples, total_steps, inner)
    slots = kept_slots(flags, order, total_steps)
    row = sample_row(coefs, order, first)
    if first_turn:
        halo = halo_picks.shape[0] // 4
        half = scales.shape[1]
        usual = sides(space_even(), elems, halo)
        count = len(slots)
        for w in range(2):
            lines = [
                row(usual[w][0], t if t < count else 0) for t in range(2 * half)
            ]
            sides_of = [jnp.concatenate(lines[:half], 0), jnp.concatenate(lines[half:], 0)]
            scales[w] = time_step * exact_select(
                jnp.concatenate(sides_of, axis=1),
                halo_picks[w * 2 * halo : (w + 1) * 2 * halo, :],
                1,
            )
        diag = jnp.concatenate(
            [coefs[FACES, pl.ds(first + s, 1), :] for s in range(samples)], axis=0
        )
        for i, (k, _, im) in enumerate(frequencies(total_steps)):
            rate_real, rate_imag = theta_rows(k, total_steps, diag)
            thetas[2 * i] = rate_real
            if im is not None:
                thetas[2 * i + 1] = rate_imag
    local_part(fields, slots, row, picks, blocks, total, high, low)
    for s in range(samples):
        base = s * total_steps
        spectrum = spectra[s // (samples // inner)]
        own = s % (samples // inner) * total_steps
        for k, re, im in frequencies(total_steps):
            shift_real, shift_imag = shift_of(k, total_steps)
            value = fields[base + re]
            kept = spectrum[own + re] - (shift_real * value + time_step * total[base + re])
            if im is not None:
                other = fields[base + im]
                kept = kept + shift_imag * other
                out[base + im] = spectrum[own + im] - (
                    shift_real * other + shift_imag * value + time_step * total[base + im]
                )
            out[base + re] = kept


def sweep_update_kernel(
    flags,
    coefs,
    face_nbr,
    face_blocks,
    halo_picks,
    *rest,
    turn,
    total_steps,
    last,
    parts,
    tables,
):
    even = space_even()
    take = lambda count: (rest[:count], rest[count:])
    currents, rest = take(parts)
    inners, rest = take(parts)
    arrived0, rest = take(parts)
    arrived1, rest = take(parts)
    thetas, rest = take(tables)
    scale_refs, rest = take(tables)
    if last:
        outs, (total, solved) = rest[:total_steps], rest[total_steps:]
    else:
        send_ref, solved, pack0, pack1, total = rest
    fields, dofs, elems = currents[0].shape
    part_samples = fields // total_steps
    samples = parts * part_samples
    table_samples = samples // tables
    first = my_first(samples, 0, 1)
    halo = halo_picks.shape[0] // 4
    usual = sides(even, elems, halo)
    for part in range(parts):
        per = tables // parts
        mine = scale_refs[part * per : (part + 1) * per]
        scales = [jnp.concatenate([ref[w] for ref in mine], axis=0) for w in range(2)]
        half = scales[0].shape[0]
        arrived = (arrived0[part], arrived1[part])
        order = slot_order(part_samples, total_steps, per)
        slots = kept_slots(flags, order, total_steps)
        brought = usual_halo(
            arrived,
            scales,
            [face_blocks[usual[w][0]] for w in range(2)],
            halo_picks[...],
        )
        for t, field in enumerate(slots):
            total[part * fields + field] = (
                inners[part][field] - brought[pair_place(t, half, dofs, elems)]
            )
        add_others(
            arrived,
            even,
            flags,
            face_nbr,
            face_blocks,
            halo,
            half,
            [part * fields + field for field in slots],
            sample_row(coefs, order, first + part * part_samples),
            -time_step,
            total,
        )
    for s in range(samples):
        base = s * total_steps
        current = currents[s // part_samples]
        own = s % part_samples * total_steps
        theta = thetas[s // table_samples]
        line = slice(s % table_samples, s % table_samples + 1)
        for i, (k, re, im) in enumerate(frequencies(total_steps)):
            active = flags[0, 2 + k] > turn + 1
            rate_real = theta[2 * i, line, :]
            value, rest_real = current[own + re], total[base + re]
            change = rate_real * rest_real
            if im is not None:
                rate_imag = theta[2 * i + 1, line, :]
                other, rest_imag = current[own + im], total[base + im]
                change = change - rate_imag * rest_imag
                solved[base + im] = jnp.where(
                    active, other + (rate_real * rest_imag + rate_imag * rest_real), other
                )
            solved[base + re] = jnp.where(active, value + change, value)
    slots = kept_slots(flags, slot_order(samples, total_steps, tables), total_steps)
    if not last:
        pack_fields(solved, even_slots(slots), send_ref[...], (pack0, pack1))
        return
    rank = lax.axis_index("tm")
    for s in range(samples):
        base = s * total_steps
        for n in range(total_steps):
            scale = alpha_circ ** (-n / total_steps) / total_steps
            terms = []
            for k, re, im in frequencies(total_steps):
                c, sn = cos_sin(k, n, total_steps)
                if im is None:
                    terms.append((c, solved[base + re]))
                else:
                    terms += [(2.0 * c, solved[base + re]), (-2.0 * sn, solved[base + im])]
            total[n * samples + s] = scale * weighted(terms)
    for turn_to, out in enumerate(outs):
        step = partner(rank, turn_to, total_steps)
        for s in range(samples):
            out[s] = total[step * samples + s]


def assemble_kernel(*rest, turns, total_steps):
    count = len(turns)
    pieces, (out, done) = rest[:count], rest[-2:]
    size = pieces[0].shape[0]
    rank = lax.axis_index("tm")
    copies = [
        pltpu.make_async_copy(
            piece, out.at[pl.ds(partner(rank, turn, total_steps) * size, size)], done.at[which]
        )
        for which, (turn, piece) in enumerate(zip(turns, pieces))
    ]
    for copy in copies:
        copy.start()
    for copy in copies:
        copy.wait()


vmem = pl.BlockSpec(memory_space=pltpu.VMEM)


def run(
    kernel, inputs, outs, scratch=(), in_hbm=(), out_hbm=(), aliases=(), flops=10**9
):
    def spec(i, outside):
        return pl.BlockSpec(memory_space=pltpu.HBM) if i in outside else vmem

    inputs = [
        pltpu.with_memory_space_constraint(value, pltpu.HBM) if i in in_hbm else value
        for i, value in enumerate(inputs)
    ]
    return pl.pallas_call(
        kernel,
        out_shape=[jax.ShapeDtypeStruct(*o) for o in outs],
        in_specs=[spec(i, in_hbm) for i in range(len(inputs))],
        out_specs=[spec(i, out_hbm) for i in range(len(outs))],
        input_output_aliases=dict(aliases),
        scratch_shapes=[pltpu.VMEM(*s) if isinstance(s, tuple) else s for s in scratch],
        compiler_params=pltpu.CompilerParams(vmem_limit_bytes=40 << 20),
        cost_estimate=pl.CostEstimate(flops=flops, bytes_accessed=1 << 22, transcendentals=0),
    )(*inputs)


def neighbour_swap(value, start):
    axes = ("groups", "tm", "space")
    parts, devs, count = (lax.axis_size(axis) for axis in axes)
    pairs = []
    for part in range(parts):
        for tm in range(devs):
            for space in range(count):
                step = 1 if (space + tm + start) % 2 == 0 else -1
                to_part, to_space = part, space + step
                if not 0 <= to_space < count:
                    to_part, to_space = part ^ 1, space
                if to_part < parts:
                    pairs.append(
                        ((part * devs + tm) * count + space, (to_part * devs + tm) * count + to_space)
                    )
    return lax.ppermute(value, axes, pairs)


def time_swap(value, turn):
    count = lax.axis_size("tm")
    pairs = [(i, int(partner(i, turn, count))) for i in range(count)]
    return value if turn == 0 else lax.ppermute(value, "tm", pairs)


def per_device(
    forcing,
    iterate,
    kappa_mean,
    kappa_modes,
    grad_mats,
    face_mats,
    lattice_shift,
    gen_vector,
    sweep_counts,
    face_nbr,
    halo_send,
):
    samples, steps_dev, dofs, elems = forcing.shape
    halo = halo_send.shape[1]
    devs = lax.axis_size("tm")
    total_steps = steps_dev * devs
    part = samples // devs
    half = samples // 2
    cube = (samples, dofs, elems)
    forcing = forcing.reshape(cube)
    iterate = iterate.reshape(cube)
    onward = [(i, (i + 1) % devs) for i in range(devs)]
    rows = half * dofs
    copies = 2 * (half // group_size(half))
    (
        pack0, pack1, send, conduct, low, high, face_nbr, grad_mats, face_mats, counts_line
    ) = run(
        prepare_kernel,
        (
            iterate,
            halo_send,
            lattice_shift.reshape(1, -1),
            gen_vector.reshape(1, -1),
            kappa_mean.reshape(1, -1),
            kappa_modes,
            face_nbr,
            grad_mats,
            face_mats,
            sweep_counts.reshape(1, -1),
        ),
        [
            ((rows + half, 2 * halo), f32),
            ((rows + half, 2 * halo), f32),
            ((2 * elems, 4 * halo), bf16),
            ((samples, elems), f32),
            ((half, dofs, elems), f32),
            ((half, dofs, elems), f32),
            (face_nbr.shape, i32),
            (grad_mats.shape, f32),
            (face_mats.shape, f32),
            ((1, sweep_counts.shape[0]), i32),
        ],
        [
            (halo_send.shape, i32),
            ((1, lattice_shift.shape[0]), f32),
            ((1, gen_vector.shape[0]), i32),
            ((1, elems), f32),
            (kappa_modes.shape, f32),
            pltpu.SemaphoreType.DMA((5,)),
            pltpu.SemaphoreType.DMA((copies,)),
            pltpu.SemaphoreType.DMA((4,)),
        ],
        in_hbm=range(10),
    )
    arrived0 = neighbour_swap(pack0, 0)
    arrived1 = neighbour_swap(pack1, 1)
    earlier_high = lax.ppermute(high, "tm", onward)
    if two_chips(devs):
        earlier_low = time_swap(low, 1)
    else:
        earlier_low = lax.ppermute(low, "tm", onward)
    blocks_wide = (FACES + 1) * dofs
    splits = lambda count: [((count, blocks_wide, elems), bf16)] * 2
    (
        local, coefs, picks, blocks, face_blocks, halo_picks, flags, facing
    ) = run(
        first_local_kernel,
        (low, high, conduct, face_nbr, grad_mats, face_mats, counts_line),
        [
            (cube, f32),
            ((FACES + 2, samples, elems), f32),
            ((elems, FACES * elems), bf16),
            ((2 * dofs, blocks_wide), bf16),
            ((FACES, 2 * dofs, dofs), bf16),
            ((4 * halo, 2 * elems), bf16),
            ((1, 2 * halo), i32),
            ((2, half, 2 * halo), f32),
        ],
        splits(samples) + [((blocks_wide, 2 * dofs), f32)],
        flops=4 * 10**9,
    )
    groups = GROUPS
    if part % groups or (part // groups * (total_steps - 1)) % 2:
        groups = 1
    share = part // groups
    piece = ((share, dofs, elems), f32)
    *scaled, coefs = run(
        functools.partial(residual_kernel, total_steps=total_steps, groups=groups),
        (
            forcing,
            low,
            high,
            earlier_low,
            earlier_high,
            local,
            arrived0,
            arrived1,
            coefs,
            face_nbr,
            blocks,
            face_blocks,
            halo_picks,
            facing,
            flags,
        ),
        [piece] * (groups * devs) + [((FACES + 2, samples, elems), f32)],
        [(cube, f32), ((samples, elems), f32)],
    )
    sizes = lambda share: (
        ((share * total_steps, dofs, elems), f32),
        (((share * (total_steps - 1) + 1) // 2 * dofs, 2 * halo), f32),
        (share * (total_steps - 1) + 1) // 2,
    )
    some, packed, pairs = sizes(share)
    currents, spectra, inners, arrived0, arrived1, thetas, scales = ([] for _ in range(7))
    for at in range(groups):
        mine = dict(total_steps=total_steps, at=at, groups=groups)
        pieces = [time_swap(scaled[at * devs + turn], turn) for turn in range(devs)]
        spectrum, current, pack0, pack1 = run(
            functools.partial(spectrum_kernel, **mine),
            (flags, coefs, send, low, earlier_low, *pieces, *thetas[-1:]),
            [some, some, packed, packed],
            [((total_steps, share, dofs, elems), f32)],
        )
        arrived0.append(neighbour_swap(pack0, 0))
        arrived1.append(neighbour_swap(pack1, 1))
        inner, theta, scale = run(
            functools.partial(sweep_local_kernel, first_turn=True, inner=1, **mine),
            (flags, current, coefs, picks, blocks, halo_picks, spectrum),
            [
                some,
                ((2 * len(frequencies(total_steps)), share, elems), f32),
                ((2, pairs, 2 * halo), f32),
            ],
            [some] + splits(share * (total_steps - 1)),
            flops=3 * 10**9 // groups,
        )
        currents.append(current)
        spectra.append(spectrum)
        inners.append(inner)
        thetas.append(theta)
        scales.append(scale)
    some, packed, pairs = sizes(part)
    tables = (flags, coefs, face_nbr, face_blocks, halo_picks)
    update = lambda turn, parts: functools.partial(
        sweep_update_kernel,
        turn=turn,
        total_steps=total_steps,
        last=turn == MAXS - 2,
        parts=parts,
        tables=groups,
    )
    current, pack0, pack1 = run(
        update(0, groups),
        (*tables, *currents, *inners, *arrived0, *arrived1, *thetas, *scales, send),
        [some, packed, packed],
        [some],
    )
    arrived0 = neighbour_swap(pack0, 0)
    arrived1 = neighbour_swap(pack1, 1)
    (inner,) = run(
        functools.partial(
            sweep_local_kernel,
            first_turn=False,
            inner=groups,
            total_steps=total_steps,
            at=0,
            groups=1,
        ),
        (flags, current, coefs, picks, blocks, halo_picks, *spectra),
        [some],
        [some] + splits(part * (total_steps - 1)),
        flops=3 * 10**9,
    )
    series = run(
        update(1, 1),
        (*tables, current, inner, arrived0, arrived1, *thetas, *scales),
        [((part, dofs, elems), f32)] * devs,
        [some, some],
    )
    restored = [time_swap(series[turn], turn) for turn in range(devs)]
    out = None
    for turns in (range(devs - 1), range(devs - 1, devs)):
        inputs = [restored[turn] for turn in turns] + ([] if out is None else [out])
        (out,) = run(
            functools.partial(assemble_kernel, turns=turns, total_steps=total_steps),
            tuple(inputs),
            [(cube, f32)],
            [pltpu.SemaphoreType.DMA((len(turns),))],
            in_hbm=() if out is None else (len(turns),),
            out_hbm=(0,),
            aliases=() if out is None else ((len(turns), 0),),
        )
    return out.reshape(samples, steps_dev, dofs, elems)


def solution(mesh):
    placed = (
        P("groups", "tm", None, "space"),
        P("groups", "tm", None, "space"),
        P("space"),
        P(None, "space"),
        P(),
        P(),
        P("groups"),
        P(),
        P(),
        P(None, "space"),
        P(None, "space"),
    )
    return jax.shard_map(
        per_device,
        mesh=mesh,
        in_specs=placed,
        out_specs=P("groups", "tm", None, "space"),
        check_vma=False,
    )
```

```python
import functools
import math

import jax
import jax.numpy as jnp
from jax import lax
from jax.experimental import pallas as pl
from jax.experimental.pallas import tpu as pltpu
from jax.sharding import PartitionSpec as P

MAXS = 3
alpha_circ = 0.05
time_step = 0.1
relax_rho = 2.3
highest = lax.Precision.HIGHEST
f32, bf16, i32 = jnp.float32, jnp.bfloat16, jnp.int32
FACES = 6
GROUPS = 2


def dot(a, b):
    return jnp.dot(a, b, preferred_element_type=f32)


def split(x):
    hi = x.astype(bf16)
    return hi, (x - hi.astype(f32)).astype(bf16)


def exact_select(x, onehot, across=0):
    a, b = split(x)
    c = (x - a.astype(f32) - b.astype(f32)).astype(bf16)
    times = lambda v: lax.dot_general(
        v, onehot, (((1,), (across,)), ((), ())), preferred_element_type=f32
    )
    return times(a) + (times(b) + times(c))


def times_block(stacked, x):
    rows = stacked.shape[0] // 2
    hi, lo = split(x)
    both = dot(stacked, hi)
    return both[:rows] + (both[rows:] + dot(stacked[:rows], lo))


def rows_iota(shape):
    return lax.broadcasted_iota(i32, shape, 0)


def halo_onehot(nbr_row, base, halo):
    elems = nbr_row.shape[1]
    entry = nbr_row - base
    here = (entry >= 0) & (entry < halo)
    entry = jnp.where(here, entry, -2 * halo)
    row = rows_iota((2 * halo, elems))
    left = (row == entry).astype(f32).astype(bf16)
    right = (row == entry + halo).astype(f32).astype(bf16)
    return jnp.concatenate([left, right], axis=1)


def space_even():
    return lax.rem(lax.axis_index("space") + lax.axis_index("tm"), 2) == 0


def sides(even, elems, halo):
    below, above = elems, elems + halo
    return (
        (jnp.where(even, 5, 4), jnp.where(even, above, below)),
        (jnp.where(even, 4, 5), jnp.where(even, below, above)),
    )


def group_size(count):
    return next(size for size in (4, 3, 2, 1) if count % size == 0)


def pack_group(ref, left, right, send, first, outs):
    dofs = ref.shape[1]
    width = send.shape[1] // 2
    sides_by_side = [jnp.concatenate([ref[i] for i in side], axis=0) for side in (left, right)]
    hi, lo = split(jnp.concatenate(sides_by_side, axis=1))
    got = dot(hi, send) + dot(lo, send)
    rows = slice(first * dofs, (first + len(left)) * dofs)
    for which, out in enumerate(outs):
        out[rows, :] = got[:, which * width : (which + 1) * width]


def pack_fields(ref, fields, send, outs):
    half = len(fields) // 2
    size = group_size(half)
    for j in range(0, half, size):
        pack_group(
            ref, fields[j : j + size], fields[half + j : half + j + size], send, j, outs
        )


def prepare_kernel(
    iterate_in,
    halo_send_in,
    shift_in,
    gen_in,
    mean_in,
    modes_in,
    nbr_in,
    grads_in,
    face_mats_in,
    counts_in,
    pack0,
    pack1,
    send_out,
    conduct_out,
    low,
    high,
    nbr,
    grads,
    face_mats,
    counts,
    halo_send,
    shift,
    gen,
    mean,
    modes,
    small_done,
    field_done,
    later_done,
):
    iterate = Halves(low, high)
    samples, dofs, elems = iterate.shape
    halo = halo_send.shape[1]
    half = samples // 2
    size = group_size(half)
    small = [
        pltpu.make_async_copy(source, target, small_done.at[i])
        for i, (source, target) in enumerate(
            (
                (halo_send_in, halo_send),
                (shift_in, shift),
                (gen_in, gen),
                (mean_in, mean),
                (modes_in, modes),
            )
        )
    ]
    large = []
    for j in range(0, half, size):
        for at, side in ((j, low), (half + j, high)):
            large.append(
                pltpu.make_async_copy(
                    iterate_in.at[pl.ds(at, size)],
                    side.at[pl.ds(j, size)],
                    field_done.at[len(large)],
                )
            )
    later = [
        pltpu.make_async_copy(source, target, later_done.at[i])
        for i, (source, target) in enumerate(
            ((nbr_in, nbr), (grads_in, grads), (face_mats_in, face_mats), (counts_in, counts))
        )
    ]
    for copy in small + large + later:
        copy.start()
    for copy in small + large:
        copy.wait()
    even = space_even()
    down = jnp.concatenate([halo_send[0:1, :]] * 2, axis=1)
    up = jnp.concatenate([halo_send[1:2, :]] * 2, axis=1)
    lane = lax.broadcasted_iota(i32, (1, 2 * halo), 1)
    row = rows_iota((2 * elems, 2 * halo))
    for which in range(2):
        ids = jnp.where(even == (which == 0), up, down)
        ids = jnp.where(lane < halo, ids, ids + elems)
        send_out[:, which * 2 * halo : (which + 1) * 2 * halo] = (
            (row == ids).astype(f32).astype(bf16)
        )
    position = rows_iota((samples, gen.shape[1]))
    residue = lax.rem(position * gen[...], samples)
    shifted = residue.astype(f32) / samples + shift[...]
    fraction = shifted - jnp.floor(shifted)
    points = 0.5 - jnp.abs(2.0 * fraction - 1.0)
    conduct = mean[...] * (
        1.0 + jnp.dot(points, modes[...], precision=highest, preferred_element_type=f32)
    )
    conduct_out[...] = conduct
    send = send_out[...]
    got = exact_select(jnp.concatenate([conduct[:half], conduct[half:]], axis=1), send)
    pack0[half * dofs :, :] = got[:, : 2 * halo]
    pack1[half * dofs :, :] = got[:, 2 * halo :]
    for j in range(0, half, size):
        left = list(range(j, j + size))
        pack_group(iterate, left, [half + i for i in left], send, j, (pack0, pack1))
    for copy in later:
        copy.wait()


def local_part(read, slots, coef_row, picks, blocks, out, high, low):
    dofs, elems = out.shape[1], out.shape[2]
    size = group_size(len(slots))
    for first in range(0, len(slots), size):
        group = range(first, first + size)
        values = [read(t) for t in group]
        hi, lo = split(jnp.concatenate(values, axis=0))
        for t, value in zip(group, values):
            a, b = split(value * coef_row(FACES, t))
            high[t, 0:dofs, :] = a
            low[t, 0:dofs, :] = b
        for f in range(FACES):
            pick = picks[:, f * elems : (f + 1) * elems]
            got = dot(hi, pick) + dot(lo, pick)
            at = (f + 1) * dofs
            for i, t in enumerate(group):
                a, b = split(got[i * dofs : (i + 1) * dofs] * coef_row(f, t))
                high[t, at : at + dofs, :] = a
                low[t, at : at + dofs, :] = b
        stacked = blocks[...]
        for t in group:
            both = dot(stacked, high[t])
            out[slots[t]] = both[:dofs] + (both[dofs:] + dot(stacked[:dofs], low[t]))


def first_local_kernel(
    low_fields,
    high_fields,
    conduct_ref,
    face_nbr,
    grads,
    face_mats,
    counts_in,
    out,
    coefs,
    picks,
    blocks,
    face_blocks,
    halo_picks,
    flags,
    facing,
    high,
    low,
    wide,
):
    iterate = Halves(low_fields, high_fields)
    samples, dofs, elems = iterate.shape
    halo = halo_picks.shape[0] // 4
    even = space_even()
    row = rows_iota((elems, elems))
    for f in range(FACES):
        picks[:, f * elems : (f + 1) * elems] = (
            (row == face_nbr[f : f + 1, :]).astype(f32).astype(bf16)
        )
    conduct = conduct_ref[...]
    diag = conduct
    for f in range(FACES):
        nbr = face_nbr[f : f + 1, :]
        across = exact_select(conduct, picks[:, f * elems : (f + 1) * elems])
        inside = (nbr >= 0) & (nbr < elems)
        coupling = jnp.where(inside, 0.5 * (conduct + across), 0.0)
        coefs[f] = coupling
        diag = diag + jnp.where(nbr < 0, conduct, coupling)
    coefs[FACES] = diag
    coefs[FACES + 1] = conduct
    volume = (rows_iota((dofs, dofs)) == lax.broadcasted_iota(i32, (dofs, dofs), 1)).astype(f32)
    for d in range(grads.shape[0]):
        volume = volume + lax.dot_general(
            grads[d], grads[d], (((0,), (0,)), ((), ())), precision=highest,
            preferred_element_type=f32,
        )
    wide[...] = jnp.zeros(wide.shape, f32)
    wide[0:dofs, 0:dofs] = volume
    for f in range(FACES):
        block = face_mats[f // 2]
        at = (f + 1) * dofs
        wide[at : at + dofs, 0:dofs] = block if f % 2 == 0 else block.T
    turned = wide[...].T[:dofs, :]
    hi, lo = split(turned)
    blocks[0:dofs, :] = hi
    blocks[dofs:, :] = lo
    for f in range(FACES):
        block = face_mats[f // 2]
        hi, lo = split(block.T if f % 2 == 0 else block)
        face_blocks[f, 0:dofs, :] = hi
        face_blocks[f, dofs:, :] = lo
    for which, (face, base) in enumerate(sides(even, elems, halo)):
        nbr = jnp.where(face == 4, face_nbr[4:5, :], face_nbr[5:6, :])
        pick = halo_onehot(nbr, base, halo)
        halo_picks[which * 2 * halo : (which + 1) * 2 * halo, :] = pick
        facing[which] = exact_select(side_by_side(conduct), pick, 1)
    crossing = jnp.max(jnp.where(face_nbr[0:4, :] >= elems, 1, 0))
    crossing = crossing + jnp.max(jnp.where(face_nbr[4:5, :] >= elems + halo, 1, 0))
    fifth = face_nbr[5:6, :]
    crossing = crossing + jnp.max(
        jnp.where((fifth >= elems) & (fifth < elems + halo), 1, 0)
    )
    lane = lax.broadcasted_iota(i32, flags.shape, 1)
    line = jnp.where(lane == 0, crossing, 0)
    skip = jnp.int32(0)
    for k in range(counts_in.shape[1]):
        line = jnp.where(lane == 2 + k, counts_in[0, k], line)
    for k, re, _ in frequencies(counts_in.shape[1]):
        skip = jnp.where(counts_in[0, k] == 1, re, skip)
    flags[...] = jnp.where(lane == 1, skip, line)
    local_part(
        lambda t: iterate[t],
        list(range(samples)),
        lambda f, t: coefs[f, t : t + 1, :],
        picks,
        blocks,
        out,
        high,
        low,
    )


def side_by_side(x):
    half = x.shape[0] // 2
    return jnp.concatenate([x[:half], x[half:]], axis=1)


def stacked_halves(x):
    width = x.shape[1] // 2
    return jnp.concatenate([x[:, :width], x[:, width:]], axis=0)


def usual_halo(arrived, scales, blocks, picks, chosen=None):
    dofs = blocks[0].shape[1]
    columns = []
    for which in range(2):
        value = arrived[which]
        width = value.shape[1]
        chosen = range(scales[which].shape[0]) if chosen is None else chosen
        pairs = len(chosen)
        scaled = [
            value[j * dofs : (j + 1) * dofs, :] * scales[which][j : j + 1, :] for j in chosen
        ]
        got = times_block(blocks[which], jnp.concatenate(scaled, axis=1))
        columns.append(
            jnp.concatenate([got[:, j * width : (j + 1) * width] for j in range(pairs)], axis=0)
        )
    hi, lo = split(jnp.concatenate(columns, axis=1))
    return dot(hi, picks) + dot(lo, picks)


class Halves:
    def __init__(self, low, high):
        self.low, self.high = low, high
        self.shape = (2 * low.shape[0],) + tuple(low.shape[1:])

    def __getitem__(self, at):
        half = self.low.shape[0]
        return self.low[at] if at < half else self.high[at - half]


def other_halo(arrived, block, pick):
    dofs = block.shape[1]
    hi, lo = split(times_block(block, arrived))
    got = dot(hi, pick) + dot(lo, pick)
    return got


def other_sides(flags, even, face_nbr, halo, body):
    elems = face_nbr.shape[1]

    @pl.when(flags[0, 0] > 0)
    def _():
        for which, (usual, base) in enumerate(sides(even, elems, halo)):

            def step(face, carry, which=which, usual=usual, base=base):
                @pl.when(face != usual)
                def _():
                    body(which, face, halo_onehot(face_nbr[pl.ds(face, 1), :], base, halo))

                return carry

            lax.fori_loop(0, FACES, step, 0)


def pair_place(t, half, dofs, elems):
    row, col = t % half * dofs, t // half * elems
    return slice(row, row + dofs), slice(col, col + elems)


def add_others(arrived, even, flags, face_nbr, face_blocks, halo, chosen, slots, coef_row, factor, total):
    elems = face_nbr.shape[1]
    dofs = total.shape[1]

    def body(which, face, pick):
        block = face_blocks[face]
        half = len(chosen)
        for i, j in enumerate(chosen):
            got = other_halo(arrived[which][j * dofs : (j + 1) * dofs, :], block, pick)
            for t in (i, half + i):
                if t < len(slots):
                    cols = slice(t // half * elems, (t // half + 1) * elems)
                    field = slots[t]
                    total[field] = total[field] + factor * coef_row(face, t) * got[:, cols]

    other_sides(flags, even, face_nbr, halo, body)


def residual_kernel(
    forcing,
    low_fields,
    high_fields,
    earlier_low,
    earlier_high,
    local,
    arrived0,
    arrived1,
    coefs_in,
    face_nbr,
    blocks,
    face_blocks,
    halo_picks,
    facing,
    flags,
    *rest,
    total_steps,
    groups,
    at,
):
    samples, dofs, elems = forcing.shape
    if at == 0:
        outs, (coefs, extra, total) = rest[:total_steps], rest[total_steps:]
    else:
        extra, outs, total = rest[0], rest[1 : total_steps + 1], rest[-1]
        coefs = coefs_in
    iterate = Halves(low_fields, high_fields)
    halo = halo_picks.shape[0] // 4
    half = samples // 2
    part = samples // total_steps
    size = part // groups
    chosen = [j for j in range(half) if j % part // size == at]
    mine = chosen + [half + j for j in chosen]
    even = space_even()
    usual = sides(even, elems, halo)
    arrived = (arrived0, arrived1)
    scales = [0.5 * (facing[w] + arrived[w][half * dofs :, :]) for w in range(2)]
    if at == 0:
        coefs[...] = coefs_in[...]
        conduct = coefs_in[FACES + 1]
        couplings = [
            stacked_halves(
                exact_select(scales[w], halo_picks[w * 2 * halo : (w + 1) * 2 * halo, :])
            )
            for w in range(2)
        ]
        extra[...] = couplings[0] + couplings[1]
        for w in range(2):
            coefs[usual[w][0]] = coefs[usual[w][0]] + couplings[w]

        def add_coupling(which, face, pick):
            got = exact_select(arrived[which][half * dofs :, :], pick)
            nbr = face_nbr[pl.ds(face, 1), :]
            base = usual[which][1]
            here = (nbr >= base) & (nbr < base + halo)
            coupling = jnp.where(here, 0.5 * (conduct + stacked_halves(got)), 0.0)
            coefs[face] = coefs[face] + coupling
            extra[...] = extra[...] + coupling

        other_sides(flags, even, face_nbr, halo, add_coupling)
        coefs[FACES] = coefs[FACES] + extra[...]
    volume = blocks[:, 0 : 2 * dofs][:, :dofs]
    brought = usual_halo(
        arrived,
        scales,
        [face_blocks[usual[w][0]] for w in range(2)],
        halo_picks[...],
        chosen,
    )
    for t, j in enumerate(mine):
        value = iterate[j]
        total[j] = value + time_step * (
            local[j]
            + brought[pair_place(t, len(chosen), dofs, elems)]
            + times_block(volume, value * extra[j : j + 1, :])
        )
    add_others(
        arrived,
        even,
        flags,
        face_nbr,
        face_blocks,
        halo,
        chosen,
        mine,
        lambda f, t: coefs[f, mine[t] : mine[t] + 1, :],
        time_step,
        total,
    )
    step = lax.axis_index("tm")
    weight = jnp.float32(0.0)
    for n in range(total_steps):
        weight = jnp.where(step == n, jnp.float32(alpha_circ ** (n / total_steps)), weight)
    gate_high = jnp.where(step > 0, weight, 0.0)
    gate_low = jnp.where(step % 2 == 1, weight, 0.0) if two_chips(total_steps) else gate_high
    for turn, out in enumerate(outs):
        first = (partner(step, turn, total_steps) * groups + at) * size
        for i in range(size):
            j = first + i
            inner = forcing[j] - total[j]
            before = lax.rem(j, half)
            late = j >= half
            earlier = jnp.where(late, earlier_high[before], earlier_low[before])
            out[i] = weight * inner + jnp.where(late, gate_high, gate_low) * earlier


def two_chips(devs):
    return devs == 4


def partner(rank, turn, count):
    if count & (count - 1) == 0:
        return rank ^ turn
    return lax.rem(turn + count - rank, count)


def real_fields(total_steps):
    order = [(0, False)]
    if total_steps % 2 == 0:
        order.append((total_steps // 2, False))
    for k in range(1, (total_steps + 1) // 2):
        order += [(k, False), (k, True)]
    return order


def cos_sin(k, n, total_steps):
    turn = 2.0 * math.pi * ((k * n) % total_steps) / total_steps
    c, s = math.cos(turn), math.sin(turn)
    snap = lambda v: float(round(v)) if abs(v - round(v)) < 1e-12 else v
    return snap(c), snap(s)


def weighted(terms):
    total = None
    for constant, value in terms:
        if constant == 0.0:
            continue
        if total is None:
            total = value if constant == 1.0 else constant * value
        elif constant == 1.0:
            total = total + value
        elif constant == -1.0:
            total = total - value
        else:
            total = total + constant * value
    return total


def shift_of(k, total_steps):
    magnitude = alpha_circ ** (1.0 / total_steps)
    c, s = cos_sin(k, 1, total_steps)
    return 1.0 - magnitude * c, magnitude * s


def theta_rows(k, total_steps, diag):
    shift_real, shift_imag = shift_of(k, total_steps)
    denom = shift_real + (time_step * relax_rho) * diag
    if shift_imag == 0.0:
        return 1.0 / denom, None
    modulus = denom * denom + shift_imag * shift_imag
    return denom / modulus, -shift_imag / modulus


def frequencies(total_steps):
    order = real_fields(total_steps)
    return [
        (k, at, order.index((k, True)) if (k, True) in order else None)
        for at, (k, imag) in enumerate(order)
        if not imag
    ]


def slot_order(samples, total_steps, inner):
    size = samples // inner
    lists = [
        [(g * size + s, i) for s in range(size) for i in range(total_steps - 1)]
        for g in range(inner)
    ]
    if inner == 1:
        return lists[0]
    middle = len(lists[0]) // 2
    return [pair for part in lists for pair in part[:middle]] + [
        pair for part in lists for pair in part[middle:]
    ]


def kept_slots(flags, order, total_steps):
    skip = flags[0, 1]
    return [s * total_steps + jnp.where(skip <= i, i + 1, i) for s, i in order]


def even_slots(slots):
    return slots + slots[: len(slots) % 2]


def my_first(samples, at, groups):
    return (lax.axis_index("tm") * groups + at) * samples


def sample_row(coefs, order, first):
    return lambda f, t: coefs[f, pl.ds(first + order[t][0], 1), :]


def spectrum_kernel(
    flags, coefs, send_ref, own, near, *rest, total_steps, at, groups
):
    arrived, (spectrum, first_w, pack0, pack1, pieces) = rest[:total_steps], rest[-5:]
    samples = arrived[0].shape[0]
    first = my_first(samples, at, groups)
    rank = lax.axis_index("tm")
    for turn, piece in enumerate(arrived):
        pieces[partner(rank, turn, total_steps)] = piece[...]
    if two_chips(total_steps):
        here = at * samples
        there = groups * samples + here
        gate = jnp.where(rank < 2, jnp.float32(alpha_circ ** (2 / total_steps)), 0.0)
        for s in range(samples):
            before = jnp.where(rank == 0, near[here + s], own[there + s])
            pieces[2, s] = pieces[2, s] + gate * before
    for s in range(samples):
        diag = coefs[FACES, pl.ds(first + s, 1), :]
        base = s * total_steps
        for k, re, im in frequencies(total_steps):
            tables = [cos_sin(k, n, total_steps) for n in range(total_steps)]
            real = weighted([(tables[n][0], pieces[n, s]) for n in range(total_steps)])
            rate_real, rate_imag = theta_rows(k, total_steps, diag)
            spectrum[base + re] = real
            if im is None:
                first_w[base + re] = rate_real * real
            else:
                imag = weighted([(-tables[n][1], pieces[n, s]) for n in range(total_steps)])
                spectrum[base + im] = imag
                first_w[base + re] = rate_real * real - rate_imag * imag
                first_w[base + im] = rate_real * imag + rate_imag * real
    slots = kept_slots(flags, slot_order(samples, total_steps, 1), total_steps)
    pack_fields(first_w, even_slots(slots), send_ref[...], (pack0, pack1))


def sweep_local_kernel(
    flags,
    coefs,
    picks,
    blocks,
    halo_picks,
    *rest,
    total_steps,
    at,
    groups,
    first_turn,
    inner,
):
    fields, spectra, rest = rest[:inner], rest[inner : 2 * inner], rest[2 * inner :]
    if first_turn:
        out, thetas, scales, total, high, low = rest
    else:
        out, total, high, low = rest
    elems = fields[0].shape[2]
    each = fields[0].shape[0] // total_steps
    samples = inner * each
    first = my_first(samples, at, groups)
    order = slot_order(samples, total_steps, inner)
    slots = kept_slots(flags, order, total_steps)
    row = sample_row(coefs, order, first)
    if first_turn:
        halo = halo_picks.shape[0] // 4
        half = scales.shape[1]
        usual = sides(space_even(), elems, halo)
        count = len(slots)
        for w in range(2):
            lines = [
                row(usual[w][0], t if t < count else 0) for t in range(2 * half)
            ]
            sides_of = [jnp.concatenate(lines[:half], 0), jnp.concatenate(lines[half:], 0)]
            scales[w] = time_step * exact_select(
                jnp.concatenate(sides_of, axis=1),
                halo_picks[w * 2 * halo : (w + 1) * 2 * halo, :],
                1,
            )
        diag = jnp.concatenate(
            [coefs[FACES, pl.ds(first + s, 1), :] for s in range(samples)], axis=0
        )
        for i, (k, _, im) in enumerate(frequencies(total_steps)):
            rate_real, rate_imag = theta_rows(k, total_steps, diag)
            thetas[2 * i] = rate_real
            if im is not None:
                thetas[2 * i + 1] = rate_imag

    def read(t):
        which = order[t][0] // each
        return fields[which][slots[t] - which * each * total_steps]

    local_part(read, slots, row, picks, blocks, total, high, low)
    for s in range(samples):
        base = s * total_steps
        spectrum, current = spectra[s // each], fields[s // each]
        own = s % each * total_steps
        for k, re, im in frequencies(total_steps):
            shift_real, shift_imag = shift_of(k, total_steps)
            value = current[own + re]
            kept = spectrum[own + re] - (shift_real * value + time_step * total[base + re])
            if im is not None:
                other = current[own + im]
                kept = kept + shift_imag * other
                out[base + im] = spectrum[own + im] - (
                    shift_real * other + shift_imag * value + time_step * total[base + im]
                )
            out[base + re] = kept


def sweep_update_kernel(
    flags,
    coefs,
    face_nbr,
    face_blocks,
    halo_picks,
    *rest,
    turn,
    total_steps,
    last,
    sources,
    at,
    groups,
):
    even = space_even()
    take = lambda count: (rest[:count], rest[count:])
    (inner, arrived0, arrived1), rest = take(3)
    currents, rest = take(sources)
    thetas, rest = take(sources)
    scale_refs, rest = take(sources)
    if last:
        outs, (total, solved) = rest[:total_steps], rest[total_steps:]
    else:
        send_ref, *before, solved, pack0, pack1, total = rest
    fields, dofs, elems = inner.shape
    samples = fields // total_steps
    each = samples // sources
    first = my_first(samples, at, groups)
    halo = halo_picks.shape[0] // 4
    usual = sides(even, elems, halo)
    scales = [jnp.concatenate([ref[w] for ref in scale_refs], axis=0) for w in range(2)]
    half = scales[0].shape[0]
    arrived = (arrived0, arrived1)
    order = slot_order(samples, total_steps, sources)
    slots = kept_slots(flags, order, total_steps)
    brought = usual_halo(
        arrived,
        scales,
        [face_blocks[usual[w][0]] for w in range(2)],
        halo_picks[...],
    )
    for t, field in enumerate(slots):
        total[field] = inner[field] - brought[pair_place(t, half, dofs, elems)]
    add_others(
        arrived,
        even,
        flags,
        face_nbr,
        face_blocks,
        halo,
        range(half),
        slots,
        sample_row(coefs, order, first),
        -time_step,
        total,
    )
    for s in range(samples):
        base = s * total_steps
        current, theta = currents[s // each], thetas[s // each]
        own = s % each * total_steps
        line = slice(s % each, s % each + 1)
        for i, (k, re, im) in enumerate(frequencies(total_steps)):
            active = flags[0, 2 + k] > turn + 1
            rate_real = theta[2 * i, line, :]
            value, rest_real = current[own + re], total[base + re]
            change = rate_real * rest_real
            if im is not None:
                rate_imag = theta[2 * i + 1, line, :]
                other, rest_imag = current[own + im], total[base + im]
                change = change - rate_imag * rest_imag
                solved[base + im] = jnp.where(
                    active, other + (rate_real * rest_imag + rate_imag * rest_real), other
                )
            solved[base + re] = jnp.where(active, value + change, value)
    if not last:
        rows = half * dofs
        start = at * rows if before else 0
        for ref, out in zip(before, (pack0, pack1)):
            out[:start, :] = ref[...]
        pack_fields(
            solved,
            even_slots(slots),
            send_ref[...],
            [out.at[start : start + rows] for out in (pack0, pack1)],
        )
        return
    rank = lax.axis_index("tm")
    for s in range(samples):
        base = s * total_steps
        for n in range(total_steps):
            scale = alpha_circ ** (-n / total_steps) / total_steps
            terms = []
            for k, re, im in frequencies(total_steps):
                c, sn = cos_sin(k, n, total_steps)
                if im is None:
                    terms.append((c, solved[base + re]))
                else:
                    terms += [(2.0 * c, solved[base + re]), (-2.0 * sn, solved[base + im])]
            total[n * samples + s] = scale * weighted(terms)
    for turn_to, out in enumerate(outs):
        step = partner(rank, turn_to, total_steps)
        for s in range(samples):
            out[s] = total[step * samples + s]


def assemble_kernel(*rest, turns, total_steps):
    count = len(turns)
    pieces, (out, done) = rest[:count], rest[-2:]
    size = pieces[0].shape[0]
    rank = lax.axis_index("tm")
    copies = [
        pltpu.make_async_copy(
            piece, out.at[pl.ds(partner(rank, turn, total_steps) * size, size)], done.at[which]
        )
        for which, (turn, piece) in enumerate(zip(turns, pieces))
    ]
    for copy in copies:
        copy.start()
    for copy in copies:
        copy.wait()


vmem = pl.BlockSpec(memory_space=pltpu.VMEM)


def run(
    kernel, inputs, outs, scratch=(), in_hbm=(), out_hbm=(), aliases=(), flops=10**9
):
    def spec(i, outside):
        return pl.BlockSpec(memory_space=pltpu.HBM) if i in outside else vmem

    inputs = [
        pltpu.with_memory_space_constraint(value, pltpu.HBM) if i in in_hbm else value
        for i, value in enumerate(inputs)
    ]
    return pl.pallas_call(
        kernel,
        out_shape=[jax.ShapeDtypeStruct(*o) for o in outs],
        in_specs=[spec(i, in_hbm) for i in range(len(inputs))],
        out_specs=[spec(i, out_hbm) for i in range(len(outs))],
        input_output_aliases=dict(aliases),
        scratch_shapes=[pltpu.VMEM(*s) if isinstance(s, tuple) else s for s in scratch],
        compiler_params=pltpu.CompilerParams(vmem_limit_bytes=40 << 20),
        cost_estimate=pl.CostEstimate(flops=flops, bytes_accessed=1 << 22, transcendentals=0),
    )(*inputs)


def neighbour_swap(value, start):
    axes = ("groups", "tm", "space")
    parts, devs, count = (lax.axis_size(axis) for axis in axes)
    pairs = []
    for part in range(parts):
        for tm in range(devs):
            for space in range(count):
                step = 1 if (space + tm + start) % 2 == 0 else -1
                to_part, to_space = part, space + step
                if not 0 <= to_space < count:
                    to_part, to_space = part ^ 1, space
                if to_part < parts:
                    pairs.append(
                        ((part * devs + tm) * count + space, (to_part * devs + tm) * count + to_space)
                    )
    return lax.ppermute(value, axes, pairs)


def time_swap(value, turn):
    count = lax.axis_size("tm")
    pairs = [(i, int(partner(i, turn, count))) for i in range(count)]
    return value if turn == 0 else lax.ppermute(value, "tm", pairs)


def per_device(
    forcing,
    iterate,
    kappa_mean,
    kappa_modes,
    grad_mats,
    face_mats,
    lattice_shift,
    gen_vector,
    sweep_counts,
    face_nbr,
    halo_send,
):
    samples, steps_dev, dofs, elems = forcing.shape
    halo = halo_send.shape[1]
    devs = lax.axis_size("tm")
    total_steps = steps_dev * devs
    part = samples // devs
    half = samples // 2
    cube = (samples, dofs, elems)
    forcing = forcing.reshape(cube)
    iterate = iterate.reshape(cube)
    onward = [(i, (i + 1) % devs) for i in range(devs)]
    rows = half * dofs
    copies = 2 * (half // group_size(half))
    (
        pack0, pack1, send, conduct, low, high, face_nbr, grad_mats, face_mats, counts_line
    ) = run(
        prepare_kernel,
        (
            iterate,
            halo_send,
            lattice_shift.reshape(1, -1),
            gen_vector.reshape(1, -1),
            kappa_mean.reshape(1, -1),
            kappa_modes,
            face_nbr,
            grad_mats,
            face_mats,
            sweep_counts.reshape(1, -1),
        ),
        [
            ((rows + half, 2 * halo), f32),
            ((rows + half, 2 * halo), f32),
            ((2 * elems, 4 * halo), bf16),
            ((samples, elems), f32),
            ((half, dofs, elems), f32),
            ((half, dofs, elems), f32),
            (face_nbr.shape, i32),
            (grad_mats.shape, f32),
            (face_mats.shape, f32),
            ((1, sweep_counts.shape[0]), i32),
        ],
        [
            (halo_send.shape, i32),
            ((1, lattice_shift.shape[0]), f32),
            ((1, gen_vector.shape[0]), i32),
            ((1, elems), f32),
            (kappa_modes.shape, f32),
            pltpu.SemaphoreType.DMA((5,)),
            pltpu.SemaphoreType.DMA((copies,)),
            pltpu.SemaphoreType.DMA((4,)),
        ],
        in_hbm=range(10),
    )
    arrived0 = neighbour_swap(pack0, 0)
    arrived1 = neighbour_swap(pack1, 1)
    earlier_high = lax.ppermute(high, "tm", onward)
    if two_chips(devs):
        earlier_low = time_swap(low, 1)
    else:
        earlier_low = lax.ppermute(low, "tm", onward)
    blocks_wide = (FACES + 1) * dofs
    splits = lambda count: [((count, blocks_wide, elems), bf16)] * 2
    (
        local, coefs, picks, blocks, face_blocks, halo_picks, flags, facing
    ) = run(
        first_local_kernel,
        (low, high, conduct, face_nbr, grad_mats, face_mats, counts_line),
        [
            (cube, f32),
            ((FACES + 2, samples, elems), f32),
            ((elems, FACES * elems), bf16),
            ((2 * dofs, blocks_wide), bf16),
            ((FACES, 2 * dofs, dofs), bf16),
            ((4 * halo, 2 * elems), bf16),
            ((1, 2 * halo), i32),
            ((2, half, 2 * halo), f32),
        ],
        splits(samples) + [((blocks_wide, 2 * dofs), f32)],
        flops=4 * 10**9,
    )
    groups = GROUPS
    if part % groups or (part // groups * (total_steps - 1)) % 2:
        groups = 1
    share = part // groups
    piece = ((share, dofs, elems), f32)
    scaled, extra = [], ()
    for at in range(groups):
        results = run(
            functools.partial(residual_kernel, total_steps=total_steps, groups=groups, at=at),
            (
                forcing,
                low,
                high,
                earlier_low,
                earlier_high,
                local,
                arrived0,
                arrived1,
                coefs,
                face_nbr,
                blocks,
                face_blocks,
                halo_picks,
                facing,
                flags,
                *extra,
            ),
            [piece] * devs
            + [((FACES + 2, samples, elems), f32), ((samples, elems), f32)] * (at == 0),
            [(cube, f32)],
        )
        scaled += results[:devs]
        if at == 0:
            coefs, extra = results[devs], (results[devs + 1],)
    sizes = lambda share: (
        ((share * total_steps, dofs, elems), f32),
        (((share * (total_steps - 1) + 1) // 2 * dofs, 2 * halo), f32),
        (share * (total_steps - 1) + 1) // 2,
    )
    some, packed, pairs = sizes(share)
    currents, spectra, inners, arrived0, arrived1, thetas, scales = ([] for _ in range(7))
    for at in range(groups):
        mine = dict(total_steps=total_steps, at=at, groups=groups)
        pieces = [time_swap(scaled[at * devs + turn], turn) for turn in range(devs)]
        spectrum, current, pack0, pack1 = run(
            functools.partial(spectrum_kernel, **mine),
            (flags, coefs, send, low, earlier_low, *pieces, *thetas[-1:]),
            [some, some, packed, packed],
            [((total_steps, share, dofs, elems), f32)],
        )
        arrived0.append(neighbour_swap(pack0, 0))
        arrived1.append(neighbour_swap(pack1, 1))
        inner, theta, scale = run(
            functools.partial(sweep_local_kernel, first_turn=True, inner=1, **mine),
            (flags, coefs, picks, blocks, halo_picks, current, spectrum),
            [
                some,
                ((2 * len(frequencies(total_steps)), share, elems), f32),
                ((2, pairs, 2 * halo), f32),
            ],
            [some] + splits(share * (total_steps - 1)),
            flops=3 * 10**9 // groups,
        )
        currents.append(current)
        spectra.append(spectrum)
        inners.append(inner)
        thetas.append(theta)
        scales.append(scale)
    tables = (flags, coefs, face_nbr, face_blocks, halo_picks)
    after, packs = [], ()
    for at in range(groups):
        rows = (at + 1) * pairs * dofs
        current, *packs = run(
            functools.partial(
                sweep_update_kernel,
                turn=0,
                total_steps=total_steps,
                last=False,
                sources=1,
                at=at,
                groups=groups,
            ),
            (
                *tables,
                inners[at],
                arrived0[at],
                arrived1[at],
                currents[at],
                thetas[at],
                scales[at],
                send,
                *packs,
            ),
            [some] + [((rows, 2 * halo), f32)] * 2,
            [some],
        )
        after.append(current)
    some, packed, pairs = sizes(part)
    arrived0 = neighbour_swap(packs[0], 0)
    arrived1 = neighbour_swap(packs[1], 1)
    (inner,) = run(
        functools.partial(
            sweep_local_kernel,
            first_turn=False,
            inner=groups,
            total_steps=total_steps,
            at=0,
            groups=1,
        ),
        (flags, coefs, picks, blocks, halo_picks, *after, *spectra),
        [some],
        [some] + splits(part * (total_steps - 1)),
        flops=3 * 10**9,
    )
    series = run(
        functools.partial(
            sweep_update_kernel,
            turn=1,
            total_steps=total_steps,
            last=True,
            sources=groups,
            at=0,
            groups=1,
        ),
        (*tables, inner, arrived0, arrived1, *after, *thetas, *scales),
        [((part, dofs, elems), f32)] * devs,
        [some, some],
    )
    restored = [time_swap(series[turn], turn) for turn in range(devs)]
    out = None
    for turns in (range(devs - 1), range(devs - 1, devs)):
        inputs = [restored[turn] for turn in turns] + ([] if out is None else [out])
        (out,) = run(
            functools.partial(assemble_kernel, turns=turns, total_steps=total_steps),
            tuple(inputs),
            [(cube, f32)],
            [pltpu.SemaphoreType.DMA((len(turns),))],
            in_hbm=() if out is None else (len(turns),),
            out_hbm=(0,),
            aliases=() if out is None else ((len(turns), 0),),
        )
    return out.reshape(samples, steps_dev, dofs, elems)


def solution(mesh):
    placed = (
        P("groups", "tm", None, "space"),
        P("groups", "tm", None, "space"),
        P("space"),
        P(None, "space"),
        P(),
        P(),
        P("groups"),
        P(),
        P(),
        P(None, "space"),
        P(None, "space"),
    )
    return jax.shard_map(
        per_device,
        mesh=mesh,
        in_specs=placed,
        out_specs=P("groups", "tm", None, "space"),
        check_vma=False,
    )
```

```python
import functools
import math

import jax
import jax.numpy as jnp
from jax import lax
from jax.experimental import pallas as pl
from jax.experimental.pallas import tpu as pltpu
from jax.sharding import PartitionSpec as P

MAXS = 3
alpha_circ = 0.05
time_step = 0.1
relax_rho = 2.3
highest = lax.Precision.HIGHEST
f32, bf16, i32 = jnp.float32, jnp.bfloat16, jnp.int32
FACES = 6
GROUPS = 2


def dot(a, b):
    return jnp.dot(a, b, preferred_element_type=f32)


def split(x):
    hi = x.astype(bf16)
    return hi, (x - hi.astype(f32)).astype(bf16)


def exact_select(x, onehot, across=0):
    a, b = split(x)
    c = (x - a.astype(f32) - b.astype(f32)).astype(bf16)
    times = lambda v: lax.dot_general(
        v, onehot, (((1,), (across,)), ((), ())), preferred_element_type=f32
    )
    return times(a) + (times(b) + times(c))


def times_block(stacked, x):
    rows = stacked.shape[0] // 2
    hi, lo = split(x)
    both = dot(stacked, hi)
    return both[:rows] + (both[rows:] + dot(stacked[:rows], lo))


def rows_iota(shape):
    return lax.broadcasted_iota(i32, shape, 0)


def halo_onehot(nbr_row, base, halo):
    elems = nbr_row.shape[1]
    entry = nbr_row - base
    here = (entry >= 0) & (entry < halo)
    entry = jnp.where(here, entry, -2 * halo)
    row = rows_iota((2 * halo, elems))
    left = (row == entry).astype(f32).astype(bf16)
    right = (row == entry + halo).astype(f32).astype(bf16)
    return jnp.concatenate([left, right], axis=1)


def space_even():
    return lax.rem(lax.axis_index("space") + lax.axis_index("tm"), 2) == 0


def sides(even, elems, halo):
    below, above = elems, elems + halo
    return (
        (jnp.where(even, 5, 4), jnp.where(even, above, below)),
        (jnp.where(even, 4, 5), jnp.where(even, below, above)),
    )


def group_size(count):
    return next(size for size in (4, 3, 2, 1) if count % size == 0)


def pack_group(ref, left, right, send, first, outs):
    dofs = ref.shape[1]
    width = send.shape[1] // 2
    sides_by_side = [jnp.concatenate([ref[i] for i in side], axis=0) for side in (left, right)]
    hi, lo = split(jnp.concatenate(sides_by_side, axis=1))
    got = dot(hi, send) + dot(lo, send)
    rows = slice(first * dofs, (first + len(left)) * dofs)
    for which, out in enumerate(outs):
        out[rows, :] = got[:, which * width : (which + 1) * width]


def pack_fields(ref, fields, send, outs):
    half = len(fields) // 2
    size = group_size(half)
    for j in range(0, half, size):
        pack_group(
            ref, fields[j : j + size], fields[half + j : half + j + size], send, j, outs
        )


def prepare_kernel(
    iterate_in,
    halo_send_in,
    shift_in,
    gen_in,
    mean_in,
    modes_in,
    nbr_in,
    grads_in,
    face_mats_in,
    counts_in,
    pack0,
    pack1,
    send_out,
    conduct_out,
    low,
    high,
    nbr,
    grads,
    face_mats,
    counts,
    halo_send,
    shift,
    gen,
    mean,
    modes,
    small_done,
    field_done,
    later_done,
):
    iterate = Halves(low, high)
    samples, dofs, elems = iterate.shape
    halo = halo_send.shape[1]
    half = samples // 2
    size = group_size(half)
    small = [
        pltpu.make_async_copy(source, target, small_done.at[i])
        for i, (source, target) in enumerate(
            (
                (halo_send_in, halo_send),
                (shift_in, shift),
                (gen_in, gen),
                (mean_in, mean),
                (modes_in, modes),
            )
        )
    ]
    large = []
    for j in range(0, half, size):
        for at, side in ((j, low), (half + j, high)):
            large.append(
                pltpu.make_async_copy(
                    iterate_in.at[pl.ds(at, size)],
                    side.at[pl.ds(j, size)],
                    field_done.at[len(large)],
                )
            )
    later = [
        pltpu.make_async_copy(source, target, later_done.at[i])
        for i, (source, target) in enumerate(
            ((nbr_in, nbr), (grads_in, grads), (face_mats_in, face_mats), (counts_in, counts))
        )
    ]
    for copy in small + large + later:
        copy.start()
    for copy in small + large:
        copy.wait()
    even = space_even()
    down = jnp.concatenate([halo_send[0:1, :]] * 2, axis=1)
    up = jnp.concatenate([halo_send[1:2, :]] * 2, axis=1)
    lane = lax.broadcasted_iota(i32, (1, 2 * halo), 1)
    row = rows_iota((2 * elems, 2 * halo))
    for which in range(2):
        ids = jnp.where(even == (which == 0), up, down)
        ids = jnp.where(lane < halo, ids, ids + elems)
        send_out[:, which * 2 * halo : (which + 1) * 2 * halo] = (
            (row == ids).astype(f32).astype(bf16)
        )
    position = rows_iota((samples, gen.shape[1]))
    residue = lax.rem(position * gen[...], samples)
    shifted = residue.astype(f32) / samples + shift[...]
    fraction = shifted - jnp.floor(shifted)
    points = 0.5 - jnp.abs(2.0 * fraction - 1.0)
    conduct = mean[...] * (
        1.0 + jnp.dot(points, modes[...], precision=highest, preferred_element_type=f32)
    )
    conduct_out[...] = conduct
    send = send_out[...]
    got = exact_select(jnp.concatenate([conduct[:half], conduct[half:]], axis=1), send)
    pack0[half * dofs :, :] = got[:, : 2 * halo]
    pack1[half * dofs :, :] = got[:, 2 * halo :]
    for j in range(0, half, size):
        left = list(range(j, j + size))
        pack_group(iterate, left, [half + i for i in left], send, j, (pack0, pack1))
    for copy in later:
        copy.wait()


def local_part(read, slots, coef_row, picks, blocks, out, high, low):
    dofs, elems = out.shape[1], out.shape[2]
    size = group_size(len(slots))
    for first in range(0, len(slots), size):
        group = range(first, first + size)
        values = [read(t) for t in group]
        hi, lo = split(jnp.concatenate(values, axis=0))
        for t, value in zip(group, values):
            a, b = split(value * coef_row(FACES, t))
            high[t, 0:dofs, :] = a
            low[t, 0:dofs, :] = b
        for f in range(FACES):
            pick = picks[:, f * elems : (f + 1) * elems]
            got = dot(hi, pick) + dot(lo, pick)
            at = (f + 1) * dofs
            for i, t in enumerate(group):
                a, b = split(got[i * dofs : (i + 1) * dofs] * coef_row(f, t))
                high[t, at : at + dofs, :] = a
                low[t, at : at + dofs, :] = b
        stacked = blocks[...]
        for t in group:
            both = dot(stacked, high[t])
            out[slots[t]] = both[:dofs] + (both[dofs:] + dot(stacked[:dofs], low[t]))


def first_local_kernel(
    low_fields,
    high_fields,
    conduct_ref,
    face_nbr,
    grads,
    face_mats,
    counts_in,
    out,
    coefs,
    picks,
    blocks,
    face_blocks,
    halo_picks,
    flags,
    facing,
    high,
    low,
    wide,
):
    iterate = Halves(low_fields, high_fields)
    samples, dofs, elems = iterate.shape
    halo = halo_picks.shape[0] // 4
    even = space_even()
    row = rows_iota((elems, elems))
    for f in range(FACES):
        picks[:, f * elems : (f + 1) * elems] = (
            (row == face_nbr[f : f + 1, :]).astype(f32).astype(bf16)
        )
    conduct = conduct_ref[...]
    diag = conduct
    for f in range(FACES):
        nbr = face_nbr[f : f + 1, :]
        across = exact_select(conduct, picks[:, f * elems : (f + 1) * elems])
        inside = (nbr >= 0) & (nbr < elems)
        coupling = jnp.where(inside, 0.5 * (conduct + across), 0.0)
        coefs[f] = coupling
        diag = diag + jnp.where(nbr < 0, conduct, coupling)
    coefs[FACES] = diag
    coefs[FACES + 1] = conduct
    volume = (rows_iota((dofs, dofs)) == lax.broadcasted_iota(i32, (dofs, dofs), 1)).astype(f32)
    for d in range(grads.shape[0]):
        volume = volume + lax.dot_general(
            grads[d], grads[d], (((0,), (0,)), ((), ())), precision=highest,
            preferred_element_type=f32,
        )
    wide[...] = jnp.zeros(wide.shape, f32)
    wide[0:dofs, 0:dofs] = volume
    for f in range(FACES):
        block = face_mats[f // 2]
        at = (f + 1) * dofs
        wide[at : at + dofs, 0:dofs] = block if f % 2 == 0 else block.T
    turned = wide[...].T[:dofs, :]
    hi, lo = split(turned)
    blocks[0:dofs, :] = hi
    blocks[dofs:, :] = lo
    for f in range(FACES):
        block = face_mats[f // 2]
        hi, lo = split(block.T if f % 2 == 0 else block)
        face_blocks[f, 0:dofs, :] = hi
        face_blocks[f, dofs:, :] = lo
    for which, (face, base) in enumerate(sides(even, elems, halo)):
        nbr = jnp.where(face == 4, face_nbr[4:5, :], face_nbr[5:6, :])
        pick = halo_onehot(nbr, base, halo)
        halo_picks[which * 2 * halo : (which + 1) * 2 * halo, :] = pick
        facing[which] = exact_select(side_by_side(conduct), pick, 1)
    crossing = jnp.max(jnp.where(face_nbr[0:4, :] >= elems, 1, 0))
    crossing = crossing + jnp.max(jnp.where(face_nbr[4:5, :] >= elems + halo, 1, 0))
    fifth = face_nbr[5:6, :]
    crossing = crossing + jnp.max(
        jnp.where((fifth >= elems) & (fifth < elems + halo), 1, 0)
    )
    lane = lax.broadcasted_iota(i32, flags.shape, 1)
    line = jnp.where(lane == 0, crossing, 0)
    skip = jnp.int32(0)
    for k in range(counts_in.shape[1]):
        line = jnp.where(lane == 2 + k, counts_in[0, k], line)
    for k, re, _ in frequencies(counts_in.shape[1]):
        skip = jnp.where(counts_in[0, k] == 1, re, skip)
    flags[...] = jnp.where(lane == 1, skip, line)
    local_part(
        lambda t: iterate[t],
        list(range(samples)),
        lambda f, t: coefs[f, t : t + 1, :],
        picks,
        blocks,
        out,
        high,
        low,
    )


def side_by_side(x):
    half = x.shape[0] // 2
    return jnp.concatenate([x[:half], x[half:]], axis=1)


def stacked_halves(x):
    width = x.shape[1] // 2
    return jnp.concatenate([x[:, :width], x[:, width:]], axis=0)


def usual_halo(arrived, scales, blocks, picks, chosen=None):
    dofs = blocks[0].shape[1]
    columns = []
    for which in range(2):
        value = arrived[which]
        width = value.shape[1]
        chosen = range(scales[which].shape[0]) if chosen is None else chosen
        pairs = len(chosen)
        scaled = [
            value[j * dofs : (j + 1) * dofs, :] * scales[which][j : j + 1, :] for j in chosen
        ]
        got = times_block(blocks[which], jnp.concatenate(scaled, axis=1))
        columns.append(
            jnp.concatenate([got[:, j * width : (j + 1) * width] for j in range(pairs)], axis=0)
        )
    hi, lo = split(jnp.concatenate(columns, axis=1))
    return dot(hi, picks) + dot(lo, picks)


class Halves:
    def __init__(self, low, high):
        self.low, self.high = low, high
        self.shape = (2 * low.shape[0],) + tuple(low.shape[1:])

    def __getitem__(self, at):
        half = self.low.shape[0]
        return self.low[at] if at < half else self.high[at - half]


def other_halo(arrived, block, pick):
    dofs = block.shape[1]
    hi, lo = split(times_block(block, arrived))
    got = dot(hi, pick) + dot(lo, pick)
    return got


def other_sides(flags, even, face_nbr, halo, body):
    elems = face_nbr.shape[1]

    @pl.when(flags[0, 0] > 0)
    def _():
        for which, (usual, base) in enumerate(sides(even, elems, halo)):

            def step(face, carry, which=which, usual=usual, base=base):
                @pl.when(face != usual)
                def _():
                    body(which, face, halo_onehot(face_nbr[pl.ds(face, 1), :], base, halo))

                return carry

            lax.fori_loop(0, FACES, step, 0)


def pair_place(t, half, dofs, elems):
    row, col = t % half * dofs, t // half * elems
    return slice(row, row + dofs), slice(col, col + elems)


def add_others(arrived, even, flags, face_nbr, face_blocks, halo, chosen, slots, coef_row, factor, total):
    elems = face_nbr.shape[1]
    dofs = total.shape[1]

    def body(which, face, pick):
        block = face_blocks[face]
        half = len(chosen)
        for i, j in enumerate(chosen):
            got = other_halo(arrived[which][j * dofs : (j + 1) * dofs, :], block, pick)
            for t in (i, half + i):
                if t < len(slots):
                    cols = slice(t // half * elems, (t // half + 1) * elems)
                    field = slots[t]
                    total[field] = total[field] + factor * coef_row(face, t) * got[:, cols]

    other_sides(flags, even, face_nbr, halo, body)


def residual_kernel(
    forcing,
    low_fields,
    high_fields,
    earlier_low,
    earlier_high,
    local,
    arrived0,
    arrived1,
    coefs_in,
    face_nbr,
    blocks,
    face_blocks,
    halo_picks,
    facing,
    flags,
    *rest,
    total_steps,
    groups,
    at,
):
    samples, dofs, elems = forcing.shape
    if at == 0:
        outs, (coefs, extra, total) = rest[:total_steps], rest[total_steps:]
    else:
        extra, outs, total = rest[0], rest[1 : total_steps + 1], rest[-1]
        coefs = coefs_in
    iterate = Halves(low_fields, high_fields)
    halo = halo_picks.shape[0] // 4
    half = samples // 2
    part = samples // total_steps
    size = part // groups
    chosen = [j for j in range(half) if j % part // size == at]
    mine = chosen + [half + j for j in chosen]
    even = space_even()
    usual = sides(even, elems, halo)
    arrived = (arrived0, arrived1)
    scales = [0.5 * (facing[w] + arrived[w][half * dofs :, :]) for w in range(2)]
    if at == 0:
        coefs[...] = coefs_in[...]
        conduct = coefs_in[FACES + 1]
        couplings = [
            stacked_halves(
                exact_select(scales[w], halo_picks[w * 2 * halo : (w + 1) * 2 * halo, :])
            )
            for w in range(2)
        ]
        extra[...] = couplings[0] + couplings[1]
        for w in range(2):
            coefs[usual[w][0]] = coefs[usual[w][0]] + couplings[w]

        def add_coupling(which, face, pick):
            got = exact_select(arrived[which][half * dofs :, :], pick)
            nbr = face_nbr[pl.ds(face, 1), :]
            base = usual[which][1]
            here = (nbr >= base) & (nbr < base + halo)
            coupling = jnp.where(here, 0.5 * (conduct + stacked_halves(got)), 0.0)
            coefs[face] = coefs[face] + coupling
            extra[...] = extra[...] + coupling

        other_sides(flags, even, face_nbr, halo, add_coupling)
        coefs[FACES] = coefs[FACES] + extra[...]
    volume = blocks[:, 0 : 2 * dofs][:, :dofs]
    brought = usual_halo(
        arrived,
        scales,
        [face_blocks[usual[w][0]] for w in range(2)],
        halo_picks[...],
        chosen,
    )
    for t, j in enumerate(mine):
        value = iterate[j]
        total[j] = value + time_step * (
            local[j]
            + brought[pair_place(t, len(chosen), dofs, elems)]
            + times_block(volume, value * extra[j : j + 1, :])
        )
    add_others(
        arrived,
        even,
        flags,
        face_nbr,
        face_blocks,
        halo,
        chosen,
        mine,
        lambda f, t: coefs[f, mine[t] : mine[t] + 1, :],
        time_step,
        total,
    )
    step = lax.axis_index("tm")
    weight = jnp.float32(0.0)
    for n in range(total_steps):
        weight = jnp.where(step == n, jnp.float32(alpha_circ ** (n / total_steps)), weight)
    gate_high = jnp.where(step > 0, weight, 0.0)
    gate_low = jnp.where(step % 2 == 1, weight, 0.0) if two_chips(total_steps) else gate_high
    for turn, out in enumerate(outs):
        first = (partner(step, turn, total_steps) * groups + at) * size
        for i in range(size):
            j = first + i
            inner = forcing[j] - total[j]
            before = lax.rem(j, half)
            late = j >= half
            earlier = jnp.where(late, earlier_high[before], earlier_low[before])
            out[i] = weight * inner + jnp.where(late, gate_high, gate_low) * earlier


def two_chips(devs):
    return devs == 4


def partner(rank, turn, count):
    if count & (count - 1) == 0:
        return rank ^ turn
    return lax.rem(turn + count - rank, count)


def real_fields(total_steps):
    order = [(0, False)]
    if total_steps % 2 == 0:
        order.append((total_steps // 2, False))
    for k in range(1, (total_steps + 1) // 2):
        order += [(k, False), (k, True)]
    return order


def cos_sin(k, n, total_steps):
    turn = 2.0 * math.pi * ((k * n) % total_steps) / total_steps
    c, s = math.cos(turn), math.sin(turn)
    snap = lambda v: float(round(v)) if abs(v - round(v)) < 1e-12 else v
    return snap(c), snap(s)


def weighted(terms):
    total = None
    for constant, value in terms:
        if constant == 0.0:
            continue
        if total is None:
            total = value if constant == 1.0 else constant * value
        elif constant == 1.0:
            total = total + value
        elif constant == -1.0:
            total = total - value
        else:
            total = total + constant * value
    return total


def shift_of(k, total_steps):
    magnitude = alpha_circ ** (1.0 / total_steps)
    c, s = cos_sin(k, 1, total_steps)
    return 1.0 - magnitude * c, magnitude * s


def theta_rows(k, total_steps, diag):
    shift_real, shift_imag = shift_of(k, total_steps)
    denom = shift_real + (time_step * relax_rho) * diag
    if shift_imag == 0.0:
        return 1.0 / denom, None
    modulus = denom * denom + shift_imag * shift_imag
    return denom / modulus, -shift_imag / modulus


def frequencies(total_steps):
    order = real_fields(total_steps)
    return [
        (k, at, order.index((k, True)) if (k, True) in order else None)
        for at, (k, imag) in enumerate(order)
        if not imag
    ]


def slot_order(samples, total_steps, inner):
    size = samples // inner
    lists = [
        [(g * size + s, i) for s in range(size) for i in range(total_steps - 1)]
        for g in range(inner)
    ]
    if inner == 1:
        return lists[0]
    middle = len(lists[0]) // 2
    return [pair for part in lists for pair in part[:middle]] + [
        pair for part in lists for pair in part[middle:]
    ]


def kept_slots(flags, order, total_steps):
    skip = flags[0, 1]
    return [s * total_steps + jnp.where(skip <= i, i + 1, i) for s, i in order]


def even_slots(slots):
    return slots + slots[: len(slots) % 2]


def my_first(samples, at, groups):
    return (lax.axis_index("tm") * groups + at) * samples


def sample_row(coefs, order, first):
    return lambda f, t: coefs[f, pl.ds(first + order[t][0], 1), :]


def spectrum_kernel(
    flags, coefs, send_ref, own, near, *rest, total_steps, at, groups
):
    arrived, (spectrum, first_w, pack0, pack1, pieces) = rest[:total_steps], rest[-5:]
    samples = arrived[0].shape[0]
    first = my_first(samples, at, groups)
    rank = lax.axis_index("tm")
    for turn, piece in enumerate(arrived):
        pieces[partner(rank, turn, total_steps)] = piece[...]
    if two_chips(total_steps):
        here = at * samples
        there = groups * samples + here
        gate = jnp.where(rank < 2, jnp.float32(alpha_circ ** (2 / total_steps)), 0.0)
        for s in range(samples):
            before = jnp.where(rank == 0, near[here + s], own[there + s])
            pieces[2, s] = pieces[2, s] + gate * before
    for s in range(samples):
        diag = coefs[FACES, pl.ds(first + s, 1), :]
        base = s * total_steps
        for k, re, im in frequencies(total_steps):
            tables = [cos_sin(k, n, total_steps) for n in range(total_steps)]
            real = weighted([(tables[n][0], pieces[n, s]) for n in range(total_steps)])
            rate_real, rate_imag = theta_rows(k, total_steps, diag)
            spectrum[base + re] = real
            if im is None:
                first_w[base + re] = rate_real * real
            else:
                imag = weighted([(-tables[n][1], pieces[n, s]) for n in range(total_steps)])
                spectrum[base + im] = imag
                first_w[base + re] = rate_real * real - rate_imag * imag
                first_w[base + im] = rate_real * imag + rate_imag * real
    slots = kept_slots(flags, slot_order(samples, total_steps, 1), total_steps)
    pack_fields(first_w, even_slots(slots), send_ref[...], (pack0, pack1))


def sweep_local_kernel(
    flags,
    coefs,
    picks,
    blocks,
    halo_picks,
    *rest,
    total_steps,
    at,
    groups,
    first_turn,
    inner,
):
    fields, spectra, rest = rest[:inner], rest[inner : 2 * inner], rest[2 * inner :]
    if first_turn:
        out, thetas, scales, total, high, low = rest
    else:
        out, total, high, low = rest[-4:]
    elems = fields[0].shape[2]
    each = fields[0].shape[0] // total_steps
    samples = inner * each
    first = my_first(samples, at, groups)
    order = slot_order(samples, total_steps, inner)
    slots = kept_slots(flags, order, total_steps)
    row = sample_row(coefs, order, first)
    if first_turn:
        halo = halo_picks.shape[0] // 4
        half = scales.shape[1]
        usual = sides(space_even(), elems, halo)
        count = len(slots)
        for w in range(2):
            lines = [
                row(usual[w][0], t if t < count else 0) for t in range(2 * half)
            ]
            sides_of = [jnp.concatenate(lines[:half], 0), jnp.concatenate(lines[half:], 0)]
            scales[w] = time_step * exact_select(
                jnp.concatenate(sides_of, axis=1),
                halo_picks[w * 2 * halo : (w + 1) * 2 * halo, :],
                1,
            )
        diag = jnp.concatenate(
            [coefs[FACES, pl.ds(first + s, 1), :] for s in range(samples)], axis=0
        )
        for i, (k, _, im) in enumerate(frequencies(total_steps)):
            rate_real, rate_imag = theta_rows(k, total_steps, diag)
            thetas[2 * i] = rate_real
            if im is not None:
                thetas[2 * i + 1] = rate_imag

    def read(t):
        which = order[t][0] // each
        return fields[which][slots[t] - which * each * total_steps]

    local_part(read, slots, row, picks, blocks, total, high, low)
    for s in range(samples):
        base = s * total_steps
        spectrum, current = spectra[s // each], fields[s // each]
        own = s % each * total_steps
        for k, re, im in frequencies(total_steps):
            shift_real, shift_imag = shift_of(k, total_steps)
            value = current[own + re]
            kept = spectrum[own + re] - (shift_real * value + time_step * total[base + re])
            if im is not None:
                other = current[own + im]
                kept = kept + shift_imag * other
                out[base + im] = spectrum[own + im] - (
                    shift_real * other + shift_imag * value + time_step * total[base + im]
                )
            out[base + re] = kept


def sweep_update_kernel(
    flags,
    coefs,
    face_nbr,
    face_blocks,
    halo_picks,
    *rest,
    turn,
    total_steps,
    last,
    sources,
    at,
    groups,
):
    even = space_even()
    take = lambda count: (rest[:count], rest[count:])
    (inner, arrived0, arrived1), rest = take(3)
    currents, rest = take(sources)
    thetas, rest = take(sources)
    scale_refs, rest = take(sources)
    if last:
        outs, (total, solved) = rest[:total_steps], rest[total_steps:]
    else:
        send_ref, *before, solved, pack0, pack1, total = rest
    fields, dofs, elems = inner.shape
    samples = fields // total_steps
    each = samples // sources
    first = my_first(samples, at, groups)
    halo = halo_picks.shape[0] // 4
    usual = sides(even, elems, halo)
    scales = [jnp.concatenate([ref[w] for ref in scale_refs], axis=0) for w in range(2)]
    half = scales[0].shape[0]
    arrived = (arrived0, arrived1)
    order = slot_order(samples, total_steps, sources)
    slots = kept_slots(flags, order, total_steps)
    brought = usual_halo(
        arrived,
        scales,
        [face_blocks[usual[w][0]] for w in range(2)],
        halo_picks[...],
    )
    for t, field in enumerate(slots):
        total[field] = inner[field] - brought[pair_place(t, half, dofs, elems)]
    add_others(
        arrived,
        even,
        flags,
        face_nbr,
        face_blocks,
        halo,
        range(half),
        slots,
        sample_row(coefs, order, first),
        -time_step,
        total,
    )
    for s in range(samples):
        base = s * total_steps
        current, theta = currents[s // each], thetas[s // each]
        own = s % each * total_steps
        line = slice(s % each, s % each + 1)
        for i, (k, re, im) in enumerate(frequencies(total_steps)):
            active = flags[0, 2 + k] > turn + 1
            rate_real = theta[2 * i, line, :]
            value, rest_real = current[own + re], total[base + re]
            change = rate_real * rest_real
            if im is not None:
                rate_imag = theta[2 * i + 1, line, :]
                other, rest_imag = current[own + im], total[base + im]
                change = change - rate_imag * rest_imag
                solved[base + im] = jnp.where(
                    active, other + (rate_real * rest_imag + rate_imag * rest_real), other
                )
            solved[base + re] = jnp.where(active, value + change, value)
    if not last:
        rows = half * dofs
        start = at * rows if before else 0
        for ref, out in zip(before, (pack0, pack1)):
            out[:start, :] = ref[...]
        pack_fields(
            solved,
            even_slots(slots),
            send_ref[...],
            [out.at[start : start + rows] for out in (pack0, pack1)],
        )
        return
    rank = lax.axis_index("tm")
    for s in range(samples):
        base = s * total_steps
        for n in range(total_steps):
            scale = alpha_circ ** (-n / total_steps) / total_steps
            terms = []
            for k, re, im in frequencies(total_steps):
                c, sn = cos_sin(k, n, total_steps)
                if im is None:
                    terms.append((c, solved[base + re]))
                else:
                    terms += [(2.0 * c, solved[base + re]), (-2.0 * sn, solved[base + im])]
            total[n * samples + s] = scale * weighted(terms)
    for turn_to, out in enumerate(outs):
        step = partner(rank, turn_to, total_steps)
        for s in range(samples):
            out[s] = total[step * samples + s]


def assemble_kernel(*rest, places, total_steps, groups):
    count = len(places)
    pieces, (out, done) = rest[:count], rest[-2:]
    size = pieces[0].shape[0]
    rank = lax.axis_index("tm")
    copies = []
    for which, ((at, turn), piece) in enumerate(zip(places, pieces)):
        first = (partner(rank, turn, total_steps) * groups + at) * size
        copies.append(
            pltpu.make_async_copy(piece, out.at[pl.ds(first, size)], done.at[which])
        )
    for copy in copies:
        copy.start()
    for copy in copies:
        copy.wait()


vmem = pl.BlockSpec(memory_space=pltpu.VMEM)


def run(
    kernel, inputs, outs, scratch=(), in_hbm=(), out_hbm=(), aliases=(), flops=10**9
):
    def spec(i, outside):
        return pl.BlockSpec(memory_space=pltpu.HBM) if i in outside else vmem

    inputs = [
        pltpu.with_memory_space_constraint(value, pltpu.HBM) if i in in_hbm else value
        for i, value in enumerate(inputs)
    ]
    return pl.pallas_call(
        kernel,
        out_shape=[jax.ShapeDtypeStruct(*o) for o in outs],
        in_specs=[spec(i, in_hbm) for i in range(len(inputs))],
        out_specs=[spec(i, out_hbm) for i in range(len(outs))],
        input_output_aliases=dict(aliases),
        scratch_shapes=[pltpu.VMEM(*s) if isinstance(s, tuple) else s for s in scratch],
        compiler_params=pltpu.CompilerParams(vmem_limit_bytes=40 << 20),
        cost_estimate=pl.CostEstimate(flops=flops, bytes_accessed=1 << 22, transcendentals=0),
    )(*inputs)


def neighbour_swap(value, start):
    axes = ("groups", "tm", "space")
    parts, devs, count = (lax.axis_size(axis) for axis in axes)
    pairs = []
    for part in range(parts):
        for tm in range(devs):
            for space in range(count):
                step = 1 if (space + tm + start) % 2 == 0 else -1
                to_part, to_space = part, space + step
                if not 0 <= to_space < count:
                    to_part, to_space = part ^ 1, space
                if to_part < parts:
                    pairs.append(
                        ((part * devs + tm) * count + space, (to_part * devs + tm) * count + to_space)
                    )
    return lax.ppermute(value, axes, pairs)


def time_swap(value, turn):
    count = lax.axis_size("tm")
    pairs = [(i, int(partner(i, turn, count))) for i in range(count)]
    return value if turn == 0 else lax.ppermute(value, "tm", pairs)


def per_device(
    forcing,
    iterate,
    kappa_mean,
    kappa_modes,
    grad_mats,
    face_mats,
    lattice_shift,
    gen_vector,
    sweep_counts,
    face_nbr,
    halo_send,
):
    samples, steps_dev, dofs, elems = forcing.shape
    halo = halo_send.shape[1]
    devs = lax.axis_size("tm")
    total_steps = steps_dev * devs
    part = samples // devs
    half = samples // 2
    cube = (samples, dofs, elems)
    forcing = forcing.reshape(cube)
    iterate = iterate.reshape(cube)
    onward = [(i, (i + 1) % devs) for i in range(devs)]
    rows = half * dofs
    copies = 2 * (half // group_size(half))
    (
        pack0, pack1, send, conduct, low, high, face_nbr, grad_mats, face_mats, counts_line
    ) = run(
        prepare_kernel,
        (
            iterate,
            halo_send,
            lattice_shift.reshape(1, -1),
            gen_vector.reshape(1, -1),
            kappa_mean.reshape(1, -1),
            kappa_modes,
            face_nbr,
            grad_mats,
            face_mats,
            sweep_counts.reshape(1, -1),
        ),
        [
            ((rows + half, 2 * halo), f32),
            ((rows + half, 2 * halo), f32),
            ((2 * elems, 4 * halo), bf16),
            ((samples, elems), f32),
            ((half, dofs, elems), f32),
            ((half, dofs, elems), f32),
            (face_nbr.shape, i32),
            (grad_mats.shape, f32),
            (face_mats.shape, f32),
            ((1, sweep_counts.shape[0]), i32),
        ],
        [
            (halo_send.shape, i32),
            ((1, lattice_shift.shape[0]), f32),
            ((1, gen_vector.shape[0]), i32),
            ((1, elems), f32),
            (kappa_modes.shape, f32),
            pltpu.SemaphoreType.DMA((5,)),
            pltpu.SemaphoreType.DMA((copies,)),
            pltpu.SemaphoreType.DMA((4,)),
        ],
        in_hbm=range(10),
    )
    arrived0 = neighbour_swap(pack0, 0)
    arrived1 = neighbour_swap(pack1, 1)
    earlier_high = lax.ppermute(high, "tm", onward)
    if two_chips(devs):
        earlier_low = time_swap(low, 1)
    else:
        earlier_low = lax.ppermute(low, "tm", onward)
    blocks_wide = (FACES + 1) * dofs
    splits = lambda count: [((count, blocks_wide, elems), bf16)] * 2
    (
        local, coefs, picks, blocks, face_blocks, halo_picks, flags, facing
    ) = run(
        first_local_kernel,
        (low, high, conduct, face_nbr, grad_mats, face_mats, counts_line),
        [
            (cube, f32),
            ((FACES + 2, samples, elems), f32),
            ((elems, FACES * elems), bf16),
            ((2 * dofs, blocks_wide), bf16),
            ((FACES, 2 * dofs, dofs), bf16),
            ((4 * halo, 2 * elems), bf16),
            ((1, 2 * halo), i32),
            ((2, half, 2 * halo), f32),
        ],
        splits(samples) + [((blocks_wide, 2 * dofs), f32)],
        flops=4 * 10**9,
    )
    groups = GROUPS
    if part % groups or (part // groups * (total_steps - 1)) % 2:
        groups = 1
    share = part // groups
    piece = ((share, dofs, elems), f32)
    scaled, extra = [], ()
    for at in range(groups):
        results = run(
            functools.partial(residual_kernel, total_steps=total_steps, groups=groups, at=at),
            (
                forcing,
                low,
                high,
                earlier_low,
                earlier_high,
                local,
                arrived0,
                arrived1,
                coefs,
                face_nbr,
                blocks,
                face_blocks,
                halo_picks,
                facing,
                flags,
                *extra,
            ),
            [piece] * devs
            + [((FACES + 2, samples, elems), f32), ((samples, elems), f32)] * (at == 0),
            [(cube, f32)],
        )
        scaled += results[:devs]
        if at == 0:
            coefs, extra = results[devs], (results[devs + 1],)
    sizes = lambda share: (
        ((share * total_steps, dofs, elems), f32),
        (((share * (total_steps - 1) + 1) // 2 * dofs, 2 * halo), f32),
        (share * (total_steps - 1) + 1) // 2,
    )
    some, packed, pairs = sizes(share)
    currents, spectra, inners, arrived0, arrived1, thetas, scales = ([] for _ in range(7))
    for at in range(groups):
        mine = dict(total_steps=total_steps, at=at, groups=groups)
        pieces = [time_swap(scaled[at * devs + turn], turn) for turn in range(devs)]
        spectrum, current, pack0, pack1 = run(
            functools.partial(spectrum_kernel, **mine),
            (flags, coefs, send, low, earlier_low, *pieces, *thetas[-1:]),
            [some, some, packed, packed],
            [((total_steps, share, dofs, elems), f32)],
        )
        arrived0.append(neighbour_swap(pack0, 0))
        arrived1.append(neighbour_swap(pack1, 1))
        inner, theta, scale = run(
            functools.partial(sweep_local_kernel, first_turn=True, inner=1, **mine),
            (flags, coefs, picks, blocks, halo_picks, current, spectrum),
            [
                some,
                ((2 * len(frequencies(total_steps)), share, elems), f32),
                ((2, pairs, 2 * halo), f32),
            ],
            [some] + splits(share * (total_steps - 1)),
            flops=3 * 10**9 // groups,
        )
        currents.append(current)
        spectra.append(spectrum)
        inners.append(inner)
        thetas.append(theta)
        scales.append(scale)
    tables = (flags, coefs, face_nbr, face_blocks, halo_picks)
    restored = {}
    arrived = []
    for at in range(groups):
        mine = dict(total_steps=total_steps, at=at, groups=groups)
        current, *packs = run(
            functools.partial(sweep_update_kernel, turn=0, last=False, sources=1, **mine),
            (
                *tables,
                inners[at],
                arrived0[at],
                arrived1[at],
                currents[at],
                thetas[at],
                scales[at],
                send,
            ),
            [some, packed, packed],
            [some],
        )
        currents[at] = current
        arrived.append([neighbour_swap(pack, which) for which, pack in enumerate(packs)])
    series = ()
    for at in range(groups):
        mine = dict(total_steps=total_steps, at=at, groups=groups)
        (inner,) = run(
            functools.partial(sweep_local_kernel, first_turn=False, inner=1, **mine),
            (flags, coefs, picks, blocks, halo_picks, currents[at], spectra[at], *series[:1]),
            [some],
            [some] + splits(share * (total_steps - 1)),
            flops=3 * 10**9 // groups,
        )
        series = run(
            functools.partial(sweep_update_kernel, turn=1, last=True, sources=1, **mine),
            (*tables, inner, *arrived[at], currents[at], thetas[at], scales[at]),
            [piece] * devs,
            [some, some],
        )
        for turn in range(devs):
            restored[at, turn] = time_swap(series[turn], turn)
    out = None
    places = list(restored)
    for chosen in (places[:-1], places[-1:]):
        inputs = [restored[place] for place in chosen] + ([] if out is None else [out])
        (out,) = run(
            functools.partial(
                assemble_kernel, places=chosen, total_steps=total_steps, groups=groups
            ),
            tuple(inputs),
            [(cube, f32)],
            [pltpu.SemaphoreType.DMA((len(chosen),))],
            in_hbm=() if out is None else (len(chosen),),
            out_hbm=(0,),
            aliases=() if out is None else ((len(chosen), 0),),
        )
    return out.reshape(samples, steps_dev, dofs, elems)


def solution(mesh):
    placed = (
        P("groups", "tm", None, "space"),
        P("groups", "tm", None, "space"),
        P("space"),
        P(None, "space"),
        P(),
        P(),
        P("groups"),
        P(),
        P(),
        P(None, "space"),
        P(None, "space"),
    )
    return jax.shard_map(
        per_device,
        mesh=mesh,
        in_specs=placed,
        out_specs=P("groups", "tm", None, "space"),
        check_vma=False,
    )
```

```python
import functools
import math

import jax
import jax.numpy as jnp
from jax import lax
from jax.experimental import pallas as pl
from jax.experimental.pallas import tpu as pltpu
from jax.sharding import PartitionSpec as P

MAXS = 3
alpha_circ = 0.05
time_step = 0.1
relax_rho = 2.3
highest = lax.Precision.HIGHEST
f32, bf16, i32 = jnp.float32, jnp.bfloat16, jnp.int32
FACES = 6
GROUPS = 2


def dot(a, b):
    return jnp.dot(a, b, preferred_element_type=f32)


def split(x):
    hi = x.astype(bf16)
    return hi, (x - hi.astype(f32)).astype(bf16)


def exact_select(x, onehot, across=0):
    a, b = split(x)
    c = (x - a.astype(f32) - b.astype(f32)).astype(bf16)
    times = lambda v: lax.dot_general(
        v, onehot, (((1,), (across,)), ((), ())), preferred_element_type=f32
    )
    return times(a) + (times(b) + times(c))


def times_block(stacked, x):
    rows = stacked.shape[0] // 2
    hi, lo = split(x)
    both = dot(stacked, hi)
    return both[:rows] + (both[rows:] + dot(stacked[:rows], lo))


def rows_iota(shape):
    return lax.broadcasted_iota(i32, shape, 0)


def halo_onehot(nbr_row, base, halo):
    elems = nbr_row.shape[1]
    entry = nbr_row - base
    here = (entry >= 0) & (entry < halo)
    entry = jnp.where(here, entry, -2 * halo)
    row = rows_iota((2 * halo, elems))
    left = (row == entry).astype(f32).astype(bf16)
    right = (row == entry + halo).astype(f32).astype(bf16)
    return jnp.concatenate([left, right], axis=1)


def space_even():
    return lax.rem(lax.axis_index("space") + lax.axis_index("tm"), 2) == 0


def sides(even, elems, halo):
    below, above = elems, elems + halo
    return (
        (jnp.where(even, 5, 4), jnp.where(even, above, below)),
        (jnp.where(even, 4, 5), jnp.where(even, below, above)),
    )


def group_size(count):
    return next(size for size in (4, 3, 2, 1) if count % size == 0)


def pack_group(ref, left, right, send, first, outs):
    dofs = ref.shape[1]
    width = send.shape[1] // 2
    sides_by_side = [jnp.concatenate([ref[i] for i in side], axis=0) for side in (left, right)]
    hi, lo = split(jnp.concatenate(sides_by_side, axis=1))
    got = dot(hi, send) + dot(lo, send)
    rows = slice(first * dofs, (first + len(left)) * dofs)
    for which, out in enumerate(outs):
        out[rows, :] = got[:, which * width : (which + 1) * width]


def pack_fields(ref, fields, send, outs):
    half = len(fields) // 2
    size = group_size(half)
    for j in range(0, half, size):
        pack_group(
            ref, fields[j : j + size], fields[half + j : half + j + size], send, j, outs
        )


def prepare_kernel(
    iterate_in,
    halo_send_in,
    shift_in,
    gen_in,
    mean_in,
    modes_in,
    nbr_in,
    grads_in,
    face_mats_in,
    counts_in,
    pack0,
    pack1,
    send_out,
    conduct_out,
    low,
    high,
    nbr,
    grads,
    face_mats,
    counts,
    halo_send,
    shift,
    gen,
    mean,
    modes,
    small_done,
    field_done,
    later_done,
):
    iterate = Halves(low, high)
    samples, dofs, elems = iterate.shape
    halo = halo_send.shape[1]
    half = samples // 2
    size = group_size(half)
    small = [
        pltpu.make_async_copy(source, target, small_done.at[i])
        for i, (source, target) in enumerate(
            (
                (halo_send_in, halo_send),
                (shift_in, shift),
                (gen_in, gen),
                (mean_in, mean),
                (modes_in, modes),
            )
        )
    ]
    large = []
    for j in range(0, half, size):
        for at, side in ((j, low), (half + j, high)):
            large.append(
                pltpu.make_async_copy(
                    iterate_in.at[pl.ds(at, size)],
                    side.at[pl.ds(j, size)],
                    field_done.at[len(large)],
                )
            )
    later = [
        pltpu.make_async_copy(source, target, later_done.at[i])
        for i, (source, target) in enumerate(
            ((nbr_in, nbr), (grads_in, grads), (face_mats_in, face_mats), (counts_in, counts))
        )
    ]
    for copy in small + large + later:
        copy.start()
    for copy in small + large:
        copy.wait()
    even = space_even()
    down = jnp.concatenate([halo_send[0:1, :]] * 2, axis=1)
    up = jnp.concatenate([halo_send[1:2, :]] * 2, axis=1)
    lane = lax.broadcasted_iota(i32, (1, 2 * halo), 1)
    row = rows_iota((2 * elems, 2 * halo))
    for which in range(2):
        ids = jnp.where(even == (which == 0), up, down)
        ids = jnp.where(lane < halo, ids, ids + elems)
        send_out[:, which * 2 * halo : (which + 1) * 2 * halo] = (
            (row == ids).astype(f32).astype(bf16)
        )
    position = rows_iota((samples, gen.shape[1]))
    residue = lax.rem(position * gen[...], samples)
    shifted = residue.astype(f32) / samples + shift[...]
    fraction = shifted - jnp.floor(shifted)
    points = 0.5 - jnp.abs(2.0 * fraction - 1.0)
    conduct = mean[...] * (
        1.0 + jnp.dot(points, modes[...], precision=highest, preferred_element_type=f32)
    )
    conduct_out[...] = conduct
    send = send_out[...]
    got = exact_select(jnp.concatenate([conduct[:half], conduct[half:]], axis=1), send)
    pack0[half * dofs :, :] = got[:, : 2 * halo]
    pack1[half * dofs :, :] = got[:, 2 * halo :]
    for j in range(0, half, size):
        left = list(range(j, j + size))
        pack_group(iterate, left, [half + i for i in left], send, j, (pack0, pack1))
    for copy in later:
        copy.wait()


def local_part(read, slots, coef_row, picks, blocks, out, high, low):
    dofs, elems = out.shape[1], out.shape[2]
    size = next(size for size in (8, 6, 4, 3, 2, 1) if len(slots) % size == 0)
    for first in range(0, len(slots), size):
        group = range(first, first + size)
        values = [read(t) for t in group]
        hi, lo = split(jnp.concatenate(values, axis=0))
        for t, value in zip(group, values):
            a, b = split(value * coef_row(FACES, t))
            high[t, 0:dofs, :] = a
            low[t, 0:dofs, :] = b
        for f in range(FACES):
            pick = picks[:, f * elems : (f + 1) * elems]
            got = dot(hi, pick) + dot(lo, pick)
            at = (f + 1) * dofs
            for i, t in enumerate(group):
                a, b = split(got[i * dofs : (i + 1) * dofs] * coef_row(f, t))
                high[t, at : at + dofs, :] = a
                low[t, at : at + dofs, :] = b
        stacked = blocks[...]
        for t in group:
            both = dot(stacked, high[t])
            out[slots[t]] = both[:dofs] + (both[dofs:] + dot(stacked[:dofs], low[t]))


def first_local_kernel(
    low_fields,
    high_fields,
    conduct_ref,
    face_nbr,
    grads,
    face_mats,
    counts_in,
    out,
    coefs,
    picks,
    blocks,
    face_blocks,
    halo_picks,
    flags,
    facing,
    high,
    low,
    wide,
):
    iterate = Halves(low_fields, high_fields)
    samples, dofs, elems = iterate.shape
    halo = halo_picks.shape[0] // 4
    even = space_even()
    row = rows_iota((elems, elems))
    for f in range(FACES):
        picks[:, f * elems : (f + 1) * elems] = (
            (row == face_nbr[f : f + 1, :]).astype(f32).astype(bf16)
        )
    conduct = conduct_ref[...]
    diag = conduct
    for f in range(FACES):
        nbr = face_nbr[f : f + 1, :]
        across = exact_select(conduct, picks[:, f * elems : (f + 1) * elems])
        inside = (nbr >= 0) & (nbr < elems)
        coupling = jnp.where(inside, 0.5 * (conduct + across), 0.0)
        coefs[f] = coupling
        diag = diag + jnp.where(nbr < 0, conduct, coupling)
    coefs[FACES] = diag
    coefs[FACES + 1] = conduct
    volume = (rows_iota((dofs, dofs)) == lax.broadcasted_iota(i32, (dofs, dofs), 1)).astype(f32)
    for d in range(grads.shape[0]):
        volume = volume + lax.dot_general(
            grads[d], grads[d], (((0,), (0,)), ((), ())), precision=highest,
            preferred_element_type=f32,
        )
    wide[...] = jnp.zeros(wide.shape, f32)
    wide[0:dofs, 0:dofs] = volume
    for f in range(FACES):
        block = face_mats[f // 2]
        at = (f + 1) * dofs
        wide[at : at + dofs, 0:dofs] = block if f % 2 == 0 else block.T
    turned = wide[...].T[:dofs, :]
    hi, lo = split(turned)
    blocks[0:dofs, :] = hi
    blocks[dofs:, :] = lo
    for f in range(FACES):
        block = face_mats[f // 2]
        hi, lo = split(block.T if f % 2 == 0 else block)
        face_blocks[f, 0:dofs, :] = hi
        face_blocks[f, dofs:, :] = lo
    for which, (face, base) in enumerate(sides(even, elems, halo)):
        nbr = jnp.where(face == 4, face_nbr[4:5, :], face_nbr[5:6, :])
        pick = halo_onehot(nbr, base, halo)
        halo_picks[which * 2 * halo : (which + 1) * 2 * halo, :] = pick
        facing[which] = exact_select(side_by_side(conduct), pick, 1)
    crossing = jnp.max(jnp.where(face_nbr[0:4, :] >= elems, 1, 0))
    crossing = crossing + jnp.max(jnp.where(face_nbr[4:5, :] >= elems + halo, 1, 0))
    fifth = face_nbr[5:6, :]
    crossing = crossing + jnp.max(
        jnp.where((fifth >= elems) & (fifth < elems + halo), 1, 0)
    )
    lane = lax.broadcasted_iota(i32, flags.shape, 1)
    line = jnp.where(lane == 0, crossing, 0)
    skip = jnp.int32(0)
    for k in range(counts_in.shape[1]):
        line = jnp.where(lane == 2 + k, counts_in[0, k], line)
    for k, re, _ in frequencies(counts_in.shape[1]):
        skip = jnp.where(counts_in[0, k] == 1, re, skip)
    flags[...] = jnp.where(lane == 1, skip, line)
    local_part(
        lambda t: iterate[t],
        list(range(samples)),
        lambda f, t: coefs[f, t : t + 1, :],
        picks,
        blocks,
        out,
        high,
        low,
    )


def side_by_side(x):
    half = x.shape[0] // 2
    return jnp.concatenate([x[:half], x[half:]], axis=1)


def stacked_halves(x):
    width = x.shape[1] // 2
    return jnp.concatenate([x[:, :width], x[:, width:]], axis=0)


def usual_halo(arrived, scales, blocks, picks, chosen=None):
    dofs = blocks[0].shape[1]
    columns = []
    for which in range(2):
        value = arrived[which]
        width = value.shape[1]
        chosen = range(scales[which].shape[0]) if chosen is None else chosen
        pairs = len(chosen)
        scaled = [
            value[j * dofs : (j + 1) * dofs, :] * scales[which][j : j + 1, :] for j in chosen
        ]
        got = times_block(blocks[which], jnp.concatenate(scaled, axis=1))
        columns.append(
            jnp.concatenate([got[:, j * width : (j + 1) * width] for j in range(pairs)], axis=0)
        )
    hi, lo = split(jnp.concatenate(columns, axis=1))
    return dot(hi, picks) + dot(lo, picks)


class Halves:
    def __init__(self, low, high):
        self.low, self.high = low, high
        self.shape = (2 * low.shape[0],) + tuple(low.shape[1:])

    def __getitem__(self, at):
        half = self.low.shape[0]
        return self.low[at] if at < half else self.high[at - half]


def other_halo(arrived, block, pick):
    dofs = block.shape[1]
    hi, lo = split(times_block(block, arrived))
    got = dot(hi, pick) + dot(lo, pick)
    return got


def other_sides(flags, even, face_nbr, halo, body):
    elems = face_nbr.shape[1]

    @pl.when(flags[0, 0] > 0)
    def _():
        for which, (usual, base) in enumerate(sides(even, elems, halo)):

            def step(face, carry, which=which, usual=usual, base=base):
                @pl.when(face != usual)
                def _():
                    body(which, face, halo_onehot(face_nbr[pl.ds(face, 1), :], base, halo))

                return carry

            lax.fori_loop(0, FACES, step, 0)


def pair_place(t, half, dofs, elems):
    row, col = t % half * dofs, t // half * elems
    return slice(row, row + dofs), slice(col, col + elems)


def add_others(arrived, even, flags, face_nbr, face_blocks, halo, chosen, slots, coef_row, factor, total):
    elems = face_nbr.shape[1]
    dofs = total.shape[1]

    def body(which, face, pick):
        block = face_blocks[face]
        half = len(chosen)
        for i, j in enumerate(chosen):
            got = other_halo(arrived[which][j * dofs : (j + 1) * dofs, :], block, pick)
            for t in (i, half + i):
                if t < len(slots):
                    cols = slice(t // half * elems, (t // half + 1) * elems)
                    field = slots[t]
                    total[field] = total[field] + factor * coef_row(face, t) * got[:, cols]

    other_sides(flags, even, face_nbr, halo, body)


def residual_kernel(
    forcing,
    low_fields,
    high_fields,
    earlier_low,
    earlier_high,
    local,
    arrived0,
    arrived1,
    coefs_in,
    face_nbr,
    blocks,
    face_blocks,
    halo_picks,
    facing,
    flags,
    *rest,
    total_steps,
    groups,
    at,
):
    samples, dofs, elems = forcing.shape
    if at == 0:
        outs, (coefs, extra, total) = rest[:total_steps], rest[total_steps:]
    else:
        extra, outs, total = rest[0], rest[1 : total_steps + 1], rest[-1]
        coefs = coefs_in
    iterate = Halves(low_fields, high_fields)
    halo = halo_picks.shape[0] // 4
    half = samples // 2
    part = samples // total_steps
    size = part // groups
    chosen = [j for j in range(half) if j % part // size == at]
    mine = chosen + [half + j for j in chosen]
    even = space_even()
    usual = sides(even, elems, halo)
    arrived = (arrived0, arrived1)
    scales = [0.5 * (facing[w] + arrived[w][half * dofs :, :]) for w in range(2)]
    if at == 0:
        coefs[...] = coefs_in[...]
        conduct = coefs_in[FACES + 1]
        couplings = [
            stacked_halves(
                exact_select(scales[w], halo_picks[w * 2 * halo : (w + 1) * 2 * halo, :])
            )
            for w in range(2)
        ]
        extra[...] = couplings[0] + couplings[1]
        for w in range(2):
            coefs[usual[w][0]] = coefs[usual[w][0]] + couplings[w]

        def add_coupling(which, face, pick):
            got = exact_select(arrived[which][half * dofs :, :], pick)
            nbr = face_nbr[pl.ds(face, 1), :]
            base = usual[which][1]
            here = (nbr >= base) & (nbr < base + halo)
            coupling = jnp.where(here, 0.5 * (conduct + stacked_halves(got)), 0.0)
            coefs[face] = coefs[face] + coupling
            extra[...] = extra[...] + coupling

        other_sides(flags, even, face_nbr, halo, add_coupling)
        coefs[FACES] = coefs[FACES] + extra[...]
    volume = blocks[:, 0 : 2 * dofs][:, :dofs]
    brought = usual_halo(
        arrived,
        scales,
        [face_blocks[usual[w][0]] for w in range(2)],
        halo_picks[...],
        chosen,
    )
    for t, j in enumerate(mine):
        value = iterate[j]
        total[j] = value + time_step * (
            local[j]
            + brought[pair_place(t, len(chosen), dofs, elems)]
            + times_block(volume, value * extra[j : j + 1, :])
        )
    add_others(
        arrived,
        even,
        flags,
        face_nbr,
        face_blocks,
        halo,
        chosen,
        mine,
        lambda f, t: coefs[f, mine[t] : mine[t] + 1, :],
        time_step,
        total,
    )
    step = lax.axis_index("tm")
    weight = jnp.float32(0.0)
    for n in range(total_steps):
        weight = jnp.where(step == n, jnp.float32(alpha_circ ** (n / total_steps)), weight)
    gate_high = jnp.where(step > 0, weight, 0.0)
    gate_low = jnp.where(step % 2 == 1, weight, 0.0) if two_chips(total_steps) else gate_high
    for turn, out in enumerate(outs):
        first = (partner(step, turn, total_steps) * groups + at) * size
        for i in range(size):
            j = first + i
            inner = forcing[j] - total[j]
            before = lax.rem(j, half)
            late = j >= half
            earlier = jnp.where(late, earlier_high[before], earlier_low[before])
            out[i] = weight * inner + jnp.where(late, gate_high, gate_low) * earlier


def two_chips(devs):
    return devs == 4


def partner(rank, turn, count):
    if count & (count - 1) == 0:
        return rank ^ turn
    return lax.rem(turn + count - rank, count)


def real_fields(total_steps):
    order = [(0, False)]
    if total_steps % 2 == 0:
        order.append((total_steps // 2, False))
    for k in range(1, (total_steps + 1) // 2):
        order += [(k, False), (k, True)]
    return order


def cos_sin(k, n, total_steps):
    turn = 2.0 * math.pi * ((k * n) % total_steps) / total_steps
    c, s = math.cos(turn), math.sin(turn)
    snap = lambda v: float(round(v)) if abs(v - round(v)) < 1e-12 else v
    return snap(c), snap(s)


def weighted(terms):
    total = None
    for constant, value in terms:
        if constant == 0.0:
            continue
        if total is None:
            total = value if constant == 1.0 else constant * value
        elif constant == 1.0:
            total = total + value
        elif constant == -1.0:
            total = total - value
        else:
            total = total + constant * value
    return total


def shift_of(k, total_steps):
    magnitude = alpha_circ ** (1.0 / total_steps)
    c, s = cos_sin(k, 1, total_steps)
    return 1.0 - magnitude * c, magnitude * s


def theta_rows(k, total_steps, diag):
    shift_real, shift_imag = shift_of(k, total_steps)
    denom = shift_real + (time_step * relax_rho) * diag
    if shift_imag == 0.0:
        return 1.0 / denom, None
    modulus = denom * denom + shift_imag * shift_imag
    return denom / modulus, -shift_imag / modulus


def frequencies(total_steps):
    order = real_fields(total_steps)
    return [
        (k, at, order.index((k, True)) if (k, True) in order else None)
        for at, (k, imag) in enumerate(order)
        if not imag
    ]


def slot_order(samples, total_steps, inner):
    size = samples // inner
    lists = [
        [(g * size + s, i) for s in range(size) for i in range(total_steps - 1)]
        for g in range(inner)
    ]
    if inner == 1:
        return lists[0]
    middle = len(lists[0]) // 2
    return [pair for part in lists for pair in part[:middle]] + [
        pair for part in lists for pair in part[middle:]
    ]


def kept_slots(flags, order, total_steps):
    skip = flags[0, 1]
    return [s * total_steps + jnp.where(skip <= i, i + 1, i) for s, i in order]


def even_slots(slots):
    return slots + slots[: len(slots) % 2]


def my_first(samples, at, groups):
    return (lax.axis_index("tm") * groups + at) * samples


def sample_row(coefs, order, first):
    return lambda f, t: coefs[f, pl.ds(first + order[t][0], 1), :]


def spectrum_kernel(
    flags, coefs, send_ref, own, near, *rest, total_steps, at, groups
):
    arrived, (spectrum, first_w, pack0, pack1, pieces) = rest[:total_steps], rest[-5:]
    samples = arrived[0].shape[0]
    first = my_first(samples, at, groups)
    rank = lax.axis_index("tm")
    for turn, piece in enumerate(arrived):
        pieces[partner(rank, turn, total_steps)] = piece[...]
    if two_chips(total_steps):
        here = at * samples
        there = groups * samples + here
        gate = jnp.where(rank < 2, jnp.float32(alpha_circ ** (2 / total_steps)), 0.0)
        for s in range(samples):
            before = jnp.where(rank == 0, near[here + s], own[there + s])
            pieces[2, s] = pieces[2, s] + gate * before
    for s in range(samples):
        diag = coefs[FACES, pl.ds(first + s, 1), :]
        base = s * total_steps
        for k, re, im in frequencies(total_steps):
            tables = [cos_sin(k, n, total_steps) for n in range(total_steps)]
            real = weighted([(tables[n][0], pieces[n, s]) for n in range(total_steps)])
            rate_real, rate_imag = theta_rows(k, total_steps, diag)
            spectrum[base + re] = real
            if im is None:
                first_w[base + re] = rate_real * real
            else:
                imag = weighted([(-tables[n][1], pieces[n, s]) for n in range(total_steps)])
                spectrum[base + im] = imag
                first_w[base + re] = rate_real * real - rate_imag * imag
                first_w[base + im] = rate_real * imag + rate_imag * real
    slots = kept_slots(flags, slot_order(samples, total_steps, 1), total_steps)
    pack_fields(first_w, even_slots(slots), send_ref[...], (pack0, pack1))


def sweep_local_kernel(
    flags,
    coefs,
    picks,
    blocks,
    halo_picks,
    *rest,
    total_steps,
    at,
    groups,
    first_turn,
    inner,
):
    fields, spectra, rest = rest[:inner], rest[inner : 2 * inner], rest[2 * inner :]
    if first_turn:
        out, thetas, scales, total, high, low = rest
    else:
        out, total, high, low = rest[-4:]
    elems = fields[0].shape[2]
    each = fields[0].shape[0] // total_steps
    samples = inner * each
    first = my_first(samples, at, groups)
    order = slot_order(samples, total_steps, inner)
    slots = kept_slots(flags, order, total_steps)
    row = sample_row(coefs, order, first)
    if first_turn:
        halo = halo_picks.shape[0] // 4
        half = scales.shape[1]
        usual = sides(space_even(), elems, halo)
        count = len(slots)
        for w in range(2):
            lines = [
                row(usual[w][0], t if t < count else 0) for t in range(2 * half)
            ]
            sides_of = [jnp.concatenate(lines[:half], 0), jnp.concatenate(lines[half:], 0)]
            scales[w] = time_step * exact_select(
                jnp.concatenate(sides_of, axis=1),
                halo_picks[w * 2 * halo : (w + 1) * 2 * halo, :],
                1,
            )
        diag = jnp.concatenate(
            [coefs[FACES, pl.ds(first + s, 1), :] for s in range(samples)], axis=0
        )
        for i, (k, _, im) in enumerate(frequencies(total_steps)):
            rate_real, rate_imag = theta_rows(k, total_steps, diag)
            thetas[2 * i] = rate_real
            if im is not None:
                thetas[2 * i + 1] = rate_imag

    def read(t):
        which = order[t][0] // each
        return fields[which][slots[t] - which * each * total_steps]

    local_part(read, slots, row, picks, blocks, total, high, low)
    for s in range(samples):
        base = s * total_steps
        spectrum, current = spectra[s // each], fields[s // each]
        own = s % each * total_steps
        for k, re, im in frequencies(total_steps):
            shift_real, shift_imag = shift_of(k, total_steps)
            value = current[own + re]
            kept = spectrum[own + re] - (shift_real * value + time_step * total[base + re])
            if im is not None:
                other = current[own + im]
                kept = kept + shift_imag * other
                out[base + im] = spectrum[own + im] - (
                    shift_real * other + shift_imag * value + time_step * total[base + im]
                )
            out[base + re] = kept


def sweep_update_kernel(
    flags,
    coefs,
    face_nbr,
    face_blocks,
    halo_picks,
    *rest,
    turn,
    total_steps,
    last,
    sources,
    at,
    groups,
):
    even = space_even()
    take = lambda count: (rest[:count], rest[count:])
    (inner, arrived0, arrived1), rest = take(3)
    currents, rest = take(sources)
    thetas, rest = take(sources)
    scale_refs, rest = take(sources)
    if last:
        outs, (total, solved) = rest[:total_steps], rest[total_steps:]
    else:
        send_ref, *before, solved, pack0, pack1, total = rest
    fields, dofs, elems = inner.shape
    samples = fields // total_steps
    each = samples // sources
    first = my_first(samples, at, groups)
    halo = halo_picks.shape[0] // 4
    usual = sides(even, elems, halo)
    scales = [jnp.concatenate([ref[w] for ref in scale_refs], axis=0) for w in range(2)]
    half = scales[0].shape[0]
    arrived = (arrived0, arrived1)
    order = slot_order(samples, total_steps, sources)
    slots = kept_slots(flags, order, total_steps)
    brought = usual_halo(
        arrived,
        scales,
        [face_blocks[usual[w][0]] for w in range(2)],
        halo_picks[...],
    )
    for t, field in enumerate(slots):
        total[field] = inner[field] - brought[pair_place(t, half, dofs, elems)]
    add_others(
        arrived,
        even,
        flags,
        face_nbr,
        face_blocks,
        halo,
        range(half),
        slots,
        sample_row(coefs, order, first),
        -time_step,
        total,
    )
    for s in range(samples):
        base = s * total_steps
        current, theta = currents[s // each], thetas[s // each]
        own = s % each * total_steps
        line = slice(s % each, s % each + 1)
        for i, (k, re, im) in enumerate(frequencies(total_steps)):
            active = flags[0, 2 + k] > turn + 1
            rate_real = theta[2 * i, line, :]
            value, rest_real = current[own + re], total[base + re]
            change = rate_real * rest_real
            if im is not None:
                rate_imag = theta[2 * i + 1, line, :]
                other, rest_imag = current[own + im], total[base + im]
                change = change - rate_imag * rest_imag
                solved[base + im] = jnp.where(
                    active, other + (rate_real * rest_imag + rate_imag * rest_real), other
                )
            solved[base + re] = jnp.where(active, value + change, value)
    if not last:
        rows = half * dofs
        start = at * rows if before else 0
        for ref, out in zip(before, (pack0, pack1)):
            out[:start, :] = ref[...]
        pack_fields(
            solved,
            even_slots(slots),
            send_ref[...],
            [out.at[start : start + rows] for out in (pack0, pack1)],
        )
        return
    rank = lax.axis_index("tm")
    for s in range(samples):
        base = s * total_steps
        for n in range(total_steps):
            scale = alpha_circ ** (-n / total_steps) / total_steps
            terms = []
            for k, re, im in frequencies(total_steps):
                c, sn = cos_sin(k, n, total_steps)
                if im is None:
                    terms.append((c, solved[base + re]))
                else:
                    terms += [(2.0 * c, solved[base + re]), (-2.0 * sn, solved[base + im])]
            total[n * samples + s] = scale * weighted(terms)
    for turn_to, out in enumerate(outs):
        step = partner(rank, turn_to, total_steps)
        for s in range(samples):
            out[s] = total[step * samples + s]


def assemble_kernel(*rest, places, total_steps, groups):
    count = len(places)
    pieces, (out, done) = rest[:count], rest[-2:]
    size = pieces[0].shape[0]
    rank = lax.axis_index("tm")
    copies = []
    for which, ((at, turn), piece) in enumerate(zip(places, pieces)):
        first = (partner(rank, turn, total_steps) * groups + at) * size
        copies.append(
            pltpu.make_async_copy(piece, out.at[pl.ds(first, size)], done.at[which])
        )
    for copy in copies:
        copy.start()
    for copy in copies:
        copy.wait()


vmem = pl.BlockSpec(memory_space=pltpu.VMEM)


def run(
    kernel, inputs, outs, scratch=(), in_hbm=(), out_hbm=(), aliases=(), flops=10**9
):
    def spec(i, outside):
        return pl.BlockSpec(memory_space=pltpu.HBM) if i in outside else vmem

    inputs = [
        pltpu.with_memory_space_constraint(value, pltpu.HBM) if i in in_hbm else value
        for i, value in enumerate(inputs)
    ]
    return pl.pallas_call(
        kernel,
        out_shape=[jax.ShapeDtypeStruct(*o) for o in outs],
        in_specs=[spec(i, in_hbm) for i in range(len(inputs))],
        out_specs=[spec(i, out_hbm) for i in range(len(outs))],
        input_output_aliases=dict(aliases),
        scratch_shapes=[pltpu.VMEM(*s) if isinstance(s, tuple) else s for s in scratch],
        compiler_params=pltpu.CompilerParams(vmem_limit_bytes=40 << 20),
        cost_estimate=pl.CostEstimate(flops=flops, bytes_accessed=1 << 22, transcendentals=0),
    )(*inputs)


def neighbour_swap(value, start):
    axes = ("groups", "tm", "space")
    parts, devs, count = (lax.axis_size(axis) for axis in axes)
    pairs = []
    for part in range(parts):
        for tm in range(devs):
            for space in range(count):
                step = 1 if (space + tm + start) % 2 == 0 else -1
                to_part, to_space = part, space + step
                if not 0 <= to_space < count:
                    to_part, to_space = part ^ 1, space
                if to_part < parts:
                    pairs.append(
                        ((part * devs + tm) * count + space, (to_part * devs + tm) * count + to_space)
                    )
    return lax.ppermute(value, axes, pairs)


def time_swap(value, turn):
    count = lax.axis_size("tm")
    pairs = [(i, int(partner(i, turn, count))) for i in range(count)]
    return value if turn == 0 else lax.ppermute(value, "tm", pairs)


def per_device(
    forcing,
    iterate,
    kappa_mean,
    kappa_modes,
    grad_mats,
    face_mats,
    lattice_shift,
    gen_vector,
    sweep_counts,
    face_nbr,
    halo_send,
):
    samples, steps_dev, dofs, elems = forcing.shape
    halo = halo_send.shape[1]
    devs = lax.axis_size("tm")
    total_steps = steps_dev * devs
    part = samples // devs
    half = samples // 2
    cube = (samples, dofs, elems)
    forcing = forcing.reshape(cube)
    iterate = iterate.reshape(cube)
    onward = [(i, (i + 1) % devs) for i in range(devs)]
    rows = half * dofs
    copies = 2 * (half // group_size(half))
    (
        pack0, pack1, send, conduct, low, high, face_nbr, grad_mats, face_mats, counts_line
    ) = run(
        prepare_kernel,
        (
            iterate,
            halo_send,
            lattice_shift.reshape(1, -1),
            gen_vector.reshape(1, -1),
            kappa_mean.reshape(1, -1),
            kappa_modes,
            face_nbr,
            grad_mats,
            face_mats,
            sweep_counts.reshape(1, -1),
        ),
        [
            ((rows + half, 2 * halo), f32),
            ((rows + half, 2 * halo), f32),
            ((2 * elems, 4 * halo), bf16),
            ((samples, elems), f32),
            ((half, dofs, elems), f32),
            ((half, dofs, elems), f32),
            (face_nbr.shape, i32),
            (grad_mats.shape, f32),
            (face_mats.shape, f32),
            ((1, sweep_counts.shape[0]), i32),
        ],
        [
            (halo_send.shape, i32),
            ((1, lattice_shift.shape[0]), f32),
            ((1, gen_vector.shape[0]), i32),
            ((1, elems), f32),
            (kappa_modes.shape, f32),
            pltpu.SemaphoreType.DMA((5,)),
            pltpu.SemaphoreType.DMA((copies,)),
            pltpu.SemaphoreType.DMA((4,)),
        ],
        in_hbm=range(10),
    )
    arrived0 = neighbour_swap(pack0, 0)
    arrived1 = neighbour_swap(pack1, 1)
    earlier_high = lax.ppermute(high, "tm", onward)
    if two_chips(devs):
        earlier_low = time_swap(low, 1)
    else:
        earlier_low = lax.ppermute(low, "tm", onward)
    blocks_wide = (FACES + 1) * dofs
    splits = lambda count: [((count, blocks_wide, elems), bf16)] * 2
    (
        local, coefs, picks, blocks, face_blocks, halo_picks, flags, facing
    ) = run(
        first_local_kernel,
        (low, high, conduct, face_nbr, grad_mats, face_mats, counts_line),
        [
            (cube, f32),
            ((FACES + 2, samples, elems), f32),
            ((elems, FACES * elems), bf16),
            ((2 * dofs, blocks_wide), bf16),
            ((FACES, 2 * dofs, dofs), bf16),
            ((4 * halo, 2 * elems), bf16),
            ((1, 2 * halo), i32),
            ((2, half, 2 * halo), f32),
        ],
        splits(samples) + [((blocks_wide, 2 * dofs), f32)],
        flops=4 * 10**9,
    )
    groups = GROUPS
    if part % groups or (part // groups * (total_steps - 1)) % 2:
        groups = 1
    share = part // groups
    piece = ((share, dofs, elems), f32)
    scaled, extra = [], ()
    for at in range(groups):
        results = run(
            functools.partial(residual_kernel, total_steps=total_steps, groups=groups, at=at),
            (
                forcing,
                low,
                high,
                earlier_low,
                earlier_high,
                local,
                arrived0,
                arrived1,
                coefs,
                face_nbr,
                blocks,
                face_blocks,
                halo_picks,
                facing,
                flags,
                *extra,
            ),
            [piece] * devs
            + [((FACES + 2, samples, elems), f32), ((samples, elems), f32)] * (at == 0),
            [(cube, f32)],
        )
        scaled += results[:devs]
        if at == 0:
            coefs, extra = results[devs], (results[devs + 1],)
    sizes = lambda share: (
        ((share * total_steps, dofs, elems), f32),
        (((share * (total_steps - 1) + 1) // 2 * dofs, 2 * halo), f32),
        (share * (total_steps - 1) + 1) // 2,
    )
    some, packed, pairs = sizes(share)
    currents, spectra, inners, arrived0, arrived1, thetas, scales = ([] for _ in range(7))
    for at in range(groups):
        mine = dict(total_steps=total_steps, at=at, groups=groups)
        pieces = [time_swap(scaled[at * devs + turn], turn) for turn in range(devs)]
        spectrum, current, pack0, pack1 = run(
            functools.partial(spectrum_kernel, **mine),
            (flags, coefs, send, low, earlier_low, *pieces, *thetas[-1:]),
            [some, some, packed, packed],
            [((total_steps, share, dofs, elems), f32)],
        )
        arrived0.append(neighbour_swap(pack0, 0))
        arrived1.append(neighbour_swap(pack1, 1))
        inner, theta, scale = run(
            functools.partial(sweep_local_kernel, first_turn=True, inner=1, **mine),
            (flags, coefs, picks, blocks, halo_picks, current, spectrum),
            [
                some,
                ((2 * len(frequencies(total_steps)), share, elems), f32),
                ((2, pairs, 2 * halo), f32),
            ],
            [some] + splits(share * (total_steps - 1)),
            flops=3 * 10**9 // groups,
        )
        currents.append(current)
        spectra.append(spectrum)
        inners.append(inner)
        thetas.append(theta)
        scales.append(scale)
    tables = (flags, coefs, face_nbr, face_blocks, halo_picks)
    restored = {}
    arrived = []
    for at in range(groups):
        mine = dict(total_steps=total_steps, at=at, groups=groups)
        current, *packs = run(
            functools.partial(sweep_update_kernel, turn=0, last=False, sources=1, **mine),
            (
                *tables,
                inners[at],
                arrived0[at],
                arrived1[at],
                currents[at],
                thetas[at],
                scales[at],
                send,
            ),
            [some, packed, packed],
            [some],
        )
        currents[at] = current
        arrived.append([neighbour_swap(pack, which) for which, pack in enumerate(packs)])
    series = ()
    for at in range(groups):
        mine = dict(total_steps=total_steps, at=at, groups=groups)
        (inner,) = run(
            functools.partial(sweep_local_kernel, first_turn=False, inner=1, **mine),
            (flags, coefs, picks, blocks, halo_picks, currents[at], spectra[at], *series[:1]),
            [some],
            [some] + splits(share * (total_steps - 1)),
            flops=3 * 10**9 // groups,
        )
        series = run(
            functools.partial(sweep_update_kernel, turn=1, last=True, sources=1, **mine),
            (*tables, inner, *arrived[at], currents[at], thetas[at], scales[at]),
            [piece] * devs,
            [some, some],
        )
        for turn in range(devs):
            restored[at, turn] = time_swap(series[turn], turn)
    out = None
    places = list(restored)
    for chosen in (places[:-1], places[-1:]):
        inputs = [restored[place] for place in chosen] + ([] if out is None else [out])
        (out,) = run(
            functools.partial(
                assemble_kernel, places=chosen, total_steps=total_steps, groups=groups
            ),
            tuple(inputs),
            [(cube, f32)],
            [pltpu.SemaphoreType.DMA((len(chosen),))],
            in_hbm=() if out is None else (len(chosen),),
            out_hbm=(0,),
            aliases=() if out is None else ((len(chosen), 0),),
        )
    return out.reshape(samples, steps_dev, dofs, elems)


def solution(mesh):
    placed = (
        P("groups", "tm", None, "space"),
        P("groups", "tm", None, "space"),
        P("space"),
        P(None, "space"),
        P(),
        P(),
        P("groups"),
        P(),
        P(),
        P(None, "space"),
        P(None, "space"),
    )
    return jax.shard_map(
        per_device,
        mesh=mesh,
        in_specs=placed,
        out_specs=P("groups", "tm", None, "space"),
        check_vma=False,
    )
```
